128 devices in a mesh: dirs: 4 (over z), slab: 32 (over y, x, core).
Axes of the slice: x: 4, y: 4, z: 4, core: 2. Of those that a mesh axis runs over, the one named last changes fastest.
Arguments:
- perturbations: float32 [16, 128, 128, 256], P('dirs', 'slab'), may hold values from -6 to 6
- background_now: float32 [128, 128, 256], P('slab'), may hold values from -9 to 9
- background_prev: float32 [128, 128, 256], P('slab'), may hold values from -9 to 9
- stiffness: float32 [128, 128, 256], P('slab'), may hold values from 0.06 to 0.3
- buoyancy: float32 [128, 128, 256], P('slab'), may hold values from 0.5 to 0.9
- absorb_mask: int32 [128, 128, 256], P('slab'), may hold values 0 or 1
- source_cells: int32 [512], P('slab'), may hold values from 0 to 131071
- source_amp: float32 [512], P('slab'), may hold values from -12 to 12
- receiver_cells: int32 [32768], P('slab'), may hold values from 0 to 131071
- column_order: int32 [16], replicated, may hold values from 0 to 15, each once
Outputs:
- basis: float32 [16, 128, 128, 256], P(None, 'slab', 'dirs')
- triangle: float32 [16, 16], replicated
The draws below stay inside these ranges and needn't reach their ends.
Inputs may be any that keep to these rules, and one draw needn't show every extreme that they name: `source_cells`: entry i names a cell of depth slab i // 16, numbered (layer * 128 + row) * 256 + column inside that slab; cells may repeat. `receiver_cells`: entry i names a cell of depth slab i // 1024, numbered (layer * 128 + row) * 256 + column inside that slab; cells may repeat. `column_order`: each number of 0 to 15 appears once.
All inputs are finite; a program needn't handle non-finite values. No bound on the sum of `absorb_mask` on one device may be relied on, other than what follows from the above.
Results may differ from the reference program's by a relative error of at most 0.0003.
Values sent between devices are 32-bit elements; how exact they have to be, the bound alone decides.
No kernel may reach another device: no remote copies, remote signals or barrier semaphores. Data moves between devices by JAX's collectives and lax.ppermute only.
A program may use at most 256 MiB of HBM per device.

```python
import math
import jax
import jax.numpy as jnp
from jax import lax

CZ = 4
NY = 128
NX = 256
STEPS = 4
SRC_DEV = 16
REC_DEV = 1024
KDIR = 16
NZ = 128
NSRC = 512
NREC = 32768


def rough_field(key):
    depth_share = (jnp.arange(NZ, dtype=jnp.float32) / NZ)[:, None, None]
    row_share = (jnp.arange(NY, dtype=jnp.float32) / NY)[None, :, None]
    factor = (0.6 + 1.2 * depth_share) * (0.8 + 0.4 * row_share)
    values = jnp.clip(jax.random.normal(key, (NZ, NY, NX), jnp.float32), -4.0, 4.0)
    return values * factor


def draw_background_now(key, part):
    return rough_field(jax.random.fold_in(key, 11))


def draw_background_prev(key, part):
    return rough_field(jax.random.fold_in(key, 12))


def place_ends(values, key, least, largest):
    longest = values.shape.index(max(values.shape))
    spots = []
    for shift in (0, 1):
        where = [jax.random.randint(jax.random.fold_in(key, axis), (), 0, length) for axis, length in enumerate(values.shape)]
        where[longest] = (where[longest] + shift) % values.shape[longest]
        spots.append(tuple(where))
    return values.at[spots[0]].set(least).at[spots[1]].set(largest)


def level_of(rng, shape, cuts, smallest, top_value):
    loudness = 1.0
    for dim, blocks in cuts:
        steps = jax.random.uniform(jax.random.fold_in(jax.random.fold_in(rng, 6), dim), (blocks,), jnp.float32, smallest / len(cuts), top_value / len(cuts))
        loudness = loudness * jnp.repeat(jnp.exp(steps), shape[dim] // blocks).reshape((-1,) + (1,) * (len(shape) - 1 - dim))
    return loudness


def scatter_about(key, shape, spread, most, split=(), held_as=jnp.bfloat16):
    result = jax.random.normal(key, shape, jnp.float32) * spread
    if len(split) > 0:
        result = level_of(key, shape, split, -0.22, 0.18) * result
    return jnp.clip(result, min=-most, max=most).astype(held_as)


def setup_inputs(seed: int = 0) -> dict:
    key_list = jax.random.split(jax.random.key(seed), 11)
    perturbations = scatter_about(key_list[0], (KDIR, NZ, NY, NX), 1.0, 6.0, ((0, 4), (1, 32)), jnp.float32)
    background_now = draw_background_now(jax.random.fold_in(key_list[10], 71), 0)
    background_prev = draw_background_prev(jax.random.fold_in(key_list[10], 71), 0)
    stiffness = jnp.clip(jnp.exp(math.log(0.3) - 1.609438 * jax.random.uniform(key_list[3], (NZ, NY, NX), jnp.float32) ** level_of(key_list[3], (NZ, NY, NX), ((0, 32),), -0.2, 0.2)), 0.06, 0.3)
    buoyancy = jnp.clip(0.5 + 0.39999998 * jax.random.uniform(key_list[4], (NZ, NY, NX), jnp.float32) ** level_of(key_list[4], (NZ, NY, NX), ((0, 32),), -0.2, 0.2), 0.5, 0.9)
    absorb_mask = place_ends((jax.random.randint(key_list[5], (NZ, NY, NX), 0, 4) < 1).astype(jnp.int32), jax.random.fold_in(key_list[5], 1), 0, 1)
    source_cells = place_ends(jax.random.randint(key_list[6], (NSRC,), 0, CZ * NY * NX), jax.random.fold_in(key_list[6], 1), 0, (CZ * NY * NX) - 1).astype(jnp.int32)
    source_amp = scatter_about(key_list[7], (NSRC,), 3.0, 12.0, ((0, 32),), jnp.float32)
    receiver_cells = place_ends(jax.random.randint(key_list[8], (NREC,), 0, CZ * NY * NX), jax.random.fold_in(key_list[8], 1), 0, (CZ * NY * NX) - 1).astype(jnp.int32)
    column_order = jax.random.permutation(key_list[9], KDIR).astype(jnp.int32)
    return dict(perturbations=perturbations, background_now=background_now, background_prev=background_prev, stiffness=stiffness, buoyancy=buoyancy, absorb_mask=absorb_mask, source_cells=source_cells, source_amp=source_amp, receiver_cells=receiver_cells, column_order=column_order)


COEFFS = (1.6, -0.2, 8.0 / 315.0, -1.0 / 560.0)
DAMPING = 0.3

def source_weight(t):
    return (1.0 - 0.4 * t) * math.exp(-0.125 * t * t)

def shifted(padded, k, dimension, extent):
    starts = [4, 4, 4]
    starts[dimension] += k
    return padded[starts[0]:starts[0] + extent[0], starts[1]:starts[1] + extent[1], starts[2]:starts[2] + extent[2]]

def laplace(field, buoy_padded):
    extent = field.shape
    padded = jnp.pad(field, 4)
    centre = shifted(padded, 0, 0, extent)
    buoy_centre = shifted(buoy_padded, 0, 0, extent)
    summed = jnp.zeros(extent, jnp.float32)
    for k in range(1, 5):
        partial_value = jnp.zeros(extent, jnp.float32)
        for dimension in range(3):
            beyond = shifted(padded, k, dimension, extent)
            behind = shifted(padded, -k, dimension, extent)
            buoy_beyond = shifted(buoy_padded, k, dimension, extent)
            buoy_behind = shifted(buoy_padded, -k, dimension, extent)
            partial_value = partial_value + ((buoy_centre + buoy_beyond) * (beyond - centre) - (buoy_centre + buoy_behind) * (centre - behind))
        summed = summed + 0.5 * COEFFS[k - 1] * partial_value
    return summed

def global_cells(local_cells, per_slab, slab_cells):
    owners = jnp.arange(local_cells.shape[0], dtype=jnp.int32) // per_slab
    return (owners * slab_cells + local_cells).astype(jnp.int32)

def factor(gram):
    count = gram.shape[0]
    identity = jnp.eye(count, dtype=gram.dtype)
    lower = jnp.zeros_like(gram)
    for column in range(count):
        values = gram[:, column] - lax.optimization_barrier(jnp.sum(lower * lower[column][None, :], 1))
        pivot = jnp.sqrt(values[column])
        below = jnp.arange(count) >= column
        lower = lower + jnp.where(below, values / pivot, 0.0)[:, None] * identity[column][None, :]
    inverse_lower = jnp.zeros_like(gram)
    for row in range(count):
        solved = (identity[row] - lax.optimization_barrier(jnp.sum(lower[row][:, None] * inverse_lower, 0))) / lower[row, row]
        inverse_lower = inverse_lower + identity[row][:, None] * solved[None, :]
    return (lower.T, inverse_lower.T)

def product(left, right):
    return jnp.dot(left, right, precision=lax.Precision.HIGHEST, preferred_element_type=jnp.float32)

def reference(perturbations, background_now, background_prev, stiffness, buoyancy, absorb_mask, source_cells, source_amp, receiver_cells, column_order):
    slab_cells = CZ * NY * NX
    grid_cells = NZ * NY * NX
    buoy_padded = jnp.pad(buoyancy, 4)
    tapering = 1.0 - DAMPING * absorb_mask.astype(jnp.float32)
    source_index = global_cells(source_cells, SRC_DEV, slab_cells)
    source_field = jnp.zeros((grid_cells,), jnp.float32).at[source_index].add(source_amp).reshape(NZ, NY, NX)
    receiver_index = global_cells(receiver_cells, REC_DEV, slab_cells)
    older, current = (background_prev, background_now)
    laplace_back = []
    for t in range(STEPS):
        lapped = laplace(current, buoy_padded)
        laplace_back.append(lapped)
        newer = tapering * (2.0 * current - older + stiffness * lapped) + source_weight(t) * source_field
        older, current = (current, newer)

    def one_direction(direction_field):
        born_old = jnp.zeros((NZ, NY, NX), jnp.float32)
        born_now = jnp.zeros((NZ, NY, NX), jnp.float32)
        records = []
        for t in range(STEPS):
            born_new = tapering * (2.0 * born_now - born_old + stiffness * laplace(born_now, buoy_padded) + direction_field * laplace_back[t])
            records.append(born_new.reshape(-1)[receiver_index])
            born_old, born_now = (born_now, born_new)
        adjoint_far = jnp.zeros((NZ, NY, NX), jnp.float32)
        adjoint_near = jnp.zeros((NZ, NY, NX), jnp.float32)
        images = jnp.zeros((NZ, NY, NX), jnp.float32)
        for t in reversed(range(STEPS)):
            injected = jnp.zeros((grid_cells,), jnp.float32).at[receiver_index].add(records[t]).reshape(NZ, NY, NX)
            if t == STEPS - 1:
                adjoint_now = injected
            else:
                adjoint_now = tapering * (2.0 * adjoint_near - adjoint_far + stiffness * laplace(adjoint_near, buoy_padded)) + injected
            images = images + laplace_back[t] * adjoint_now
            adjoint_far, adjoint_near = (adjoint_near, adjoint_now)
        return images
    sketch = lax.map(one_direction, perturbations)
    ordered = sketch[column_order].reshape(KDIR, grid_cells)
    half_count = KDIR // 2
    first_rows = ordered[:half_count]
    second_rows = ordered[half_count:]
    first_gram = product(first_rows, first_rows.T)
    upper_first, inverse_first = factor(first_gram)
    first_basis = product(inverse_first.T, first_rows)
    coupling = product(first_basis, second_rows.T)
    remainder = second_rows - product(coupling.T, first_basis)
    second_gram = product(remainder, remainder.T)
    upper_second, inverse_second = factor(second_gram)
    second_basis = product(inverse_second.T, remainder)
    factor_cells = math.sqrt(grid_cells)
    basis = (jnp.concatenate([first_basis, second_basis], 0) * factor_cells).reshape(KDIR, NZ, NY, NX)
    top_rows = jnp.concatenate([upper_first, coupling], 1)
    low_rows = jnp.concatenate([jnp.zeros((half_count, half_count), jnp.float32), upper_second], 1)
    triangle = jnp.concatenate([top_rows, low_rows], 0) / factor_cells
    return (basis, triangle)
```

```python
import functools
import math

import jax
import jax.numpy as jnp
import ml_dtypes
import numpy as np
from jax import lax
from jax.experimental import pallas as pl
from jax.experimental.pallas import tpu as pltpu
from jax.sharding import PartitionSpec as P

STEPS = 4
DAMPING = 0.3
TAPS = (8064.0, -1008.0, 128.0, -9.0)
CENTRE = 6.0 * sum(TAPS)
HALF = 0.5 / 5040.0
GROUPS = 2
VMEM = 40 * 1024 * 1024
LANE = 128


def band(size):
    matrix = np.zeros((size, size), np.float32)
    for k, tap in enumerate(TAPS, 1):
        matrix += tap * (np.eye(size, k=k) + np.eye(size, k=-k))
    return matrix.astype(ml_dtypes.bfloat16)


def source_weight(t):
    return (1.0 - 0.4 * t) * math.exp(-0.125 * t * t)


def params(**more):
    return pltpu.CompilerParams(vmem_limit_bytes=VMEM, **more)


def split_rows(y_ref, slot, layer, row, values, parts, rows):
    size = values.shape[0]
    for s in range(parts):
        part = values.astype(jnp.bfloat16)
        y_ref[slot, layer, s * rows + row : s * rows + row + size, :] = part
        if s < parts - 1:
            values = values - part.astype(jnp.float32)


def plane_part(functions, y_ref, a_ref, mx_ref, my_ref, parts):
    _, layers, rows, _ = a_ref.shape
    for layer in range(layers):
        for row in range(0, rows, 32):
            for slot, values in enumerate(functions(layer, row, 32)):
                split_rows(y_ref, slot, layer, row, values, parts, rows)
    for slot in range(a_ref.shape[0]):
        for layer in range(layers):
            y = y_ref[slot, layer]
            along = jnp.dot(y, mx_ref[...], preferred_element_type=jnp.float32)
            total = jnp.dot(my_ref[...], y, preferred_element_type=jnp.float32)
            for s in range(parts):
                total = total + along[s * rows : (s + 1) * rows]
            a_ref[slot, layer] = total


def depth_part(tall, layer):
    total = None
    for k, tap in enumerate(TAPS, 1):
        term = tap * (tall[layer + 4 + k] + tall[layer + 4 - k])
        total = term if total is None else total + term
    return total


def tall_of(refs, rows, columns):
    low, mid, high = refs
    return [ref[layer, rows, columns] for ref in (low, mid, high) for layer in range(4)]


def tiles(shape, body):
    _, rows, columns = shape

    def step(i, carry):
        at = pl.ds(pl.multiple_of(i * 8, 8), 8)
        for column in range(0, columns, LANE):
            body(i, at, slice(column, column + LANE))
        return carry

    lax.fori_loop(0, rows // 8, step, 0)


def place_kernel(rc_ref, sc_ref, amp_ref, mask_ref, m_ref, src_ref, taper_ref):
    layers, rows, columns = m_ref.shape
    count = rc_ref.shape[1]
    lines = layers * rows
    chunk = min(256, count)
    total = None
    for start in range(0, count, chunk):
        cells = rc_ref[:, start : start + chunk]
        line = lax.broadcasted_iota(jnp.int32, (lines, chunk), 0) == cells // columns
        column = lax.broadcasted_iota(jnp.int32, (columns, chunk), 0) == cells % columns
        part = lax.dot_general(
            jnp.where(line, 1.0, 0.0).astype(jnp.bfloat16),
            jnp.where(column, 1.0, 0.0).astype(jnp.bfloat16),
            (((1,), (1,)), ((), ())),
            preferred_element_type=jnp.float32,
        )
        total = part if total is None else total + part
    m_ref[...] = total.reshape(m_ref.shape)
    cells = sc_ref[...]
    count = cells.shape[1]
    line = lax.broadcasted_iota(jnp.int32, (lines, count), 0) == cells // columns
    column = lax.broadcasted_iota(jnp.int32, (columns, count), 0) == cells % columns
    part = lax.dot_general(
        jnp.where(line, 1.0, 0.0),
        jnp.where(column, amp_ref[...], 0.0),
        (((1,), (1,)), ((), ())),
        precision=lax.Precision.HIGHEST,
        preferred_element_type=jnp.float32,
    )
    src_ref[...] = part.reshape(src_ref.shape)
    taper_ref[...] = 1.0 - DAMPING * mask_ref[...].astype(jnp.float32)


def background_kernel(weight, first, last, *refs):
    refs = list(refs)
    u = [refs.pop(0) for _ in range(3)]
    b = [refs.pop(0) for _ in range(3)]
    stiff_ref = refs.pop(0)
    dg_ref = None if first else refs.pop(0)
    taper_ref = src_ref = older_ref = new_ref = None
    if not last:
        taper_ref, src_ref, older_ref = (refs.pop(0) for _ in range(3))
    mx_ref, my_ref = refs.pop(0), refs.pop(0)
    lap_ref = refs.pop(0)
    if not last:
        new_ref = refs.pop(0)
    if first:
        dg_ref = refs.pop(0)
    y_ref, a_ref = refs

    def functions(layer, row, size):
        value = u[1][layer, row : row + size]
        buoy = b[1][layer, row : row + size]
        return [value, value * buoy] + ([buoy] if first else [])

    plane_part(functions, y_ref, a_ref, mx_ref, my_ref, 3)

    def body(i, at, columns):
        value = tall_of(u, at, columns)
        buoy = tall_of(b, at, columns)
        both = [x * y for x, y in zip(value, buoy)]
        for layer in range(4):
            here, b_here = value[layer + 4], buoy[layer + 4]
            if first:
                dg = depth_part(buoy, layer) + a_ref[2, layer, at, columns] + CENTRE * b_here
                dg_ref[layer, at, columns] = dg
            else:
                dg = dg_ref[layer, at, columns]
            plain = depth_part(value, layer) + a_ref[0, layer, at, columns]
            times = depth_part(both, layer) + a_ref[1, layer, at, columns]
            lap = HALF * (b_here * plain + times - here * dg)
            lap_ref[layer, at, columns] = lap
            if not last:
                new_ref[layer, at, columns] = (
                    taper_ref[layer, at, columns]
                    * (
                        2.0 * here
                        - older_ref[layer, at, columns]
                        + stiff_ref[layer, at, columns] * lap
                    )
                    + weight * src_ref[layer, at, columns]
                )

    tiles(lap_ref.shape, body)


def wave_kernel(mode, has_old, *refs):
    refs = list(refs)
    p = [refs.pop(0) for _ in range(3)]
    old_ref = refs.pop(0) if has_old else None
    add_ref, lap_ref = refs.pop(0), refs.pop(0)
    b = [refs.pop(0) for _ in range(3)]
    dg_ref, stiff_ref, taper_ref = (refs.pop(0) for _ in range(3))
    count_ref = refs.pop(0) if mode == "turn" else None
    if mode == "image":
        first_ref = refs.pop(0)
        laps = [refs.pop(0) for _ in range(4)]
    mx_ref, my_ref, out_ref, y_ref, a_ref = refs

    def functions(layer, row, size):
        value = p[1][layer, row : row + size]
        return value, value * b[1][layer, row : row + size]

    plane_part(functions, y_ref, a_ref, mx_ref, my_ref, 2)

    def body(i, at, columns):
        value = tall_of(p, at, columns)
        buoy = tall_of(b, at, columns)
        both = [x * y for x, y in zip(value, buoy)]
        for layer in range(4):
            here = value[layer + 4]
            spot = (layer, at, columns)
            plain = depth_part(value, layer) + a_ref[0, layer, at, columns]
            times = depth_part(both, layer) + a_ref[1, layer, at, columns]
            lb = buoy[layer + 4] * plain + times - here * dg_ref[spot]
            total = 2.0 * here + (HALF * stiff_ref[spot]) * lb
            old = old_ref[spot] if has_old else None
            if has_old:
                total = total - old
            added = add_ref[spot] * lap_ref[spot]
            if mode in ("born", "turn"):
                new = taper_ref[spot] * (total + added)
            else:
                new = taper_ref[spot] * total + added
            if mode == "turn":
                new = count_ref[spot] * new
            if mode == "image":
                image = laps[3][spot] * first_ref[spot] + laps[2][spot] * old
                image = image + laps[1][spot] * here + laps[0][spot] * new
                per = out_ref.shape[2] // 8
                inner = pl.ds(pl.multiple_of((i % per) * 8, 8), 8)
                out_ref[i // per, layer, inner, columns] = image
            else:
                out_ref[spot] = new

    tiles(p[1].shape, body)


def gram_kernel(parts, *refs):
    pieces, out_ref = refs[:parts], refs[parts]
    owners, each, rows, columns = pieces[0].shape
    count = owners * parts * each

    def piece(c, at, column):
        owner, rest = divmod(c, parts * each)
        group, inner = divmod(rest, each)
        return pieces[group][owner, inner, at, column : column + LANE]

    for i0 in range(0, count, 4):
        for j0 in range(0, count, 8):

            def step(r, accs, i0=i0, j0=j0):
                at = pl.ds(pl.multiple_of(r * 8, 8), 8)
                accs = list(accs)
                for column in range(0, columns, LANE):
                    left = [piece(i0 + i, at, column) for i in range(4)]
                    for j in range(8):
                        right = piece(j0 + j, at, column)
                        for i in range(4):
                            accs[i * 8 + j] = accs[i * 8 + j] + left[i] * right
                return tuple(accs)

            zero = jnp.zeros((8, LANE), jnp.float32)
            accs = lax.fori_loop(0, rows // 8, step, (zero,) * 32)
            for i in range(4):
                for j in range(8):
                    out_ref[i0 + i, j0 + j : j0 + j + 1, :] = jnp.sum(
                        accs[i * 8 + j], axis=0, keepdims=True
                    )


def exact(left, right):
    return jnp.dot(left, right, precision=lax.Precision.HIGHEST, preferred_element_type=jnp.float32)


def basis_kernel(parts, scale, gram_ref, sel_ref, selt_ref, *refs):
    pieces = refs[:parts]
    out_ref, triangle_ref, spread_ref = refs[parts:]
    count = gram_ref.shape[0]
    owners, each, layers, rows, columns = pieces[0].shape

    @pl.when(pl.program_id(0) == 0)
    def _():
        row = lax.broadcasted_iota(jnp.int32, (count, count), 0)
        column = lax.broadcasted_iota(jnp.int32, (count, count), 1)
        left = exact(exact(sel_ref[...], gram_ref[...]), selt_ref[...])
        unit = jnp.where(row == column, 1.0, 0.0)
        for i in range(count):
            pivot = jnp.sqrt(left[i : i + 1, i : i + 1])
            upper = left[i : i + 1, :] / pivot
            solved = unit[i : i + 1, :] / pivot
            below = left[:, i : i + 1] / pivot
            is_row = row == i
            left = jnp.where(is_row, upper, jnp.where(row > i, left - below * upper, left))
            unit = jnp.where(is_row, solved, jnp.where(row > i, unit - below * solved, unit))
        triangle_ref[...] = jnp.where(column >= row, left, 0.0) / scale
        weights = exact(unit, sel_ref[...]) * scale
        for i in range(count):
            for c in range(count):
                spread_ref[i * count + c] = jnp.broadcast_to(
                    weights[i : i + 1, c : c + 1], (8, LANE)
                )

    def piece(c, at, columns):
        owner, rest = divmod(c, parts * each)
        group, inner = divmod(rest, each)
        return pieces[group][owner, inner, 0, at, columns]

    for r in range(0, rows, 8):
        at = slice(r, r + 8)
        halves = [slice(column, column + LANE) for column in range(0, columns, LANE)]
        values = [[piece(c, at, half) for half in halves] for c in range(count)]

        def step(i, carry, values=values, at=at):
            totals = [None] * len(halves)
            for c in range(count):
                weight = spread_ref[i * count + c]
                for h in range(len(halves)):
                    term = weight * values[c][h]
                    totals[h] = term if totals[h] is None else totals[h] + term
            for h, half in enumerate(halves):
                out_ref[i, 0, at, half] = totals[h]
            return carry

        for i in range(count):
            step(i, 0)


def halo(block):
    count = lax.axis_size("slab")
    forward = [(i, i + 1) for i in range(count - 1)]
    backward = [(target, source) for source, target in forward]
    return lax.ppermute(block, "slab", forward), lax.ppermute(block, "slab", backward)


def whole(shape):
    zeros = (0,) * len(shape)
    return pl.BlockSpec(tuple(shape), lambda *_: zeros)


def add_up(value):
    for axis in ("slab", "dirs"):
        size, stride = lax.axis_size(axis), 1
        while stride < size:
            value = value + lax.ppermute(value, axis, [(i, i ^ stride) for i in range(size)])
            stride *= 2
    return value


def shards(
    perturbations,
    background_now,
    background_prev,
    stiffness,
    buoyancy,
    absorb_mask,
    source_cells,
    source_amp,
    receiver_cells,
    column_order,
):
    shape = buoyancy.shape
    layers, rows, columns = shape
    sketch_count = perturbations.shape[0]
    each = sketch_count // GROUPS
    owners = lax.axis_size("dirs")
    f32 = jnp.float32
    field = jax.ShapeDtypeStruct(shape, f32)
    cells_here = layers * rows * columns
    mx = jnp.asarray(band(columns))
    my = band(rows)
    my2 = jnp.asarray(np.concatenate([my] * 2, 1))
    my3 = jnp.asarray(np.concatenate([my] * 3, 1))

    b_low, b_high = halo(buoyancy)
    buoy = (b_low, buoyancy, b_high)
    current = background_now
    u_low, u_high = halo(current)

    counts, source_field, taper = pl.pallas_call(
        place_kernel,
        out_shape=(field, field, field),
        compiler_params=params(),
        cost_estimate=pl.CostEstimate(
            flops=40 * cells_here, bytes_accessed=16 * cells_here, transcendentals=0
        ),
        name="place",
    )(
        receiver_cells.reshape(1, -1),
        source_cells.reshape(1, -1),
        source_amp.reshape(1, -1),
        absorb_mask,
    )

    older = background_prev
    laps = []
    dg = None
    for t in range(STEPS):
        first, last = t == 0, t == STEPS - 1
        if not first:
            u_low, u_high = halo(current)
        operands = [u_low, current, u_high, *buoy, stiffness]
        if not first:
            operands.append(dg)
        if not last:
            operands += [taper, source_field, older]
        operands += [mx, my3]
        slots = 3 if first else 2
        results = pl.pallas_call(
            functools.partial(background_kernel, source_weight(t), first, last),
            out_shape=(field,) * (1 + (not last) + first),
            scratch_shapes=[
                pltpu.VMEM((slots, layers, 3 * rows, columns), jnp.bfloat16),
                pltpu.VMEM((slots, layers, rows, columns), f32),
            ],
            compiler_params=params(),
            cost_estimate=pl.CostEstimate(
                flops=60 * cells_here, bytes_accessed=56 * cells_here, transcendentals=0
            ),
            name=f"background{t}",
        )(*operands)
        results = list(results)
        laps.append(results.pop(0))
        if not last:
            older, current = current, results.pop(0)
        if first:
            dg = results.pop(0)

    def wave(mode, group, p, old, add, lap, extra=()):
        low, high = halo(p)
        one = pl.BlockSpec((None, *shape), lambda d: (d, 0, 0, 0))
        shifted = pl.BlockSpec((None, *shape), lambda d: (d + group * each, 0, 0, 0))
        same = whole(shape)
        operands, specs = [low, p, high], [one] * 3
        if old is not None:
            operands.append(old)
            specs.append(one)
        if mode in ("born", "turn"):
            operands += [add, lap]
            specs += [shifted, same]
        else:
            operands += [add, lap]
            specs += [one, same]
        operands += [*buoy, dg, stiffness, taper]
        specs += [same] * 6
        if mode == "turn":
            operands.append(counts)
            specs.append(same)
        if mode == "image":
            operands += list(extra)
            specs += [one] + [same] * 4
        operands += [mx, my2]
        specs += [whole(mx.shape), whole(my2.shape)]
        if mode == "image":
            split = (owners, each, layers, rows // owners, columns)
            out_shape = jax.ShapeDtypeStruct(split, f32)
            out_spec = pl.BlockSpec((owners, None, *split[2:]), lambda d: (0, d, 0, 0, 0))
        else:
            out_shape = jax.ShapeDtypeStruct((each, *shape), f32)
            out_spec = one
        return pl.pallas_call(
            functools.partial(wave_kernel, mode, old is not None),
            grid=(each,),
            in_specs=specs,
            out_specs=out_spec,
            out_shape=out_shape,
            scratch_shapes=[
                pltpu.VMEM((2, layers, 2 * rows, columns), jnp.bfloat16),
                pltpu.VMEM((2, layers, rows, columns), f32),
            ],
            compiler_params=params(),
            cost_estimate=pl.CostEstimate(
                flops=60 * each * cells_here,
                bytes_accessed=28 * each * cells_here,
                transcendentals=0,
            ),
            name=mode,
        )(*operands)

    born = [[None] * GROUPS for _ in range(STEPS + 1)]
    for g in range(GROUPS):
        mine = perturbations[g * each : (g + 1) * each]
        born[1][g] = taper * (mine * laps[0])
    for t in (1, 2):
        for g in range(GROUPS):
            old = born[t - 1][g] if t > 1 else None
            born[t + 1][g] = wave("born", g, born[t][g], old, perturbations, laps[t])
    adjoint = [[None] * GROUPS for _ in range(STEPS + 1)]
    for g in range(GROUPS):
        adjoint[3][g] = wave("turn", g, born[3][g], born[2][g], perturbations, laps[3])
    for t in (2, 1):
        for g in range(GROUPS):
            old = adjoint[t + 2][g] if t < 2 else None
            adjoint[t][g] = wave("adjoint", g, adjoint[t + 1][g], old, born[t + 1][g], counts)
    sketch = []
    for g in range(GROUPS):
        image = wave(
            "image", g, adjoint[1][g], adjoint[2][g], born[1][g], counts, (adjoint[3][g], *laps)
        )
        sketch.append(lax.all_to_all(image, "dirs", split_axis=0, concat_axis=0, tiled=True))

    total_dirs = owners * sketch_count
    local_rows = rows // owners
    spread = pl.pallas_call(
        functools.partial(gram_kernel, GROUPS),
        out_shape=jax.ShapeDtypeStruct((total_dirs, total_dirs, LANE), f32),
        compiler_params=params(),
        name="gram",
    )(*[s.reshape(owners, each, layers * local_rows, columns) for s in sketch])
    gram = add_up(jnp.sum(spread, -1))
    selector = (column_order[:, None] == jnp.arange(total_dirs, dtype=jnp.int32)[None, :]).astype(
        f32
    )
    grid_cells = layers * lax.axis_size("slab") * rows * columns
    square = (total_dirs, total_dirs)
    part = (owners, each, 1, local_rows, columns)
    basis, triangle = pl.pallas_call(
        functools.partial(basis_kernel, GROUPS, math.sqrt(grid_cells)),
        grid=(layers,),
        in_specs=[whole(square)] * 3
        + [pl.BlockSpec(part, lambda l: (0, 0, l, 0, 0))] * GROUPS,
        out_specs=[
            pl.BlockSpec((total_dirs, 1, local_rows, columns), lambda l: (0, l, 0, 0)),
            whole(square),
        ],
        out_shape=(
            jax.ShapeDtypeStruct((total_dirs, layers, local_rows, columns), f32),
            jax.ShapeDtypeStruct(square, f32),
        ),
        scratch_shapes=[pltpu.VMEM((total_dirs * total_dirs, 8, LANE), f32)],
        compiler_params=params(),
        name="basis",
    )(gram, selector, selector.T, *sketch)
    return basis, triangle


def solution(mesh):
    return jax.shard_map(
        shards,
        mesh=mesh,
        in_specs=(
            P("dirs", "slab", None, None),
            P("slab", None, None),
            P("slab", None, None),
            P("slab", None, None),
            P("slab", None, None),
            P("slab", None, None),
            P("slab"),
            P("slab"),
            P("slab"),
            P(),
        ),
        out_specs=(P(None, "slab", "dirs", None), P()),
        check_vma=False,
    )
```

```python
import functools
import math

import jax
import jax.numpy as jnp
from jax import lax
from jax.experimental import pallas as pl
from jax.experimental.pallas import tpu as pltpu
from jax.sharding import PartitionSpec as P

STEPS = 4
DAMPING = 0.3
TAPS = (8064.0, -1008.0, 128.0, -9.0)
CENTRE = 6.0 * sum(TAPS)
HALF = 0.5 / 5040.0
GROUPS = 2
VMEM = 22 * 1024 * 1024
LANE = 128


def band(shape, period):
    row = lax.broadcasted_iota(jnp.int32, shape, 0)
    column = lax.broadcasted_iota(jnp.int32, shape, 1) % period
    distance = jnp.abs(row - column)
    matrix = jnp.zeros(shape, jnp.float32)
    for k, tap in enumerate(TAPS, 1):
        matrix = jnp.where(distance == k, tap, matrix)
    return matrix.astype(jnp.bfloat16)


def source_weight(t):
    return (1.0 - 0.4 * t) * math.exp(-0.125 * t * t)


def params():
    return pltpu.CompilerParams(vmem_limit_bytes=VMEM)


def split_rows(y_ref, slot, layer, row, values, parts, rows):
    size = values.shape[0]
    for s in range(parts):
        part = values.astype(jnp.bfloat16)
        y_ref[slot, layer, s * rows + row : s * rows + row + size, :] = part
        if s < parts - 1:
            values = values - part.astype(jnp.float32)


def plane_part(functions, y_ref, a_ref, mx_ref, my_ref, parts):
    _, layers, rows, _ = a_ref.shape
    for layer in range(layers):
        for row in range(0, rows, 32):
            for slot, values in enumerate(functions(layer, row, 32)):
                split_rows(y_ref, slot, layer, row, values, parts, rows)
    for slot in range(a_ref.shape[0]):
        for layer in range(layers):
            y = y_ref[slot, layer]
            along = jnp.dot(y, mx_ref[...], preferred_element_type=jnp.float32)
            total = jnp.dot(my_ref[...], y, preferred_element_type=jnp.float32)
            for s in range(parts):
                total = total + along[s * rows : (s + 1) * rows]
            a_ref[slot, layer] = total


def depth_part(tall, layer):
    total = None
    for k, tap in enumerate(TAPS, 1):
        term = tap * (tall[layer + 4 + k] + tall[layer + 4 - k])
        total = term if total is None else total + term
    return total


def tall_of(refs, rows, columns):
    low, mid, high = refs
    return [ref[layer, rows, columns] for ref in (low, mid, high) for layer in range(4)]


def tiles(rows, columns, body, start=0):
    def step(i, carry):
        at = pl.ds(pl.multiple_of(start + i * 8, 8), 8)
        for column in range(0, columns, LANE):
            body(i, at, slice(column, column + LANE))
        return carry

    lax.fori_loop(0, rows // 8, step, 0)


def place_kernel(copies, rc_ref, sc_ref, amp_ref, mask_ref, *refs):
    sources, refs = refs[:copies], refs[copies:]
    m_ref, src_ref, taper_ref, mx_ref, my2_ref, my3_ref = refs[:6]
    for source, target in zip(sources, refs[6:]):
        target[...] = source[...]
    layers, rows, columns = m_ref.shape
    for matrix in (mx_ref, my2_ref, my3_ref):
        matrix[...] = band(matrix.shape, matrix.shape[0])
    count = rc_ref.shape[1]
    lines = layers * rows
    chunk = min(256, count)
    total = None
    for start in range(0, count, chunk):
        cells = rc_ref[:, start : start + chunk]
        line = lax.broadcasted_iota(jnp.int32, (lines, chunk), 0) == cells // columns
        column = lax.broadcasted_iota(jnp.int32, (columns, chunk), 0) == cells % columns
        part = lax.dot_general(
            jnp.where(line, 1.0, 0.0).astype(jnp.bfloat16),
            jnp.where(column, 1.0, 0.0).astype(jnp.bfloat16),
            (((1,), (1,)), ((), ())),
            preferred_element_type=jnp.float32,
        )
        total = part if total is None else total + part
    m_ref[...] = total.reshape(m_ref.shape)
    cells = sc_ref[...]
    count = cells.shape[1]
    line = lax.broadcasted_iota(jnp.int32, (lines, count), 0) == cells // columns
    column = lax.broadcasted_iota(jnp.int32, (columns, count), 0) == cells % columns
    part = lax.dot_general(
        jnp.where(line, 1.0, 0.0),
        jnp.where(column, amp_ref[...], 0.0),
        (((1,), (1,)), ((), ())),
        precision=lax.Precision.HIGHEST,
        preferred_element_type=jnp.float32,
    )
    src_ref[...] = part.reshape(src_ref.shape)
    taper_ref[...] = 1.0 - DAMPING * mask_ref[...].astype(jnp.float32)


def background_kernel(weight, first, last, *refs):
    refs = list(refs)
    u = [refs.pop(0) for _ in range(3)]
    b = [refs.pop(0) for _ in range(3)]
    stiff_ref = refs.pop(0)
    dg_ref = None if first else refs.pop(0)
    taper_ref = src_ref = older_ref = new_ref = None
    if not last:
        taper_ref, src_ref, older_ref = (refs.pop(0) for _ in range(3))
    mx_ref, my_ref = refs.pop(0), refs.pop(0)
    lap_ref = refs.pop(0)
    if not last:
        new_ref = refs.pop(0)
    if first:
        dg_ref = refs.pop(0)
    y_ref, a_ref = refs

    def functions(layer, row, size):
        value = u[1][layer, row : row + size]
        buoy = b[1][layer, row : row + size]
        return [value, value * buoy] + ([buoy] if first else [])

    plane_part(functions, y_ref, a_ref, mx_ref, my_ref, 3)

    def body(i, at, columns):
        value = tall_of(u, at, columns)
        buoy = tall_of(b, at, columns)
        both = [x * y for x, y in zip(value, buoy)]
        for layer in range(4):
            here, b_here = value[layer + 4], buoy[layer + 4]
            if first:
                dg = depth_part(buoy, layer) + a_ref[2, layer, at, columns] + CENTRE * b_here
                dg_ref[layer, at, columns] = dg
            else:
                dg = dg_ref[layer, at, columns]
            plain = depth_part(value, layer) + a_ref[0, layer, at, columns]
            times = depth_part(both, layer) + a_ref[1, layer, at, columns]
            lap = HALF * (b_here * plain + times - here * dg)
            lap_ref[layer, at, columns] = lap
            if not last:
                new_ref[layer, at, columns] = (
                    taper_ref[layer, at, columns]
                    * (
                        2.0 * here
                        - older_ref[layer, at, columns]
                        + stiff_ref[layer, at, columns] * lap
                    )
                    + weight * src_ref[layer, at, columns]
                )

    tiles(*lap_ref.shape[1:], body)


def wave_kernel(mode, has_old, *refs):
    refs = list(refs)
    p = [refs.pop(0) for _ in range(3)]
    old_ref = refs.pop(0) if has_old else None
    b = [refs.pop(0) for _ in range(3)]
    dg_ref, stiff_ref = refs.pop(0), refs.pop(0)
    if mode == "image":
        sum_ref, me_ref, weight_ref, near_ref = (refs.pop(0) for _ in range(4))
    else:
        taper_ref, add_ref, lap_ref = (refs.pop(0) for _ in range(3))
    count_ref = refs.pop(0) if mode == "turn" else None
    if mode == "fold":
        first_ref = refs.pop(0)
        laps = [refs.pop(0) for _ in range(4)]
    mx_ref, my_ref = refs.pop(0), refs.pop(0)
    y_ref, a_ref = refs[-2:]
    outs = refs[:-2]

    def functions(layer, row, size):
        value = p[1][layer, row : row + size]
        return value, value * b[1][layer, row : row + size]

    plane_part(functions, y_ref, a_ref, mx_ref, my_ref, 2)

    def body(block, i, at, columns):
        value = tall_of(p, at, columns)
        buoy = tall_of(b, at, columns)
        both = [x * y for x, y in zip(value, buoy)]
        for layer in range(4):
            here = value[layer + 4]
            spot = (layer, at, columns)
            plain = depth_part(value, layer) + a_ref[0, layer, at, columns]
            times = depth_part(both, layer) + a_ref[1, layer, at, columns]
            lb = buoy[layer + 4] * plain + times - here * dg_ref[spot]
            total = 2.0 * here + (HALF * stiff_ref[spot]) * lb
            if mode == "image":
                inner = pl.ds(pl.multiple_of(i * 8, 8), 8)
                outs[block][layer, inner, columns] = (
                    sum_ref[spot] + near_ref[spot] * here + weight_ref[spot] * total
                )
                continue
            if has_old:
                old = old_ref[spot]
                total = total - old
            taper = taper_ref[spot]
            added = add_ref[spot] * lap_ref[spot]
            if mode in ("born", "turn"):
                new = taper * (total + added)
            else:
                new = taper * total + added
            if mode == "turn":
                new = count_ref[spot] * new
            outs[0][spot] = new
            if mode == "fold":
                weight = laps[0][spot] * taper
                known = laps[3][spot] * old + laps[2][spot] * here
                known = known + laps[0][spot] * (lap_ref[spot] * first_ref[spot])
                outs[1][spot] = known - weight * here
                if len(outs) > 2:
                    outs[2][spot] = weight
                    outs[3][spot] = laps[1][spot]

    _, rows, columns = p[1].shape
    if mode == "image":
        per = rows // len(outs)
        for block in range(len(outs)):
            owner = lax.rem(me_ref[0] + block, len(outs))
            tiles(per, columns, functools.partial(body, block), owner * per)
    else:
        tiles(rows, columns, functools.partial(body, 0))


def piece_of(pieces, parts, c):
    each = pieces[0].shape[0]
    block, rest = divmod(c, parts * each)
    group, inner = divmod(rest, each)
    return pieces[group * (len(pieces) // parts) + block], inner


def gram_kernel(parts, sel_ref, selt_ref, *refs):
    *pieces, out_ref, lanes_ref = refs
    count = sel_ref.shape[0]
    _, rows, columns = pieces[0].shape

    def piece(c, at, column):
        ref, inner = piece_of(pieces, parts, c)
        return ref[inner, at, column : column + LANE]

    for i0 in range(0, count, 4):
        for j0 in range(i0 // 8 * 8, count, 8):

            def step(r, accs, i0=i0, j0=j0):
                at = pl.ds(pl.multiple_of(r * 8, 8), 8)
                accs = list(accs)
                for column in range(0, columns, LANE):
                    left = [piece(i0 + i, at, column) for i in range(4)]
                    for j in range(8):
                        right = piece(j0 + j, at, column)
                        for i in range(4):
                            accs[i * 8 + j] = accs[i * 8 + j] + left[i] * right
                return tuple(accs)

            zero = jnp.zeros((8, LANE), jnp.float32)
            accs = lax.fori_loop(0, rows // 8, step, (zero,) * 32)
            for i in range(4):
                for j in range(8):
                    lanes_ref[i0 + i, j0 + j : j0 + j + 1, :] = jnp.sum(
                        accs[i * 8 + j], axis=0, keepdims=True
                    )
    local = jnp.sum(lanes_ref[...], axis=-1)
    row = lax.broadcasted_iota(jnp.int32, local.shape, 0)
    column = lax.broadcasted_iota(jnp.int32, local.shape, 1)
    local = jnp.where(row // 8 > column // 8, local.T, local)
    out_ref[...] = exact(exact(sel_ref[...], local), selt_ref[...])


def exact(left, right):
    return jnp.dot(left, right, precision=lax.Precision.HIGHEST, preferred_element_type=jnp.float32)


def basis_kernel(parts, scale, gram_ref, sel_ref, *refs):
    *pieces, out_ref, triangle_ref, spread_ref = refs
    count = gram_ref.shape[0]
    _, _, rows, columns = pieces[0].shape

    @pl.when(pl.program_id(0) == 0)
    def _():
        row = lax.broadcasted_iota(jnp.int32, (count, count), 0)
        column = lax.broadcasted_iota(jnp.int32, (count, count), 1)
        left = gram_ref[...]
        unit = jnp.where(row == column, 1.0, 0.0)
        for i in range(count):
            pivot = jnp.sqrt(left[i : i + 1, i : i + 1])
            upper = left[i : i + 1, :] / pivot
            solved = unit[i : i + 1, :] / pivot
            below = left[:, i : i + 1] / pivot
            is_row = row == i
            left = jnp.where(is_row, upper, jnp.where(row > i, left - below * upper, left))
            unit = jnp.where(is_row, solved, jnp.where(row > i, unit - below * solved, unit))
        triangle_ref[...] = jnp.where(column >= row, left, 0.0) / scale
        weights = exact(unit, sel_ref[...]) * scale
        for i in range(count):
            for c in range(count):
                spread_ref[i * count + c] = jnp.broadcast_to(
                    weights[i : i + 1, c : c + 1], (8, LANE)
                )

    def piece(c, at, columns):
        ref, inner = piece_of(pieces, parts, c)
        return ref[inner, 0, at, columns]

    halves = [slice(column, column + LANE) for column in range(0, columns, LANE)]
    for r in range(0, rows, 8):
        at = slice(r, r + 8)
        values = [[piece(c, at, half) for half in halves] for c in range(count)]
        for i in range(count):
            totals = [None] * len(halves)
            for c in range(count):
                weight = spread_ref[i * count + c]
                for h in range(len(halves)):
                    term = weight * values[c][h]
                    totals[h] = term if totals[h] is None else totals[h] + term
            for h, half in enumerate(halves):
                out_ref[i, 0, at, half] = totals[h]


def halo(block):
    count = lax.axis_size("slab")
    forward = [(i, i + 1) for i in range(count - 1)]
    backward = [(target, source) for source, target in forward]
    return lax.ppermute(block, "slab", forward), lax.ppermute(block, "slab", backward)


def whole(shape):
    zeros = (0,) * len(shape)
    return pl.BlockSpec(tuple(shape), lambda *_: zeros)


def add_up(value):
    for axis in ("slab", "dirs"):
        size, stride = lax.axis_size(axis), 1
        while stride < size:
            value = value + lax.ppermute(value, axis, [(i, i ^ stride) for i in range(size)])
            stride *= 2
    return value


def shards(
    perturbations,
    background_now,
    background_prev,
    stiffness,
    buoyancy,
    absorb_mask,
    source_cells,
    source_amp,
    receiver_cells,
    column_order,
):
    shape = buoyancy.shape
    layers, rows, columns = shape
    sketch_count = perturbations.shape[0]
    each = sketch_count // GROUPS
    owners = lax.axis_size("dirs")
    me = lax.axis_index("dirs").astype(jnp.int32).reshape(1)
    f32 = jnp.float32
    field = jax.ShapeDtypeStruct(shape, f32)
    cells_here = layers * rows * columns
    b_low, b_high = halo(buoyancy)
    u_low, u_high = halo(background_now)

    def matrix(*size):
        return jax.ShapeDtypeStruct(size, jnp.bfloat16)

    copied = (stiffness, buoyancy, background_now, background_prev)
    matrices = (matrix(columns, columns), matrix(rows, 2 * rows), matrix(rows, 3 * rows))
    (
        counts, source_field, taper, mx, my2, my3, stiffness, b_mid, current, older
    ) = pl.pallas_call(
        functools.partial(place_kernel, len(copied)),
        out_shape=(field,) * 3 + matrices + (field,) * len(copied),
        compiler_params=params(),
        cost_estimate=pl.CostEstimate(
            flops=40 * cells_here, bytes_accessed=16 * cells_here, transcendentals=0
        ),
        name="place",
    )(
        receiver_cells.reshape(1, -1),
        source_cells.reshape(1, -1),
        source_amp.reshape(1, -1),
        absorb_mask,
        *copied,
    )

    buoy = (b_low, b_mid, b_high)
    fields = [current]
    laps = []
    dg = None
    for t in range(STEPS):
        first, last = t == 0, t == STEPS - 1
        if not first:
            u_low, u_high = halo(current)
        operands = [u_low, current, u_high, *buoy, stiffness]
        if not first:
            operands.append(dg)
        if not last:
            operands += [taper, source_field, older]
        operands += [mx, my3]
        slots = 3 if first else 2
        results = pl.pallas_call(
            functools.partial(background_kernel, source_weight(t), first, last),
            out_shape=(field,) * (1 + (not last) + first),
            scratch_shapes=[
                pltpu.VMEM((slots, layers, 3 * rows, columns), jnp.bfloat16),
                pltpu.VMEM((slots, layers, rows, columns), f32),
            ],
            compiler_params=params(),
            cost_estimate=pl.CostEstimate(
                flops=60 * cells_here, bytes_accessed=56 * cells_here, transcendentals=0
            ),
            name=f"background{t}",
        )(*operands)
        results = list(results)
        laps.append(results.pop(0))
        if not last:
            older, current = current, results.pop(0)
            fields.append(current)
        if first:
            dg = results.pop(0)

    def wave(mode, group, p, old, add, lap, extra=()):
        low, high = halo(p)
        one = pl.BlockSpec((None, *shape), lambda d: (d, 0, 0, 0))
        shifted = pl.BlockSpec((None, *shape), lambda d: (d + group * each, 0, 0, 0))
        same = whole(shape)
        operands, specs = [low, p, high], [one] * 3
        if old is not None:
            operands.append(old)
            specs.append(one)
        operands += [*buoy, dg, stiffness]
        specs += [same] * 5
        if mode != "image":
            operands += [taper, add, lap]
            specs += [same, shifted if mode in ("born", "turn") else one, same]
        if mode == "turn":
            operands.append(counts)
            specs.append(same)
        if mode == "fold":
            specs += [one] + [same] * 4
        if mode == "image":
            specs += [one, pl.BlockSpec(memory_space=pltpu.SMEM)] + [same] * 2
        operands += [*extra, mx, my2]
        specs += [whole(mx.shape), whole(my2.shape)]
        out_shape, out_spec = (jax.ShapeDtypeStruct((each, *shape), f32),), [one]
        if mode == "fold":
            out_shape, out_spec = out_shape * 2, out_spec * 2
            if group == 0:
                out_shape, out_spec = out_shape + (field,) * 2, out_spec + [same] * 2
        elif mode == "image":
            split = (layers, rows // owners, columns)
            out_shape = (jax.ShapeDtypeStruct((each, *split), f32),) * owners
            out_spec = [pl.BlockSpec((None, *split), lambda d: (d, 0, 0, 0))] * owners
        results = pl.pallas_call(
            functools.partial(wave_kernel, mode, old is not None),
            grid=(each,),
            in_specs=specs,
            out_specs=out_spec,
            out_shape=out_shape,
            scratch_shapes=[
                pltpu.VMEM((2, layers, 2 * rows, columns), jnp.bfloat16),
                pltpu.VMEM((2, layers, rows, columns), f32),
            ],
            compiler_params=params(),
            cost_estimate=pl.CostEstimate(
                flops=60 * each * cells_here,
                bytes_accessed=28 * each * cells_here,
                transcendentals=0,
            ),
            name=mode,
        )(*operands)
        return results[0] if len(results) == 1 else results

    def after(value, earlier):
        return lax.optimization_barrier((value, earlier))[0]

    born = [[None] * GROUPS for _ in range(STEPS + 1)]
    for g in range(GROUPS):
        mine = perturbations[g * each : (g + 1) * each]
        born[1][g] = taper * (mine * laps[0])
    born[1][1] = after(born[1][1], fields[2])
    ahead = {(2, 1): fields[3]}
    for t in (1, 2):
        for g in range(GROUPS):
            old = born[t - 1][g] if t > 1 else None
            new = wave("born", g, born[t][g], old, perturbations, laps[t])
            if (t + 1, g) in ahead:
                new = after(new, ahead[t + 1, g])
            born[t + 1][g] = new
    adjoint = [[None] * GROUPS for _ in range(STEPS + 1)]
    for g in range(GROUPS):
        adjoint[3][g] = wave("turn", g, born[3][g], born[2][g], perturbations, laps[3])
    for g in range(GROUPS):
        adjoint[2][g] = wave("adjoint", g, adjoint[3][g], None, born[3][g], counts)
    known = [None] * GROUPS
    for g in range(GROUPS):
        adjoint[1][g], known[g], *rest = wave(
            "fold", g, adjoint[2][g], adjoint[3][g], born[2][g], counts, (born[1][g], *laps)
        )
        if g == 0:
            weight, near = rest
    sketch = []
    for g in range(GROUPS):
        blocks = wave(
            "image", g, adjoint[1][g], None, None, None, (known[g], me, weight, near)
        )
        sketch.append(blocks[0])
        for s in range(1, owners):
            ring = [(i, (i + s) % owners) for i in range(owners)]
            sketch.append(lax.ppermute(blocks[s], "dirs", ring))

    total_dirs = owners * sketch_count
    local_rows = rows // owners
    square = (total_dirs, total_dirs)
    place = jnp.arange(total_dirs, dtype=jnp.int32)
    owner = (me[0] - place // sketch_count + owners) % owners
    local = owner * sketch_count + place % sketch_count
    selector = (column_order[:, None] == local[None, :]).astype(f32)
    gram = pl.pallas_call(
        functools.partial(gram_kernel, GROUPS),
        out_shape=jax.ShapeDtypeStruct(square, f32),
        scratch_shapes=[pltpu.VMEM((*square, LANE), f32)],
        compiler_params=params(),
        name="gram",
    )(selector, selector.T, *[s.reshape(each, layers * local_rows, columns) for s in sketch])
    gram = add_up(gram)
    grid_cells = layers * lax.axis_size("slab") * rows * columns
    part = (each, 1, local_rows, columns)
    basis, triangle = pl.pallas_call(
        functools.partial(basis_kernel, GROUPS, math.sqrt(grid_cells)),
        grid=(layers,),
        in_specs=[whole(square)] * 2
        + [pl.BlockSpec(part, lambda l: (0, l, 0, 0))] * len(sketch),
        out_specs=[
            pl.BlockSpec((total_dirs, 1, local_rows, columns), lambda l: (0, l, 0, 0)),
            whole(square),
        ],
        out_shape=(
            jax.ShapeDtypeStruct((total_dirs, layers, local_rows, columns), f32),
            jax.ShapeDtypeStruct(square, f32),
        ),
        scratch_shapes=[pltpu.VMEM((total_dirs * total_dirs, 8, LANE), f32)],
        compiler_params=params(),
        name="basis",
    )(gram, selector, *sketch)
    return basis, triangle


def solution(mesh):
    return jax.shard_map(
        shards,
        mesh=mesh,
        in_specs=(
            P("dirs", "slab", None, None),
            P("slab", None, None),
            P("slab", None, None),
            P("slab", None, None),
            P("slab", None, None),
            P("slab", None, None),
            P("slab"),
            P("slab"),
            P("slab"),
            P(),
        ),
        out_specs=(P(None, "slab", "dirs", None), P()),
        check_vma=False,
    )
```

```python
import functools
import math

import jax
import jax.numpy as jnp
from jax import lax
from jax.experimental import pallas as pl
from jax.experimental.pallas import tpu as pltpu
from jax.sharding import PartitionSpec as P

STEPS = 4
DAMPING = 0.3
TAPS = (8064.0, -1008.0, 128.0, -9.0)
CENTRE = 6.0 * sum(TAPS)
HALF = 0.5 / 5040.0
GROUPS = 2
VMEM = 22 * 1024 * 1024
LANE = 128


def band(shape, period):
    row = lax.broadcasted_iota(jnp.int32, shape, 0)
    column = lax.broadcasted_iota(jnp.int32, shape, 1) % period
    distance = jnp.abs(row - column)
    matrix = jnp.zeros(shape, jnp.float32)
    for k, tap in enumerate(TAPS, 1):
        matrix = jnp.where(distance == k, tap, matrix)
    return matrix.astype(jnp.bfloat16)


def source_weight(t):
    return (1.0 - 0.4 * t) * math.exp(-0.125 * t * t)


def params():
    return pltpu.CompilerParams(vmem_limit_bytes=VMEM)


def split_rows(y_ref, slot, layer, row, values, parts, rows):
    size = values.shape[0]
    for s in range(parts):
        part = values.astype(jnp.bfloat16)
        y_ref[slot, layer, s * rows + row : s * rows + row + size, :] = part
        if s < parts - 1:
            values = values - part.astype(jnp.float32)


def plane_part(functions, y_ref, a_ref, mx_ref, my_ref, parts):
    _, layers, rows, _ = a_ref.shape
    for layer in range(layers):
        for row in range(0, rows, 32):
            for slot, values in enumerate(functions(layer, row, 32)):
                split_rows(y_ref, slot, layer, row, values, parts, rows)
    for slot in range(a_ref.shape[0]):
        for layer in range(layers):
            y = y_ref[slot, layer]
            along = jnp.dot(y, mx_ref[...], preferred_element_type=jnp.float32)
            total = jnp.dot(my_ref[...], y, preferred_element_type=jnp.float32)
            for s in range(parts):
                total = total + along[s * rows : (s + 1) * rows]
            a_ref[slot, layer] = total


def depth_part(tall, layer):
    total = None
    for k, tap in enumerate(TAPS, 1):
        term = tap * (tall[layer + 4 + k] + tall[layer + 4 - k])
        total = term if total is None else total + term
    return total


def tall_of(refs, rows, columns):
    low, mid, high = refs
    return [ref[layer, rows, columns] for ref in (low, mid, high) for layer in range(4)]


def tiles(rows, columns, body, start=0):
    def step(i, carry):
        at = pl.ds(pl.multiple_of(start + i * 8, 8), 8)
        for column in range(0, columns, LANE):
            body(i, at, slice(column, column + LANE))
        return carry

    lax.fori_loop(0, rows // 8, step, 0)


def place_kernel(copies, rc_ref, sc_ref, amp_ref, mask_ref, *refs):
    sources, refs = refs[:copies], refs[copies:]
    m_ref, src_ref, taper_ref, mx_ref, my2_ref, my3_ref = refs[:6]
    for source, target in zip(sources, refs[6:]):
        target[...] = source[...]
    layers, rows, columns = m_ref.shape
    for matrix in (mx_ref, my2_ref, my3_ref):
        matrix[...] = band(matrix.shape, matrix.shape[0])
    count = rc_ref.shape[1]
    lines = layers * rows
    chunk = min(256, count)
    total = None
    for start in range(0, count, chunk):
        cells = rc_ref[:, start : start + chunk]
        line = lax.broadcasted_iota(jnp.int32, (lines, chunk), 0) == cells // columns
        column = lax.broadcasted_iota(jnp.int32, (columns, chunk), 0) == cells % columns
        part = lax.dot_general(
            jnp.where(line, 1.0, 0.0).astype(jnp.bfloat16),
            jnp.where(column, 1.0, 0.0).astype(jnp.bfloat16),
            (((1,), (1,)), ((), ())),
            preferred_element_type=jnp.float32,
        )
        total = part if total is None else total + part
    m_ref[...] = total.reshape(m_ref.shape)
    cells = sc_ref[...]
    count = cells.shape[1]
    line = lax.broadcasted_iota(jnp.int32, (lines, count), 0) == cells // columns
    column = lax.broadcasted_iota(jnp.int32, (columns, count), 0) == cells % columns
    part = lax.dot_general(
        jnp.where(line, 1.0, 0.0),
        jnp.where(column, amp_ref[...], 0.0),
        (((1,), (1,)), ((), ())),
        precision=lax.Precision.HIGHEST,
        preferred_element_type=jnp.float32,
    )
    src_ref[...] = part.reshape(src_ref.shape)
    taper_ref[...] = 1.0 - DAMPING * mask_ref[...].astype(jnp.float32)


def background_kernel(weight, first, last, *refs):
    refs = list(refs)
    u = [refs.pop(0) for _ in range(3)]
    b = [refs.pop(0) for _ in range(3)]
    stiff_ref = refs.pop(0)
    dg_ref = None if first else refs.pop(0)
    taper_ref = src_ref = older_ref = new_ref = None
    if not last:
        taper_ref, src_ref, older_ref = (refs.pop(0) for _ in range(3))
    mx_ref, my_ref = refs.pop(0), refs.pop(0)
    lap_ref = refs.pop(0)
    if not last:
        new_ref = refs.pop(0)
    if first:
        dg_ref = refs.pop(0)
    y_ref, a_ref = refs

    def functions(layer, row, size):
        value = u[1][layer, row : row + size]
        buoy = b[1][layer, row : row + size]
        return [value, value * buoy] + ([buoy] if first else [])

    plane_part(functions, y_ref, a_ref, mx_ref, my_ref, 3)

    def body(i, at, columns):
        value = tall_of(u, at, columns)
        buoy = tall_of(b, at, columns)
        both = [x * y for x, y in zip(value, buoy)]
        for layer in range(4):
            here, b_here = value[layer + 4], buoy[layer + 4]
            if first:
                dg = depth_part(buoy, layer) + a_ref[2, layer, at, columns] + CENTRE * b_here
                dg_ref[layer, at, columns] = dg
            else:
                dg = dg_ref[layer, at, columns]
            plain = depth_part(value, layer) + a_ref[0, layer, at, columns]
            times = depth_part(both, layer) + a_ref[1, layer, at, columns]
            lap = HALF * (b_here * plain + times - here * dg)
            lap_ref[layer, at, columns] = lap
            if not last:
                new_ref[layer, at, columns] = (
                    taper_ref[layer, at, columns]
                    * (
                        2.0 * here
                        - older_ref[layer, at, columns]
                        + stiff_ref[layer, at, columns] * lap
                    )
                    + weight * src_ref[layer, at, columns]
                )

    tiles(*lap_ref.shape[1:], body)


def wave_kernel(mode, has_old, *refs):
    refs = list(refs)
    p = [refs.pop(0) for _ in range(3)]
    old_ref = refs.pop(0) if has_old else None
    b = [refs.pop(0) for _ in range(3)]
    dg_ref, stiff_ref = refs.pop(0), refs.pop(0)
    if mode == "image":
        sum_ref, me_ref, weight_ref, near_ref = (refs.pop(0) for _ in range(4))
    else:
        taper_ref, add_ref, lap_ref = (refs.pop(0) for _ in range(3))
    count_ref = refs.pop(0) if mode == "turn" else None
    if mode == "fold":
        first_ref = refs.pop(0)
        laps = [refs.pop(0) for _ in range(4)]
    mx_ref, my_ref = refs.pop(0), refs.pop(0)
    y_ref, a_ref = refs[-2:]
    outs = refs[:-2]

    def functions(layer, row, size):
        value = p[1][layer, row : row + size]
        return value, value * b[1][layer, row : row + size]

    plane_part(functions, y_ref, a_ref, mx_ref, my_ref, 2)

    def body(block, i, at, columns):
        value = tall_of(p, at, columns)
        buoy = tall_of(b, at, columns)
        both = [x * y for x, y in zip(value, buoy)]
        for layer in range(4):
            here = value[layer + 4]
            spot = (layer, at, columns)
            plain = depth_part(value, layer) + a_ref[0, layer, at, columns]
            times = depth_part(both, layer) + a_ref[1, layer, at, columns]
            lb = buoy[layer + 4] * plain + times - here * dg_ref[spot]
            total = 2.0 * here + (HALF * stiff_ref[spot]) * lb
            if mode == "image":
                inner = pl.ds(pl.multiple_of(i * 8, 8), 8)
                outs[block][layer, inner, columns] = (
                    sum_ref[spot] + near_ref[spot] * here + weight_ref[spot] * total
                )
                continue
            if has_old:
                old = old_ref[spot]
                total = total - old
            taper = taper_ref[spot]
            added = add_ref[spot] * lap_ref[spot]
            if mode in ("born", "turn"):
                new = taper * (total + added)
            else:
                new = taper * total + added
            if mode == "turn":
                new = count_ref[spot] * new
            outs[0][spot] = new
            if mode == "fold":
                weight = laps[0][spot] * taper
                known = laps[3][spot] * old + laps[2][spot] * here
                known = known + laps[0][spot] * (lap_ref[spot] * first_ref[spot])
                outs[1][spot] = known - weight * here
                if len(outs) > 2:
                    outs[2][spot] = weight
                    outs[3][spot] = laps[1][spot]

    _, rows, columns = p[1].shape
    if mode == "image":
        per = rows // len(outs)
        for block in range(len(outs)):
            owner = lax.rem(me_ref[0] + block, len(outs))
            tiles(per, columns, functools.partial(body, block), owner * per)
    else:
        tiles(rows, columns, functools.partial(body, 0))


def piece_of(pieces, parts, c):
    each = pieces[0].shape[0]
    block, rest = divmod(c, parts * each)
    group, inner = divmod(rest, each)
    return pieces[group * (len(pieces) // parts) + block], inner


def gram_kernel(parts, sel_ref, selt_ref, *refs):
    *pieces, out_ref, lanes_ref = refs
    count = sel_ref.shape[0]
    _, rows, columns = pieces[0].shape

    def piece(c, at, column):
        ref, inner = piece_of(pieces, parts, c)
        return ref[inner, at, column : column + LANE]

    for i0 in range(0, count, 4):
        for j0 in range(i0 // 8 * 8, count, 8):

            def step(r, accs, i0=i0, j0=j0):
                at = pl.ds(pl.multiple_of(r * 8, 8), 8)
                accs = list(accs)
                for column in range(0, columns, LANE):
                    left = [piece(i0 + i, at, column) for i in range(4)]
                    for j in range(8):
                        right = piece(j0 + j, at, column)
                        for i in range(4):
                            accs[i * 8 + j] = accs[i * 8 + j] + left[i] * right
                return tuple(accs)

            zero = jnp.zeros((8, LANE), jnp.float32)
            accs = lax.fori_loop(0, rows // 8, step, (zero,) * 32)
            for i in range(4):
                for j in range(8):
                    lanes_ref[i0 + i, j0 + j : j0 + j + 1, :] = jnp.sum(
                        accs[i * 8 + j], axis=0, keepdims=True
                    )
    local = jnp.sum(lanes_ref[...], axis=-1)
    row = lax.broadcasted_iota(jnp.int32, local.shape, 0)
    column = lax.broadcasted_iota(jnp.int32, local.shape, 1)
    local = jnp.where(row // 8 > column // 8, local.T, local)
    out_ref[...] = exact(exact(sel_ref[...], local), selt_ref[...])


def exact(left, right):
    return jnp.dot(left, right, precision=lax.Precision.HIGHEST, preferred_element_type=jnp.float32)


def basis_kernel(parts, scale, gram_ref, sel_ref, *refs):
    *pieces, out_ref, triangle_ref, spread_ref = refs
    count = gram_ref.shape[0]
    _, _, rows, columns = pieces[0].shape

    @pl.when(pl.program_id(0) == 0)
    def _():
        row = lax.broadcasted_iota(jnp.int32, (count, count), 0)
        column = lax.broadcasted_iota(jnp.int32, (count, count), 1)
        left = gram_ref[...]
        unit = jnp.where(row == column, 1.0, 0.0)
        for i in range(count):
            pivot = jnp.sqrt(left[i : i + 1, i : i + 1])
            upper = left[i : i + 1, :] / pivot
            solved = unit[i : i + 1, :] / pivot
            below = left[:, i : i + 1] / pivot
            is_row = row == i
            left = jnp.where(is_row, upper, jnp.where(row > i, left - below * upper, left))
            unit = jnp.where(is_row, solved, jnp.where(row > i, unit - below * solved, unit))
        triangle_ref[...] = jnp.where(column >= row, left, 0.0) / scale
        weights = exact(unit, sel_ref[...]) * scale
        for i in range(count):
            for c in range(count):
                spread_ref[i * count + c] = jnp.broadcast_to(
                    weights[i : i + 1, c : c + 1], (8, LANE)
                )

    def piece(c, at, columns):
        ref, inner = piece_of(pieces, parts, c)
        return ref[inner, 0, at, columns]

    halves = [slice(column, column + LANE) for column in range(0, columns, LANE)]
    for r in range(0, rows, 8):
        at = slice(r, r + 8)
        values = [[piece(c, at, half) for half in halves] for c in range(count)]
        for i in range(count):
            totals = [None] * len(halves)
            for c in range(count):
                weight = spread_ref[i * count + c]
                for h in range(len(halves)):
                    term = weight * values[c][h]
                    totals[h] = term if totals[h] is None else totals[h] + term
            for h, half in enumerate(halves):
                out_ref[i, 0, at, half] = totals[h]


def halo(block):
    count = lax.axis_size("slab")
    forward = [(i, i + 1) for i in range(count - 1)]
    backward = [(target, source) for source, target in forward]
    return lax.ppermute(block, "slab", forward), lax.ppermute(block, "slab", backward)


def whole(shape):
    zeros = (0,) * len(shape)
    return pl.BlockSpec(tuple(shape), lambda *_: zeros)


def add_up(value):
    for axis in ("slab", "dirs"):
        size, stride = lax.axis_size(axis), 1
        while stride < size:
            value = value + lax.ppermute(value, axis, [(i, i ^ stride) for i in range(size)])
            stride *= 2
    return value


def shards(
    perturbations,
    background_now,
    background_prev,
    stiffness,
    buoyancy,
    absorb_mask,
    source_cells,
    source_amp,
    receiver_cells,
    column_order,
):
    shape = buoyancy.shape
    layers, rows, columns = shape
    sketch_count = perturbations.shape[0]
    each = sketch_count // GROUPS
    owners = lax.axis_size("dirs")
    me = lax.axis_index("dirs").astype(jnp.int32).reshape(1)
    f32 = jnp.float32
    field = jax.ShapeDtypeStruct(shape, f32)
    cells_here = layers * rows * columns
    b_low, b_high = halo(buoyancy)
    u_low, u_high = halo(background_now)

    def matrix(*size):
        return jax.ShapeDtypeStruct(size, jnp.bfloat16)

    copied = (stiffness, buoyancy, background_now, background_prev)
    matrices = (matrix(columns, columns), matrix(rows, 2 * rows), matrix(rows, 3 * rows))
    (
        counts, source_field, taper, mx, my2, my3, stiffness, b_mid, current, older
    ) = pl.pallas_call(
        functools.partial(place_kernel, len(copied)),
        out_shape=(field,) * 3 + matrices + (field,) * len(copied),
        compiler_params=params(),
        cost_estimate=pl.CostEstimate(
            flops=40 * cells_here, bytes_accessed=16 * cells_here, transcendentals=0
        ),
        name="place",
    )(
        receiver_cells.reshape(1, -1),
        source_cells.reshape(1, -1),
        source_amp.reshape(1, -1),
        absorb_mask,
        *copied,
    )

    buoy = (b_low, b_mid, b_high)
    fields = [current]
    laps = []
    dg = None
    for t in range(STEPS):
        first, last = t == 0, t == STEPS - 1
        if not first:
            u_low, u_high = halo(current)
        operands = [u_low, current, u_high, *buoy, stiffness]
        if not first:
            operands.append(dg)
        if not last:
            operands += [taper, source_field, older]
        operands += [mx, my3]
        slots = 3 if first else 2
        results = pl.pallas_call(
            functools.partial(background_kernel, source_weight(t), first, last),
            out_shape=(field,) * (1 + (not last) + first),
            scratch_shapes=[
                pltpu.VMEM((slots, layers, 3 * rows, columns), jnp.bfloat16),
                pltpu.VMEM((slots, layers, rows, columns), f32),
            ],
            compiler_params=params(),
            cost_estimate=pl.CostEstimate(
                flops=60 * cells_here, bytes_accessed=56 * cells_here, transcendentals=0
            ),
            name=f"background{t}",
        )(*operands)
        results = list(results)
        laps.append(results.pop(0))
        if not last:
            older, current = current, results.pop(0)
            fields.append(current)
        if first:
            dg = results.pop(0)

    def wave(mode, group, p, old, add, lap, extra=()):
        low, high = halo(p)
        one = pl.BlockSpec((None, *shape), lambda d: (d, 0, 0, 0))
        shifted = pl.BlockSpec((None, *shape), lambda d: (d + group * each, 0, 0, 0))
        same = whole(shape)
        operands, specs = [low, p, high], [one] * 3
        if old is not None:
            operands.append(old)
            specs.append(one)
        operands += [*buoy, dg, stiffness]
        specs += [same] * 5
        if mode != "image":
            operands += [taper, add, lap]
            specs += [same, shifted if mode in ("born", "turn") else one, same]
        if mode == "turn":
            operands.append(counts)
            specs.append(same)
        if mode == "fold":
            specs += [one] + [same] * 4
        if mode == "image":
            specs += [one, pl.BlockSpec(memory_space=pltpu.SMEM)] + [same] * 2
        operands += [*extra, mx, my2]
        specs += [whole(mx.shape), whole(my2.shape)]
        out_shape, out_spec = (jax.ShapeDtypeStruct((each, *shape), f32),), [one]
        if mode == "fold":
            out_shape, out_spec = out_shape * 2, out_spec * 2
            if group == 0:
                out_shape, out_spec = out_shape + (field,) * 2, out_spec + [same] * 2
        elif mode == "image":
            split = (layers, rows // owners, columns)
            out_shape = (jax.ShapeDtypeStruct((each, *split), f32),) * owners
            out_spec = [pl.BlockSpec((None, *split), lambda d: (d, 0, 0, 0))] * owners
        results = pl.pallas_call(
            functools.partial(wave_kernel, mode, old is not None),
            grid=(each,),
            in_specs=specs,
            out_specs=out_spec,
            out_shape=out_shape,
            scratch_shapes=[
                pltpu.VMEM((2, layers, 2 * rows, columns), jnp.bfloat16),
                pltpu.VMEM((2, layers, rows, columns), f32),
            ],
            compiler_params=params(),
            cost_estimate=pl.CostEstimate(
                flops=60 * each * cells_here,
                bytes_accessed=28 * each * cells_here,
                transcendentals=0,
            ),
            name=mode,
        )(*operands)
        return results[0] if len(results) == 1 else results

    def after(value, earlier):
        return lax.optimization_barrier((value, earlier))[0]

    born = [[None] * GROUPS for _ in range(STEPS + 1)]
    for g in range(GROUPS):
        mine = perturbations[g * each : (g + 1) * each]
        born[1][g] = taper * (mine * laps[0])
    born[1][1] = after(born[1][1], fields[2])
    ahead = {(2, 1): fields[3], (3, 1): laps[3]}
    for t in (1, 2):
        for g in range(GROUPS):
            old = born[t - 1][g] if t > 1 else None
            new = wave("born", g, born[t][g], old, perturbations, laps[t])
            if (t + 1, g) in ahead:
                new = after(new, ahead[t + 1, g])
            born[t + 1][g] = new
    adjoint = [[None] * GROUPS for _ in range(STEPS + 1)]
    for g in range(GROUPS):
        adjoint[3][g] = wave("turn", g, born[3][g], born[2][g], perturbations, laps[3])
    for g in range(GROUPS):
        adjoint[2][g] = wave("adjoint", g, adjoint[3][g], None, born[3][g], counts)
    known = [None] * GROUPS
    for g in range(GROUPS):
        adjoint[1][g], known[g], *rest = wave(
            "fold", g, adjoint[2][g], adjoint[3][g], born[2][g], counts, (born[1][g], *laps)
        )
        if g == 0:
            weight, near = rest
    sketch = []
    for g in range(GROUPS):
        blocks = wave(
            "image", g, adjoint[1][g], None, None, None, (known[g], me, weight, near)
        )
        sketch.append(blocks[0])
        for s in range(1, owners):
            ring = [(i, (i + s) % owners) for i in range(owners)]
            sketch.append(lax.ppermute(blocks[s], "dirs", ring))

    total_dirs = owners * sketch_count
    local_rows = rows // owners
    square = (total_dirs, total_dirs)
    place = jnp.arange(total_dirs, dtype=jnp.int32)
    owner = (me[0] - place // sketch_count + owners) % owners
    local = owner * sketch_count + place % sketch_count
    selector = (column_order[:, None] == local[None, :]).astype(f32)
    gram = pl.pallas_call(
        functools.partial(gram_kernel, GROUPS),
        out_shape=jax.ShapeDtypeStruct(square, f32),
        scratch_shapes=[pltpu.VMEM((*square, LANE), f32)],
        compiler_params=params(),
        name="gram",
    )(selector, selector.T, *[s.reshape(each, layers * local_rows, columns) for s in sketch])
    gram = add_up(gram)
    grid_cells = layers * lax.axis_size("slab") * rows * columns
    part = (each, 1, local_rows, columns)
    basis, triangle = pl.pallas_call(
        functools.partial(basis_kernel, GROUPS, math.sqrt(grid_cells)),
        grid=(layers,),
        in_specs=[whole(square)] * 2
        + [pl.BlockSpec(part, lambda l: (0, l, 0, 0))] * len(sketch),
        out_specs=[
            pl.BlockSpec((total_dirs, 1, local_rows, columns), lambda l: (0, l, 0, 0)),
            whole(square),
        ],
        out_shape=(
            jax.ShapeDtypeStruct((total_dirs, layers, local_rows, columns), f32),
            jax.ShapeDtypeStruct(square, f32),
        ),
        scratch_shapes=[pltpu.VMEM((total_dirs * total_dirs, 8, LANE), f32)],
        compiler_params=params(),
        name="basis",
    )(gram, selector, *sketch)
    return basis, triangle


def solution(mesh):
    return jax.shard_map(
        shards,
        mesh=mesh,
        in_specs=(
            P("dirs", "slab", None, None),
            P("slab", None, None),
            P("slab", None, None),
            P("slab", None, None),
            P("slab", None, None),
            P("slab", None, None),
            P("slab"),
            P("slab"),
            P("slab"),
            P(),
        ),
        out_specs=(P(None, "slab", "dirs", None), P()),
        check_vma=False,
    )
```

```python
import functools
import math

import jax
import jax.numpy as jnp
from jax import lax
from jax.experimental import pallas as pl
from jax.experimental.pallas import tpu as pltpu
from jax.sharding import PartitionSpec as P

STEPS = 4
DAMPING = 0.3
TAPS = (8064.0, -1008.0, 128.0, -9.0)
CENTRE = 6.0 * sum(TAPS)
HALF = 0.5 / 5040.0
GROUPS = 2
VMEM = 22 * 1024 * 1024
LANE = 128


def band(shape, period):
    row = lax.broadcasted_iota(jnp.int32, shape, 0)
    column = lax.broadcasted_iota(jnp.int32, shape, 1) % period
    distance = jnp.abs(row - column)
    matrix = jnp.zeros(shape, jnp.float32)
    for k, tap in enumerate(TAPS, 1):
        matrix = jnp.where(distance == k, tap, matrix)
    return matrix.astype(jnp.bfloat16)


def source_weight(t):
    return (1.0 - 0.4 * t) * math.exp(-0.125 * t * t)


def params():
    return pltpu.CompilerParams(vmem_limit_bytes=VMEM)


def split_rows(y_ref, slot, layer, row, values, parts, rows):
    size = values.shape[0]
    for s in range(parts):
        part = values.astype(jnp.bfloat16)
        y_ref[slot, layer, s * rows + row : s * rows + row + size, :] = part
        if s < parts - 1:
            values = values - part.astype(jnp.float32)


def plane_part(functions, y_ref, a_ref, mx_ref, my_ref, parts):
    _, layers, rows, _ = a_ref.shape
    for layer in range(layers):
        for row in range(0, rows, 32):
            for slot, values in enumerate(functions(layer, row, 32)):
                split_rows(y_ref, slot, layer, row, values, parts, rows)
    for slot in range(a_ref.shape[0]):
        for layer in range(layers):
            y = y_ref[slot, layer]
            along = jnp.dot(y, mx_ref[...], preferred_element_type=jnp.float32)
            total = jnp.dot(my_ref[...], y, preferred_element_type=jnp.float32)
            for s in range(parts):
                total = total + along[s * rows : (s + 1) * rows]
            a_ref[slot, layer] = total


def depth_part(tall, layer):
    total = None
    for k, tap in enumerate(TAPS, 1):
        term = tap * (tall[layer + 4 + k] + tall[layer + 4 - k])
        total = term if total is None else total + term
    return total


def tall_of(refs, rows, columns):
    low, mid, high = refs
    return [ref[layer, rows, columns] for ref in (low, mid, high) for layer in range(4)]


def tiles(rows, columns, body, start=0):
    def step(i, carry):
        at = pl.ds(pl.multiple_of(start + i * 8, 8), 8)
        for column in range(0, columns, LANE):
            body(i, at, slice(column, column + LANE))
        return carry

    lax.fori_loop(0, rows // 8, step, 0)


def place_kernel(copies, rc_ref, sc_ref, amp_ref, mask_ref, *refs):
    sources, refs = refs[:copies], refs[copies:]
    m_ref, src_ref, taper_ref, mx_ref, my2_ref, my3_ref = refs[:6]
    for source, target in zip(sources, refs[6:]):
        target[...] = source[...]
    layers, rows, columns = m_ref.shape
    for matrix in (mx_ref, my2_ref, my3_ref):
        matrix[...] = band(matrix.shape, matrix.shape[0])
    count = rc_ref.shape[1]
    lines = layers * rows
    chunk = min(256, count)
    total = None
    for start in range(0, count, chunk):
        cells = rc_ref[:, start : start + chunk]
        line = lax.broadcasted_iota(jnp.int32, (lines, chunk), 0) == cells // columns
        column = lax.broadcasted_iota(jnp.int32, (columns, chunk), 0) == cells % columns
        part = lax.dot_general(
            jnp.where(line, 1.0, 0.0).astype(jnp.bfloat16),
            jnp.where(column, 1.0, 0.0).astype(jnp.bfloat16),
            (((1,), (1,)), ((), ())),
            preferred_element_type=jnp.float32,
        )
        total = part if total is None else total + part
    m_ref[...] = total.reshape(m_ref.shape)
    cells = sc_ref[...]
    count = cells.shape[1]
    line = lax.broadcasted_iota(jnp.int32, (lines, count), 0) == cells // columns
    column = lax.broadcasted_iota(jnp.int32, (columns, count), 0) == cells % columns
    part = lax.dot_general(
        jnp.where(line, 1.0, 0.0),
        jnp.where(column, amp_ref[...], 0.0),
        (((1,), (1,)), ((), ())),
        precision=lax.Precision.HIGHEST,
        preferred_element_type=jnp.float32,
    )
    src_ref[...] = part.reshape(src_ref.shape)
    taper_ref[...] = 1.0 - DAMPING * mask_ref[...].astype(jnp.float32)


def marks_kernel(cells_ref, line_ref, column_ref):
    cells = cells_ref[...]
    columns = column_ref.shape[0]
    line = lax.broadcasted_iota(jnp.int32, line_ref.shape, 0) == cells // columns
    column = lax.broadcasted_iota(jnp.int32, column_ref.shape, 0) == cells % columns
    line_ref[...] = jnp.where(line, 1.0, 0.0).astype(jnp.bfloat16)
    column_ref[...] = jnp.where(column, 1.0, 0.0)


def halves(values):
    high = values.astype(jnp.bfloat16)
    return high, (values - high.astype(jnp.float32)).astype(jnp.bfloat16)


def read_at(field, line_ref, column_ref):
    total = None
    for part in halves(field):
        lines = lax.dot_general(
            part, line_ref[...], (((0,), (0,)), ((), ())), preferred_element_type=jnp.float32
        )
        total = lines if total is None else total + lines
    return jnp.sum(total * column_ref[...], axis=0, keepdims=True)


def add_at(records, line_ref, column_ref):
    total = None
    for part in halves(records):
        spread = (column_ref[...] * part.astype(jnp.float32)).astype(jnp.bfloat16)
        field = lax.dot_general(
            line_ref[...], spread, (((1,), (1,)), ((), ())), preferred_element_type=jnp.float32
        )
        total = field if total is None else total + field
    return total


def background_kernel(weight, first, last, *refs):
    refs = list(refs)
    u = [refs.pop(0) for _ in range(3)]
    b = [refs.pop(0) for _ in range(3)]
    stiff_ref = refs.pop(0)
    dg_ref = None if first else refs.pop(0)
    taper_ref = src_ref = older_ref = new_ref = None
    if not last:
        taper_ref, src_ref, older_ref = (refs.pop(0) for _ in range(3))
    mx_ref, my_ref = refs.pop(0), refs.pop(0)
    lap_ref = refs.pop(0)
    if not last:
        new_ref = refs.pop(0)
    if first:
        dg_ref = refs.pop(0)
    y_ref, a_ref = refs

    def functions(layer, row, size):
        value = u[1][layer, row : row + size]
        buoy = b[1][layer, row : row + size]
        return [value, value * buoy] + ([buoy] if first else [])

    plane_part(functions, y_ref, a_ref, mx_ref, my_ref, 3)

    def body(i, at, columns):
        value = tall_of(u, at, columns)
        buoy = tall_of(b, at, columns)
        both = [x * y for x, y in zip(value, buoy)]
        for layer in range(4):
            here, b_here = value[layer + 4], buoy[layer + 4]
            if first:
                dg = depth_part(buoy, layer) + a_ref[2, layer, at, columns] + CENTRE * b_here
                dg_ref[layer, at, columns] = dg
            else:
                dg = dg_ref[layer, at, columns]
            plain = depth_part(value, layer) + a_ref[0, layer, at, columns]
            times = depth_part(both, layer) + a_ref[1, layer, at, columns]
            lap = HALF * (b_here * plain + times - here * dg)
            lap_ref[layer, at, columns] = lap
            if not last:
                new_ref[layer, at, columns] = (
                    taper_ref[layer, at, columns]
                    * (
                        2.0 * here
                        - older_ref[layer, at, columns]
                        + stiff_ref[layer, at, columns] * lap
                    )
                    + weight * src_ref[layer, at, columns]
                )

    tiles(*lap_ref.shape[1:], body)


def wave_kernel(mode, has_old, *refs):
    refs = list(refs)
    p = [refs.pop(0) for _ in range(3)]
    old_ref = refs.pop(0) if has_old else None
    b = [refs.pop(0) for _ in range(3)]
    dg_ref, stiff_ref = refs.pop(0), refs.pop(0)
    if mode == "image":
        sum_ref, me_ref, weight_ref, near_ref = (refs.pop(0) for _ in range(4))
    else:
        taper_ref, add_ref, lap_ref = (refs.pop(0) for _ in range(3))
    if mode == "turn":
        count_ref, line_ref, column_ref = (refs.pop(0) for _ in range(3))
    if mode == "spread":
        marks = [refs.pop(0) for _ in range(4)]
    if mode == "fold":
        first_ref = refs.pop(0)
        laps = [refs.pop(0) for _ in range(4)]
    mx_ref, my_ref = refs.pop(0), refs.pop(0)
    if mode == "spread":
        low_ref, high_ref = refs[-2:]
        refs = refs[:-2]
        low_ref[...] = add_at(p[0][...], *marks[:2]).reshape(low_ref.shape)
        high_ref[...] = add_at(p[2][...], *marks[2:]).reshape(high_ref.shape)
        p = [low_ref, p[1], high_ref]
    y_ref, a_ref = refs[-2:]
    outs = refs[:-2]

    def functions(layer, row, size):
        value = p[1][layer, row : row + size]
        return value, value * b[1][layer, row : row + size]

    plane_part(functions, y_ref, a_ref, mx_ref, my_ref, 2)

    def body(block, i, at, columns):
        value = tall_of(p, at, columns)
        buoy = tall_of(b, at, columns)
        both = [x * y for x, y in zip(value, buoy)]
        for layer in range(4):
            here = value[layer + 4]
            spot = (layer, at, columns)
            plain = depth_part(value, layer) + a_ref[0, layer, at, columns]
            times = depth_part(both, layer) + a_ref[1, layer, at, columns]
            lb = buoy[layer + 4] * plain + times - here * dg_ref[spot]
            total = 2.0 * here + (HALF * stiff_ref[spot]) * lb
            if mode == "image":
                inner = pl.ds(pl.multiple_of(i * 8, 8), 8)
                outs[block][layer, inner, columns] = (
                    sum_ref[spot] + near_ref[spot] * here + weight_ref[spot] * total
                )
                continue
            if has_old:
                old = old_ref[spot]
                total = total - old
            taper = taper_ref[spot]
            added = add_ref[spot] * lap_ref[spot]
            if mode in ("born", "turn"):
                new = taper * (total + added)
            else:
                new = taper * total + added
            if mode == "turn":
                a_ref[0, layer, at, columns] = new
                new = count_ref[spot] * new
            outs[0][spot] = new
            if mode == "fold":
                weight = laps[0][spot] * taper
                known = laps[3][spot] * old + laps[2][spot] * here
                known = known + laps[0][spot] * (lap_ref[spot] * first_ref[spot])
                outs[1][spot] = known - weight * here
                if len(outs) > 2:
                    outs[2][spot] = weight
                    outs[3][spot] = laps[1][spot]

    _, rows, columns = p[1].shape
    if mode == "image":
        per = rows // len(outs)
        for block in range(len(outs)):
            owner = lax.rem(me_ref[0] + block, len(outs))
            tiles(per, columns, functools.partial(body, block), owner * per)
    else:
        tiles(rows, columns, functools.partial(body, 0))
    if mode == "turn":
        outs[1][...] = read_at(a_ref[0].reshape(-1, columns), line_ref, column_ref)


def piece_of(pieces, parts, c):
    each = pieces[0].shape[0]
    block, rest = divmod(c, parts * each)
    group, inner = divmod(rest, each)
    return pieces[group * (len(pieces) // parts) + block], inner


def gram_kernel(parts, sel_ref, selt_ref, *refs):
    *pieces, out_ref, lanes_ref = refs
    count = sel_ref.shape[0]
    _, rows, columns = pieces[0].shape

    def piece(c, at, column):
        ref, inner = piece_of(pieces, parts, c)
        return ref[inner, at, column : column + LANE]

    for i0 in range(0, count, 4):
        for j0 in range(i0 // 8 * 8, count, 8):

            def step(r, accs, i0=i0, j0=j0):
                at = pl.ds(pl.multiple_of(r * 8, 8), 8)
                accs = list(accs)
                for column in range(0, columns, LANE):
                    left = [piece(i0 + i, at, column) for i in range(4)]
                    for j in range(8):
                        right = piece(j0 + j, at, column)
                        for i in range(4):
                            accs[i * 8 + j] = accs[i * 8 + j] + left[i] * right
                return tuple(accs)

            zero = jnp.zeros((8, LANE), jnp.float32)
            accs = lax.fori_loop(0, rows // 8, step, (zero,) * 32)
            for i in range(4):
                for j in range(8):
                    lanes_ref[i0 + i, j0 + j : j0 + j + 1, :] = jnp.sum(
                        accs[i * 8 + j], axis=0, keepdims=True
                    )
    local = jnp.sum(lanes_ref[...], axis=-1)
    row = lax.broadcasted_iota(jnp.int32, local.shape, 0)
    column = lax.broadcasted_iota(jnp.int32, local.shape, 1)
    local = jnp.where(row // 8 > column // 8, local.T, local)
    out_ref[...] = exact(exact(sel_ref[...], local), selt_ref[...])


def exact(left, right):
    return jnp.dot(left, right, precision=lax.Precision.HIGHEST, preferred_element_type=jnp.float32)


def basis_kernel(parts, scale, gram_ref, sel_ref, *refs):
    *pieces, out_ref, triangle_ref, spread_ref = refs
    count = gram_ref.shape[0]
    _, _, rows, columns = pieces[0].shape

    @pl.when(pl.program_id(0) == 0)
    def _():
        row = lax.broadcasted_iota(jnp.int32, (count, count), 0)
        column = lax.broadcasted_iota(jnp.int32, (count, count), 1)
        left = gram_ref[...]
        unit = jnp.where(row == column, 1.0, 0.0)
        for i in range(count):
            pivot = jnp.sqrt(left[i : i + 1, i : i + 1])
            upper = left[i : i + 1, :] / pivot
            solved = unit[i : i + 1, :] / pivot
            below = left[:, i : i + 1] / pivot
            is_row = row == i
            left = jnp.where(is_row, upper, jnp.where(row > i, left - below * upper, left))
            unit = jnp.where(is_row, solved, jnp.where(row > i, unit - below * solved, unit))
        triangle_ref[...] = jnp.where(column >= row, left, 0.0) / scale
        weights = exact(unit, sel_ref[...]) * scale
        for i in range(count):
            for c in range(count):
                spread_ref[i * count + c] = jnp.broadcast_to(
                    weights[i : i + 1, c : c + 1], (8, LANE)
                )

    def piece(c, at, columns):
        ref, inner = piece_of(pieces, parts, c)
        return ref[inner, 0, at, columns]

    halves = [slice(column, column + LANE) for column in range(0, columns, LANE)]
    for r in range(0, rows, 8):
        at = slice(r, r + 8)
        values = [[piece(c, at, half) for half in halves] for c in range(count)]
        for i in range(count):
            totals = [None] * len(halves)
            for c in range(count):
                weight = spread_ref[i * count + c]
                for h in range(len(halves)):
                    term = weight * values[c][h]
                    totals[h] = term if totals[h] is None else totals[h] + term
            for h, half in enumerate(halves):
                out_ref[i, 0, at, half] = totals[h]


def halo(block):
    count = lax.axis_size("slab")
    forward = [(i, i + 1) for i in range(count - 1)]
    backward = [(target, source) for source, target in forward]
    return lax.ppermute(block, "slab", forward), lax.ppermute(block, "slab", backward)


def whole(shape):
    zeros = (0,) * len(shape)
    return pl.BlockSpec(tuple(shape), lambda *_: zeros)


def add_up(value):
    for axis in ("slab", "dirs"):
        size, stride = lax.axis_size(axis), 1
        while stride < size:
            value = value + lax.ppermute(value, axis, [(i, i ^ stride) for i in range(size)])
            stride *= 2
    return value


def shards(
    perturbations,
    background_now,
    background_prev,
    stiffness,
    buoyancy,
    absorb_mask,
    source_cells,
    source_amp,
    receiver_cells,
    column_order,
):
    shape = buoyancy.shape
    layers, rows, columns = shape
    sketch_count = perturbations.shape[0]
    each = sketch_count // GROUPS
    owners = lax.axis_size("dirs")
    me = lax.axis_index("dirs").astype(jnp.int32).reshape(1)
    f32 = jnp.float32
    field = jax.ShapeDtypeStruct(shape, f32)
    cells_here = layers * rows * columns
    b_low, b_high = halo(buoyancy)
    u_low, u_high = halo(background_now)

    def matrix(*size):
        return jax.ShapeDtypeStruct(size, jnp.bfloat16)

    copied = (stiffness, buoyancy, background_now, background_prev)
    matrices = (matrix(columns, columns), matrix(rows, 2 * rows), matrix(rows, 3 * rows))
    (
        counts, source_field, taper, mx, my2, my3, stiffness, b_mid, current, older
    ) = pl.pallas_call(
        functools.partial(place_kernel, len(copied)),
        out_shape=(field,) * 3 + matrices + (field,) * len(copied),
        compiler_params=params(),
        cost_estimate=pl.CostEstimate(
            flops=40 * cells_here, bytes_accessed=16 * cells_here, transcendentals=0
        ),
        name="place",
    )(
        receiver_cells.reshape(1, -1),
        source_cells.reshape(1, -1),
        source_amp.reshape(1, -1),
        absorb_mask,
        *copied,
    )

    buoy = (b_low, b_mid, b_high)
    fields = [current]
    laps = []
    dg = None
    for t in range(STEPS):
        first, last = t == 0, t == STEPS - 1
        if not first:
            u_low, u_high = halo(current)
        operands = [u_low, current, u_high, *buoy, stiffness]
        if not first:
            operands.append(dg)
        if not last:
            operands += [taper, source_field, older]
        operands += [mx, my3]
        slots = 3 if first else 2
        results = pl.pallas_call(
            functools.partial(background_kernel, source_weight(t), first, last),
            out_shape=(field,) * (1 + (not last) + first),
            scratch_shapes=[
                pltpu.VMEM((slots, layers, 3 * rows, columns), jnp.bfloat16),
                pltpu.VMEM((slots, layers, rows, columns), f32),
            ],
            compiler_params=params(),
            cost_estimate=pl.CostEstimate(
                flops=60 * cells_here, bytes_accessed=56 * cells_here, transcendentals=0
            ),
            name=f"background{t}",
        )(*operands)
        results = list(results)
        laps.append(results.pop(0))
        if not last:
            older, current = current, results.pop(0)
            fields.append(current)
        if first:
            dg = results.pop(0)

    def marks(cells):
        return pl.pallas_call(
            marks_kernel,
            out_shape=(
                matrix(layers * rows, cells.shape[-1]),
                jax.ShapeDtypeStruct((columns, cells.shape[-1]), f32),
            ),
            compiler_params=params(),
            name="marks",
        )(cells)

    cells = receiver_cells.reshape(1, -1)
    at_mine = marks(cells)
    at_low, at_high = (marks(other) for other in halo(cells))
    receivers = cells.shape[-1]

    def after(value, earlier):
        return lax.optimization_barrier((value, earlier))[0]

    def wave(mode, group, p, old, add, lap, extra=(), records=None, wait=None):
        low, high = halo(p if records is None else records)
        if wait is not None:
            low = after(low, wait)
        one = pl.BlockSpec((None, *shape), lambda d: (d, 0, 0, 0))
        shifted = pl.BlockSpec((None, *shape), lambda d: (d + group * each, 0, 0, 0))
        same = whole(shape)
        heard = pl.BlockSpec((None, 1, receivers), lambda d: (d, 0, 0))
        side = one if records is None else heard
        operands, specs = [low, p, high], [side, one, side]
        if old is not None:
            operands.append(old)
            specs.append(one)
        operands += [*buoy, dg, stiffness]
        specs += [same] * 5
        if mode != "image":
            operands += [taper, add, lap]
            specs += [same, shifted if mode in ("born", "turn") else one, same]
        if mode == "turn":
            operands += [counts, *at_mine]
            specs += [same] + [whole(mark.shape) for mark in at_mine]
        if mode == "spread":
            operands += [*at_low, *at_high]
            specs += [whole(mark.shape) for mark in at_low + at_high]
        if mode == "fold":
            specs += [one] + [same] * 4
        if mode == "image":
            specs += [one, pl.BlockSpec(memory_space=pltpu.SMEM)] + [same] * 2
        operands += [*extra, mx, my2]
        specs += [whole(mx.shape), whole(my2.shape)]
        out_shape, out_spec = (jax.ShapeDtypeStruct((each, *shape), f32),), [one]
        if mode == "fold":
            out_shape, out_spec = out_shape * 2, out_spec * 2
            if group == 0:
                out_shape, out_spec = out_shape + (field,) * 2, out_spec + [same] * 2
        elif mode == "turn":
            out_shape += (jax.ShapeDtypeStruct((each, 1, receivers), f32),)
            out_spec = out_spec + [heard]
        elif mode == "image":
            split = (layers, rows // owners, columns)
            out_shape = (jax.ShapeDtypeStruct((each, *split), f32),) * owners
            out_spec = [pl.BlockSpec((None, *split), lambda d: (d, 0, 0, 0))] * owners
        results = pl.pallas_call(
            functools.partial(wave_kernel, mode, old is not None),
            grid=(each,),
            in_specs=specs,
            out_specs=out_spec,
            out_shape=out_shape,
            scratch_shapes=[
                pltpu.VMEM((2, layers, 2 * rows, columns), jnp.bfloat16),
                pltpu.VMEM((2, layers, rows, columns), f32),
            ]
            + [pltpu.VMEM(shape, f32)] * (2 if mode == "spread" else 0),
            compiler_params=params(),
            cost_estimate=pl.CostEstimate(
                flops=60 * each * cells_here,
                bytes_accessed=28 * each * cells_here,
                transcendentals=0,
            ),
            name=mode,
        )(*operands)
        return results[0] if len(results) == 1 else results

    born = [[None] * GROUPS for _ in range(STEPS + 1)]
    for g in range(GROUPS):
        mine = perturbations[g * each : (g + 1) * each]
        born[1][g] = taper * (mine * laps[0])
    born[1][1] = after(born[1][1], fields[2])
    ahead = {(2, 1): fields[3], (3, 1): (laps[3], at_mine, at_low, at_high)}
    for t in (1, 2):
        for g in range(GROUPS):
            old = born[t - 1][g] if t > 1 else None
            new = wave("born", g, born[t][g], old, perturbations, laps[t])
            if (t + 1, g) in ahead:
                new = after(new, ahead[t + 1, g])
            born[t + 1][g] = new
    adjoint = [[None] * GROUPS for _ in range(STEPS + 1)]
    for g in range(GROUPS):
        wait = adjoint[2][g - 1] if g else None
        adjoint[3][g], records = wave(
            "turn", g, born[3][g], born[2][g], perturbations, laps[3], wait=wait
        )
        adjoint[2][g] = wave(
            "spread", g, adjoint[3][g], None, born[3][g], counts, records=records
        )
    known = [None] * GROUPS
    for g in range(GROUPS):
        adjoint[1][g], known[g], *rest = wave(
            "fold", g, adjoint[2][g], adjoint[3][g], born[2][g], counts, (born[1][g], *laps)
        )
        if g == 0:
            weight, near = rest
    sketch = []
    for g in range(GROUPS):
        blocks = wave(
            "image", g, adjoint[1][g], None, None, None, (known[g], me, weight, near)
        )
        sketch.append(blocks[0])
        for s in range(1, owners):
            ring = [(i, (i + s) % owners) for i in range(owners)]
            sketch.append(lax.ppermute(blocks[s], "dirs", ring))

    total_dirs = owners * sketch_count
    local_rows = rows // owners
    square = (total_dirs, total_dirs)
    place = jnp.arange(total_dirs, dtype=jnp.int32)
    owner = (me[0] - place // sketch_count + owners) % owners
    local = owner * sketch_count + place % sketch_count
    selector = (column_order[:, None] == local[None, :]).astype(f32)
    gram = pl.pallas_call(
        functools.partial(gram_kernel, GROUPS),
        out_shape=jax.ShapeDtypeStruct(square, f32),
        scratch_shapes=[pltpu.VMEM((*square, LANE), f32)],
        compiler_params=params(),
        name="gram",
    )(selector, selector.T, *[s.reshape(each, layers * local_rows, columns) for s in sketch])
    gram = add_up(gram)
    grid_cells = layers * lax.axis_size("slab") * rows * columns
    part = (each, 1, local_rows, columns)
    basis, triangle = pl.pallas_call(
        functools.partial(basis_kernel, GROUPS, math.sqrt(grid_cells)),
        grid=(layers,),
        in_specs=[whole(square)] * 2
        + [pl.BlockSpec(part, lambda l: (0, l, 0, 0))] * len(sketch),
        out_specs=[
            pl.BlockSpec((total_dirs, 1, local_rows, columns), lambda l: (0, l, 0, 0)),
            whole(square),
        ],
        out_shape=(
            jax.ShapeDtypeStruct((total_dirs, layers, local_rows, columns), f32),
            jax.ShapeDtypeStruct(square, f32),
        ),
        scratch_shapes=[pltpu.VMEM((total_dirs * total_dirs, 8, LANE), f32)],
        compiler_params=params(),
        name="basis",
    )(gram, selector, *sketch)
    return basis, triangle


def solution(mesh):
    return jax.shard_map(
        shards,
        mesh=mesh,
        in_specs=(
            P("dirs", "slab", None, None),
            P("slab", None, None),
            P("slab", None, None),
            P("slab", None, None),
            P("slab", None, None),
            P("slab", None, None),
            P("slab"),
            P("slab"),
            P("slab"),
            P(),
        ),
        out_specs=(P(None, "slab", "dirs", None), P()),
        check_vma=False,
    )
```

```python
import functools
import math

import jax
import jax.numpy as jnp
from jax import lax
from jax.experimental import pallas as pl
from jax.experimental.pallas import tpu as pltpu
from jax.sharding import PartitionSpec as P

STEPS = 4
DAMPING = 0.3
TAPS = (8064.0, -1008.0, 128.0, -9.0)
CENTRE = 6.0 * sum(TAPS)
HALF = 0.5 / 5040.0
GROUPS = 2
VMEM = 22 * 1024 * 1024
LANE = 128


def band(shape, period):
    row = lax.broadcasted_iota(jnp.int32, shape, 0)
    column = lax.broadcasted_iota(jnp.int32, shape, 1) % period
    distance = jnp.abs(row - column)
    matrix = jnp.zeros(shape, jnp.float32)
    for k, tap in enumerate(TAPS, 1):
        matrix = jnp.where(distance == k, tap, matrix)
    return matrix.astype(jnp.bfloat16)


def source_weight(t):
    return (1.0 - 0.4 * t) * math.exp(-0.125 * t * t)


def params():
    return pltpu.CompilerParams(vmem_limit_bytes=VMEM)


def split_rows(y_ref, slot, layer, row, values, parts, rows):
    size = values.shape[0]
    for s in range(parts):
        part = values.astype(jnp.bfloat16)
        y_ref[slot, layer, s * rows + row : s * rows + row + size, :] = part
        if s < parts - 1:
            values = values - part.astype(jnp.float32)


def plane_part(functions, y_ref, a_ref, mx_ref, my_ref, parts):
    _, layers, rows, _ = a_ref.shape
    for layer in range(layers):
        for row in range(0, rows, 32):
            for slot, values in enumerate(functions(layer, row, 32)):
                split_rows(y_ref, slot, layer, row, values, parts, rows)
    for slot in range(a_ref.shape[0]):
        for layer in range(layers):
            y = y_ref[slot, layer]
            along = jnp.dot(y, mx_ref[...], preferred_element_type=jnp.float32)
            total = jnp.dot(my_ref[...], y, preferred_element_type=jnp.float32)
            for s in range(parts):
                total = total + along[s * rows : (s + 1) * rows]
            a_ref[slot, layer] = total


def depth_part(tall, layer):
    total = None
    for k, tap in enumerate(TAPS, 1):
        term = tap * (tall[layer + 4 + k] + tall[layer + 4 - k])
        total = term if total is None else total + term
    return total


def tall_of(refs, rows, columns):
    low, mid, high = refs
    return [ref[layer, rows, columns] for ref in (low, mid, high) for layer in range(4)]


def tiles(rows, columns, body, start=0):
    def step(i, carry):
        at = pl.ds(pl.multiple_of(start + i * 8, 8), 8)
        for column in range(0, columns, LANE):
            body(i, at, slice(column, column + LANE))
        return carry

    lax.fori_loop(0, rows // 8, step, 0)


def place_kernel(copies, rc_ref, sc_ref, amp_ref, mask_ref, *refs):
    sources, refs = refs[:copies], refs[copies:]
    m_ref, src_ref, taper_ref, mx_ref, my2_ref, my3_ref = refs[:6]
    for source, target in zip(sources, refs[6:]):
        target[...] = source[...]
    layers, rows, columns = m_ref.shape
    for matrix in (mx_ref, my2_ref, my3_ref):
        matrix[...] = band(matrix.shape, matrix.shape[0])
    count = rc_ref.shape[1]
    lines = layers * rows
    chunk = min(256, count)
    total = None
    for start in range(0, count, chunk):
        cells = rc_ref[:, start : start + chunk]
        line = lax.broadcasted_iota(jnp.int32, (lines, chunk), 0) == cells // columns
        column = lax.broadcasted_iota(jnp.int32, (columns, chunk), 0) == cells % columns
        part = lax.dot_general(
            jnp.where(line, 1.0, 0.0).astype(jnp.bfloat16),
            jnp.where(column, 1.0, 0.0).astype(jnp.bfloat16),
            (((1,), (1,)), ((), ())),
            preferred_element_type=jnp.float32,
        )
        total = part if total is None else total + part
    m_ref[...] = total.reshape(m_ref.shape)
    cells = sc_ref[...]
    count = cells.shape[1]
    line = lax.broadcasted_iota(jnp.int32, (lines, count), 0) == cells // columns
    column = lax.broadcasted_iota(jnp.int32, (columns, count), 0) == cells % columns
    part = lax.dot_general(
        jnp.where(line, 1.0, 0.0),
        jnp.where(column, amp_ref[...], 0.0),
        (((1,), (1,)), ((), ())),
        precision=lax.Precision.HIGHEST,
        preferred_element_type=jnp.float32,
    )
    src_ref[...] = part.reshape(src_ref.shape)
    taper_ref[...] = 1.0 - DAMPING * mask_ref[...].astype(jnp.float32)


def background_kernel(weight, first, last, *refs):
    refs = list(refs)
    u = [refs.pop(0) for _ in range(3)]
    b = [refs.pop(0) for _ in range(3)]
    stiff_ref = refs.pop(0)
    dg_ref = None if first else refs.pop(0)
    taper_ref = src_ref = older_ref = new_ref = None
    if not last:
        taper_ref, src_ref, older_ref = (refs.pop(0) for _ in range(3))
    mx_ref, my_ref = refs.pop(0), refs.pop(0)
    lap_ref = refs.pop(0)
    if not last:
        new_ref = refs.pop(0)
    if first:
        dg_ref, start_ref = refs.pop(0), refs.pop(0)
    y_ref, a_ref = refs

    def functions(layer, row, size):
        value = u[1][layer, row : row + size]
        buoy = b[1][layer, row : row + size]
        return [value, value * buoy] + ([buoy] if first else [])

    plane_part(functions, y_ref, a_ref, mx_ref, my_ref, 3)

    def body(i, at, columns):
        value = tall_of(u, at, columns)
        buoy = tall_of(b, at, columns)
        both = [x * y for x, y in zip(value, buoy)]
        for layer in range(4):
            here, b_here = value[layer + 4], buoy[layer + 4]
            if first:
                dg = depth_part(buoy, layer) + a_ref[2, layer, at, columns] + CENTRE * b_here
                dg_ref[layer, at, columns] = dg
            else:
                dg = dg_ref[layer, at, columns]
            plain = depth_part(value, layer) + a_ref[0, layer, at, columns]
            times = depth_part(both, layer) + a_ref[1, layer, at, columns]
            lap = HALF * (b_here * plain + times - here * dg)
            lap_ref[layer, at, columns] = lap
            if first:
                start_ref[layer, at, columns] = taper_ref[layer, at, columns] * lap
            if not last:
                new_ref[layer, at, columns] = (
                    taper_ref[layer, at, columns]
                    * (
                        2.0 * here
                        - older_ref[layer, at, columns]
                        + stiff_ref[layer, at, columns] * lap
                    )
                    + weight * src_ref[layer, at, columns]
                )

    tiles(*lap_ref.shape[1:], body)


def wave_kernel(mode, has_old, *refs):
    refs = list(refs)
    p = [refs.pop(0) for _ in range(3)]
    old_ref = refs.pop(0) if has_old else None
    b = [refs.pop(0) for _ in range(3)]
    dg_ref, stiff_ref = refs.pop(0), refs.pop(0)
    if mode == "image":
        sum_ref, me_ref, weight_ref, near_ref = (refs.pop(0) for _ in range(4))
    else:
        taper_ref, add_ref, lap_ref = (refs.pop(0) for _ in range(3))
    count_ref = refs.pop(0) if mode == "turn" else None
    if mode == "fold":
        first_ref = refs.pop(0)
        laps = [refs.pop(0) for _ in range(4)]
    mx_ref, my_ref = refs.pop(0), refs.pop(0)
    if mode == "start":
        *refs, low_ref, high_ref = refs
        starts = [refs.pop(0) for _ in range(3)]
        for target, source, factor_ref in zip((low_ref, refs[1], high_ref), p, starts):
            target[...] = source[...] * factor_ref[...]
        p = [low_ref, refs[1], high_ref]
    y_ref, a_ref = refs[-2:]
    outs = refs[:-2]

    def functions(layer, row, size):
        value = p[1][layer, row : row + size]
        return value, value * b[1][layer, row : row + size]

    plane_part(functions, y_ref, a_ref, mx_ref, my_ref, 2)

    def body(block, i, at, columns):
        value = tall_of(p, at, columns)
        buoy = tall_of(b, at, columns)
        both = [x * y for x, y in zip(value, buoy)]
        for layer in range(4):
            here = value[layer + 4]
            spot = (layer, at, columns)
            plain = depth_part(value, layer) + a_ref[0, layer, at, columns]
            times = depth_part(both, layer) + a_ref[1, layer, at, columns]
            lb = buoy[layer + 4] * plain + times - here * dg_ref[spot]
            total = 2.0 * here + (HALF * stiff_ref[spot]) * lb
            if mode == "image":
                inner = pl.ds(pl.multiple_of(i * 8, 8), 8)
                outs[block][layer, inner, columns] = (
                    sum_ref[spot] + near_ref[spot] * here + weight_ref[spot] * total
                )
                continue
            if has_old:
                old = old_ref[spot]
                total = total - old
            taper = taper_ref[spot]
            added = add_ref[spot] * lap_ref[spot]
            if mode in ("start", "born", "turn"):
                new = taper * (total + added)
            else:
                new = taper * total + added
            if mode == "turn":
                new = count_ref[spot] * new
            outs[0][spot] = new
            if mode == "fold":
                weight = laps[0][spot] * taper
                known = laps[3][spot] * old + laps[2][spot] * here
                known = known + laps[0][spot] * (lap_ref[spot] * first_ref[spot])
                outs[1][spot] = known - weight * here
                if len(outs) > 2:
                    outs[2][spot] = weight
                    outs[3][spot] = laps[1][spot]

    _, rows, columns = p[1].shape
    if mode == "image":
        per = rows // len(outs)
        for block in range(len(outs)):
            owner = lax.rem(me_ref[0] + block, len(outs))
            tiles(per, columns, functools.partial(body, block), owner * per)
    else:
        tiles(rows, columns, functools.partial(body, 0))


def piece_of(pieces, parts, c):
    each = pieces[0].shape[0]
    block, rest = divmod(c, parts * each)
    group, inner = divmod(rest, each)
    return pieces[group * (len(pieces) // parts) + block], inner


def gram_kernel(parts, sel_ref, selt_ref, *refs):
    *pieces, out_ref, lanes_ref = refs
    count = sel_ref.shape[0]
    _, rows, columns = pieces[0].shape

    def piece(c, at, column):
        ref, inner = piece_of(pieces, parts, c)
        return ref[inner, at, column : column + LANE]

    for i0 in range(0, count, 4):
        for j0 in range(i0 // 8 * 8, count, 8):

            def step(r, accs, i0=i0, j0=j0):
                at = pl.ds(pl.multiple_of(r * 8, 8), 8)
                accs = list(accs)
                for column in range(0, columns, LANE):
                    left = [piece(i0 + i, at, column) for i in range(4)]
                    for j in range(8):
                        right = piece(j0 + j, at, column)
                        for i in range(4):
                            accs[i * 8 + j] = accs[i * 8 + j] + left[i] * right
                return tuple(accs)

            zero = jnp.zeros((8, LANE), jnp.float32)
            accs = lax.fori_loop(0, rows // 8, step, (zero,) * 32)
            for i in range(4):
                for j in range(8):
                    lanes_ref[i0 + i, j0 + j : j0 + j + 1, :] = jnp.sum(
                        accs[i * 8 + j], axis=0, keepdims=True
                    )
    local = jnp.sum(lanes_ref[...], axis=-1)
    row = lax.broadcasted_iota(jnp.int32, local.shape, 0)
    column = lax.broadcasted_iota(jnp.int32, local.shape, 1)
    local = jnp.where(row // 8 > column // 8, local.T, local)
    out_ref[...] = exact(exact(sel_ref[...], local), selt_ref[...])


def exact(left, right):
    return jnp.dot(left, right, precision=lax.Precision.HIGHEST, preferred_element_type=jnp.float32)


def basis_kernel(parts, scale, gram_ref, sel_ref, *refs):
    *pieces, out_ref, triangle_ref, spread_ref = refs
    count = gram_ref.shape[0]
    _, _, rows, columns = pieces[0].shape

    @pl.when(pl.program_id(0) == 0)
    def _():
        row = lax.broadcasted_iota(jnp.int32, (count, count), 0)
        column = lax.broadcasted_iota(jnp.int32, (count, count), 1)
        left = gram_ref[...]
        unit = jnp.where(row == column, 1.0, 0.0)
        for i in range(count):
            pivot = jnp.sqrt(left[i : i + 1, i : i + 1])
            upper = left[i : i + 1, :] / pivot
            solved = unit[i : i + 1, :] / pivot
            below = left[:, i : i + 1] / pivot
            is_row = row == i
            left = jnp.where(is_row, upper, jnp.where(row > i, left - below * upper, left))
            unit = jnp.where(is_row, solved, jnp.where(row > i, unit - below * solved, unit))
        triangle_ref[...] = jnp.where(column >= row, left, 0.0) / scale
        weights = exact(unit, sel_ref[...]) * scale
        for i in range(count):
            for c in range(count):
                spread_ref[i * count + c] = jnp.broadcast_to(
                    weights[i : i + 1, c : c + 1], (8, LANE)
                )

    def piece(c, at, columns):
        ref, inner = piece_of(pieces, parts, c)
        return ref[inner, 0, at, columns]

    halves = [slice(column, column + LANE) for column in range(0, columns, LANE)]
    for r in range(0, rows, 8):
        at = slice(r, r + 8)
        values = [[piece(c, at, half) for half in halves] for c in range(count)]
        for i in range(count):
            totals = [None] * len(halves)
            for c in range(count):
                weight = spread_ref[i * count + c]
                for h in range(len(halves)):
                    term = weight * values[c][h]
                    totals[h] = term if totals[h] is None else totals[h] + term
            for h, half in enumerate(halves):
                out_ref[i, 0, at, half] = totals[h]


def halo(block):
    count = lax.axis_size("slab")
    forward = [(i, i + 1) for i in range(count - 1)]
    backward = [(target, source) for source, target in forward]
    return lax.ppermute(block, "slab", forward), lax.ppermute(block, "slab", backward)


def whole(shape):
    zeros = (0,) * len(shape)
    return pl.BlockSpec(tuple(shape), lambda *_: zeros)


def add_up(value):
    for axis in ("slab", "dirs"):
        size, stride = lax.axis_size(axis), 1
        while stride < size:
            value = value + lax.ppermute(value, axis, [(i, i ^ stride) for i in range(size)])
            stride *= 2
    return value


def shards(
    perturbations,
    background_now,
    background_prev,
    stiffness,
    buoyancy,
    absorb_mask,
    source_cells,
    source_amp,
    receiver_cells,
    column_order,
):
    shape = buoyancy.shape
    layers, rows, columns = shape
    sketch_count = perturbations.shape[0]
    each = sketch_count // GROUPS
    owners = lax.axis_size("dirs")
    me = lax.axis_index("dirs").astype(jnp.int32).reshape(1)
    f32 = jnp.float32
    field = jax.ShapeDtypeStruct(shape, f32)
    cells_here = layers * rows * columns
    b_low, b_high = halo(buoyancy)
    u_low, u_high = u0_low, u0_high = halo(background_now)

    def matrix(*size):
        return jax.ShapeDtypeStruct(size, jnp.bfloat16)

    copied = (stiffness, buoyancy, background_now, background_prev)
    matrices = (matrix(columns, columns), matrix(rows, 2 * rows), matrix(rows, 3 * rows))
    (
        counts, source_field, taper, mx, my2, my3, stiffness, b_mid, current, older
    ) = pl.pallas_call(
        functools.partial(place_kernel, len(copied)),
        out_shape=(field,) * 3 + matrices + (field,) * len(copied),
        compiler_params=params(),
        cost_estimate=pl.CostEstimate(
            flops=40 * cells_here, bytes_accessed=16 * cells_here, transcendentals=0
        ),
        name="place",
    )(
        receiver_cells.reshape(1, -1),
        source_cells.reshape(1, -1),
        source_amp.reshape(1, -1),
        absorb_mask,
        *copied,
    )

    buoy = (b_low, b_mid, b_high)
    fields = [current]
    laps = []
    dg = None
    for t in range(STEPS):
        first, last = t == 0, t == STEPS - 1
        if not first:
            u_low, u_high = halo(current)
        operands = [u_low, current, u_high, *buoy, stiffness]
        if not first:
            operands.append(dg)
        if not last:
            operands += [taper, source_field, older]
        operands += [mx, my3]
        slots = 3 if first else 2
        results = pl.pallas_call(
            functools.partial(background_kernel, source_weight(t), first, last),
            out_shape=(field,) * (1 + (not last) + 2 * first),
            scratch_shapes=[
                pltpu.VMEM((slots, layers, 3 * rows, columns), jnp.bfloat16),
                pltpu.VMEM((slots, layers, rows, columns), f32),
            ],
            compiler_params=params(),
            cost_estimate=pl.CostEstimate(
                flops=60 * cells_here, bytes_accessed=56 * cells_here, transcendentals=0
            ),
            name=f"background{t}",
        )(*operands)
        results = list(results)
        laps.append(results.pop(0))
        if not last:
            older, current = current, results.pop(0)
            fields.append(current)
        if first:
            dg, start = results
            start_low, start_high = halo(start)

    def wave(mode, group, p, old, add, lap, extra=(), ends=None):
        low, high = halo(p) if mode != "start" else ends
        one = pl.BlockSpec((None, *shape), lambda d: (d, 0, 0, 0))
        shifted = pl.BlockSpec((None, *shape), lambda d: (d + group * each, 0, 0, 0))
        same = whole(shape)
        operands, specs = [low, p, high], [one, shifted if mode == "start" else one, one]
        if old is not None:
            operands.append(old)
            specs.append(one)
        operands += [*buoy, dg, stiffness]
        specs += [same] * 5
        if mode != "image":
            operands += [taper, add, lap]
            specs += [same, shifted if mode in ("start", "born", "turn") else one, same]
        if mode == "turn":
            operands.append(counts)
            specs.append(same)
        if mode == "fold":
            specs += [one] + [same] * 4
        if mode == "image":
            specs += [one, pl.BlockSpec(memory_space=pltpu.SMEM)] + [same] * 2
        operands += [*extra, mx, my2]
        specs += [whole(mx.shape), whole(my2.shape)]
        if mode == "start":
            operands += [start_low, start, start_high]
            specs += [same] * 3
        out_shape, out_spec = (jax.ShapeDtypeStruct((each, *shape), f32),), [one]
        if mode == "start":
            out_shape, out_spec = out_shape * 2, out_spec * 2
        if mode == "fold":
            out_shape, out_spec = out_shape * 2, out_spec * 2
            if group == 0:
                out_shape, out_spec = out_shape + (field,) * 2, out_spec + [same] * 2
        if mode == "image":
            split = (layers, rows // owners, columns)
            out_shape = (jax.ShapeDtypeStruct((each, *split), f32),) * owners
            out_spec = [pl.BlockSpec((None, *split), lambda d: (d, 0, 0, 0))] * owners
        results = pl.pallas_call(
            functools.partial(wave_kernel, mode, old is not None),
            grid=(each,),
            in_specs=specs,
            out_specs=out_spec,
            out_shape=out_shape,
            scratch_shapes=[
                pltpu.VMEM((2, layers, 2 * rows, columns), jnp.bfloat16),
                pltpu.VMEM((2, layers, rows, columns), f32),
            ]
            + [pltpu.VMEM(shape, f32)] * (2 if mode == "start" else 0),
            compiler_params=params(),
            cost_estimate=pl.CostEstimate(
                flops=60 * each * cells_here,
                bytes_accessed=28 * each * cells_here,
                transcendentals=0,
            ),
            name=mode,
        )(*operands)
        return results[0] if len(results) == 1 else results

    def after(value, earlier):
        return lax.optimization_barrier((value, earlier))[0]

    born = [[None] * GROUPS for _ in range(STEPS + 1)]
    first_after = [(b_low, b_high, u0_low, u0_high), fields[2]]
    ahead = {(2, 1): fields[3], (3, 1): laps[3]}
    for t in (1, 2):
        for g in range(GROUPS):
            if t == 1:
                mine = after(perturbations[g * each : (g + 1) * each], first_after[g])
                new, born[1][g] = wave(
                    "start", g, perturbations, None, perturbations, laps[1], ends=halo(mine)
                )
            else:
                new = wave("born", g, born[t][g], born[t - 1][g], perturbations, laps[t])
            if (t + 1, g) in ahead:
                new = after(new, ahead[t + 1, g])
            born[t + 1][g] = new
    adjoint = [[None] * GROUPS for _ in range(STEPS + 1)]
    for g in range(GROUPS):
        adjoint[3][g] = wave("turn", g, born[3][g], born[2][g], perturbations, laps[3])
    for g in range(GROUPS):
        adjoint[2][g] = wave("adjoint", g, adjoint[3][g], None, born[3][g], counts)
    known = [None] * GROUPS
    for g in range(GROUPS):
        adjoint[1][g], known[g], *rest = wave(
            "fold", g, adjoint[2][g], adjoint[3][g], born[2][g], counts, (born[1][g], *laps)
        )
        if g == 0:
            weight, near = rest
    sketch = []
    for g in range(GROUPS):
        blocks = wave(
            "image", g, adjoint[1][g], None, None, None, (known[g], me, weight, near)
        )
        sketch.append(blocks[0])
        for s in range(1, owners):
            ring = [(i, (i + s) % owners) for i in range(owners)]
            sketch.append(lax.ppermute(blocks[s], "dirs", ring))

    total_dirs = owners * sketch_count
    local_rows = rows // owners
    square = (total_dirs, total_dirs)
    place = jnp.arange(total_dirs, dtype=jnp.int32)
    owner = (me[0] - place // sketch_count + owners) % owners
    local = owner * sketch_count + place % sketch_count
    selector = (column_order[:, None] == local[None, :]).astype(f32)
    gram = pl.pallas_call(
        functools.partial(gram_kernel, GROUPS),
        out_shape=jax.ShapeDtypeStruct(square, f32),
        scratch_shapes=[pltpu.VMEM((*square, LANE), f32)],
        compiler_params=params(),
        name="gram",
    )(selector, selector.T, *[s.reshape(each, layers * local_rows, columns) for s in sketch])
    gram = add_up(gram)
    grid_cells = layers * lax.axis_size("slab") * rows * columns
    part = (each, 1, local_rows, columns)
    basis, triangle = pl.pallas_call(
        functools.partial(basis_kernel, GROUPS, math.sqrt(grid_cells)),
        grid=(layers,),
        in_specs=[whole(square)] * 2
        + [pl.BlockSpec(part, lambda l: (0, l, 0, 0))] * len(sketch),
        out_specs=[
            pl.BlockSpec((total_dirs, 1, local_rows, columns), lambda l: (0, l, 0, 0)),
            whole(square),
        ],
        out_shape=(
            jax.ShapeDtypeStruct((total_dirs, layers, local_rows, columns), f32),
            jax.ShapeDtypeStruct(square, f32),
        ),
        scratch_shapes=[pltpu.VMEM((total_dirs * total_dirs, 8, LANE), f32)],
        compiler_params=params(),
        name="basis",
    )(gram, selector, *sketch)
    return basis, triangle


def solution(mesh):
    return jax.shard_map(
        shards,
        mesh=mesh,
        in_specs=(
            P("dirs", "slab", None, None),
            P("slab", None, None),
            P("slab", None, None),
            P("slab", None, None),
            P("slab", None, None),
            P("slab", None, None),
            P("slab"),
            P("slab"),
            P("slab"),
            P(),
        ),
        out_specs=(P(None, "slab", "dirs", None), P()),
        check_vma=False,
    )
```

```python
import functools
import math

import jax
import jax.numpy as jnp
from jax import lax
from jax.experimental import pallas as pl
from jax.experimental.pallas import tpu as pltpu
from jax.sharding import PartitionSpec as P

STEPS = 4
DAMPING = 0.3
TAPS = (8064.0, -1008.0, 128.0, -9.0)
CENTRE = 6.0 * sum(TAPS)
HALF = 0.5 / 5040.0
GROUPS = 2
VMEM = 22 * 1024 * 1024
LANE = 128


def band(shape, period):
    row = lax.broadcasted_iota(jnp.int32, shape, 0)
    column = lax.broadcasted_iota(jnp.int32, shape, 1) % period
    distance = jnp.abs(row - column)
    matrix = jnp.zeros(shape, jnp.float32)
    for k, tap in enumerate(TAPS, 1):
        matrix = jnp.where(distance == k, tap, matrix)
    return matrix.astype(jnp.bfloat16)


def source_weight(t):
    return (1.0 - 0.4 * t) * math.exp(-0.125 * t * t)


def params():
    return pltpu.CompilerParams(vmem_limit_bytes=VMEM)


def split_rows(y_ref, slot, layer, row, values, parts, rows):
    size = values.shape[0]
    for s in range(parts):
        part = values.astype(jnp.bfloat16)
        y_ref[slot, layer, s * rows + row : s * rows + row + size, :] = part
        if s < parts - 1:
            values = values - part.astype(jnp.float32)


def plane_part(functions, y_ref, a_ref, mx_ref, my_ref, parts):
    _, layers, rows, _ = a_ref.shape
    for layer in range(layers):
        for row in range(0, rows, 32):
            for slot, values in enumerate(functions(layer, row, 32)):
                split_rows(y_ref, slot, layer, row, values, parts, rows)
    for slot in range(a_ref.shape[0]):
        for layer in range(layers):
            y = y_ref[slot, layer]
            along = jnp.dot(y, mx_ref[...], preferred_element_type=jnp.float32)
            total = jnp.dot(my_ref[...], y, preferred_element_type=jnp.float32)
            for s in range(parts):
                total = total + along[s * rows : (s + 1) * rows]
            a_ref[slot, layer] = total


def depth_part(tall, layer):
    total = None
    for k, tap in enumerate(TAPS, 1):
        term = tap * (tall[layer + 4 + k] + tall[layer + 4 - k])
        total = term if total is None else total + term
    return total


def tall_of(refs, rows, columns):
    low, mid, high = refs
    return [ref[layer, rows, columns] for ref in (low, mid, high) for layer in range(4)]


def tiles(rows, columns, body, start=0):
    def step(i, carry):
        at = pl.ds(pl.multiple_of(start + i * 8, 8), 8)
        for column in range(0, columns, LANE):
            body(i, at, slice(column, column + LANE))
        return carry

    lax.fori_loop(0, rows // 8, step, 0)


def place_kernel(copies, rc_ref, sc_ref, amp_ref, mask_ref, *refs):
    sources, refs = refs[:copies], refs[copies:]
    m_ref, src_ref, taper_ref, mx_ref, my2_ref, my3_ref = refs[:6]
    for source, target in zip(sources, refs[6:]):
        target[...] = source[...]
    layers, rows, columns = m_ref.shape
    for matrix in (mx_ref, my2_ref, my3_ref):
        matrix[...] = band(matrix.shape, matrix.shape[0])
    count = rc_ref.shape[1]
    lines = layers * rows
    chunk = min(256, count)
    total = None
    for start in range(0, count, chunk):
        cells = rc_ref[:, start : start + chunk]
        line = lax.broadcasted_iota(jnp.int32, (lines, chunk), 0) == cells // columns
        column = lax.broadcasted_iota(jnp.int32, (columns, chunk), 0) == cells % columns
        part = lax.dot_general(
            jnp.where(line, 1.0, 0.0).astype(jnp.bfloat16),
            jnp.where(column, 1.0, 0.0).astype(jnp.bfloat16),
            (((1,), (1,)), ((), ())),
            preferred_element_type=jnp.float32,
        )
        total = part if total is None else total + part
    m_ref[...] = total.reshape(m_ref.shape)
    cells = sc_ref[...]
    count = cells.shape[1]
    line = lax.broadcasted_iota(jnp.int32, (lines, count), 0) == cells // columns
    column = lax.broadcasted_iota(jnp.int32, (columns, count), 0) == cells % columns
    part = lax.dot_general(
        jnp.where(line, 1.0, 0.0),
        jnp.where(column, amp_ref[...], 0.0),
        (((1,), (1,)), ((), ())),
        precision=lax.Precision.HIGHEST,
        preferred_element_type=jnp.float32,
    )
    src_ref[...] = part.reshape(src_ref.shape)
    taper_ref[...] = 1.0 - DAMPING * mask_ref[...].astype(jnp.float32)


def background_kernel(weight, first, last, *refs):
    refs = list(refs)
    u = [refs.pop(0) for _ in range(3)]
    b = [refs.pop(0) for _ in range(3)]
    stiff_ref = refs.pop(0)
    dg_ref = None if first else refs.pop(0)
    taper_ref = src_ref = older_ref = new_ref = None
    if not last:
        taper_ref, src_ref, older_ref = (refs.pop(0) for _ in range(3))
    mx_ref, my_ref = refs.pop(0), refs.pop(0)
    lap_ref = refs.pop(0)
    if first:
        pair_ref, dg_ref = refs.pop(0), refs.pop(0)
        new_ref, start_ref = pair_ref.at[0], pair_ref.at[1]
    elif not last:
        new_ref = refs.pop(0)
    y_ref, a_ref = refs

    def functions(layer, row, size):
        value = u[1][layer, row : row + size]
        buoy = b[1][layer, row : row + size]
        return [value, value * buoy] + ([buoy] if first else [])

    plane_part(functions, y_ref, a_ref, mx_ref, my_ref, 3)

    def body(i, at, columns):
        value = tall_of(u, at, columns)
        buoy = tall_of(b, at, columns)
        both = [x * y for x, y in zip(value, buoy)]
        for layer in range(4):
            here, b_here = value[layer + 4], buoy[layer + 4]
            if first:
                dg = depth_part(buoy, layer) + a_ref[2, layer, at, columns] + CENTRE * b_here
                dg_ref[layer, at, columns] = dg
            else:
                dg = dg_ref[layer, at, columns]
            plain = depth_part(value, layer) + a_ref[0, layer, at, columns]
            times = depth_part(both, layer) + a_ref[1, layer, at, columns]
            lap = HALF * (b_here * plain + times - here * dg)
            lap_ref[layer, at, columns] = lap
            if first:
                start_ref[layer, at, columns] = taper_ref[layer, at, columns] * lap
            if not last:
                new_ref[layer, at, columns] = (
                    taper_ref[layer, at, columns]
                    * (
                        2.0 * here
                        - older_ref[layer, at, columns]
                        + stiff_ref[layer, at, columns] * lap
                    )
                    + weight * src_ref[layer, at, columns]
                )

    tiles(*lap_ref.shape[1:], body)


def wave_kernel(mode, has_old, *refs):
    refs = list(refs)
    p = [refs.pop(0) for _ in range(3)]
    old_ref = refs.pop(0) if has_old else None
    b = [refs.pop(0) for _ in range(3)]
    dg_ref, stiff_ref = refs.pop(0), refs.pop(0)
    if mode == "image":
        sum_ref, me_ref, weight_ref, near_ref = (refs.pop(0) for _ in range(4))
    else:
        taper_ref, add_ref, lap_ref = (refs.pop(0) for _ in range(3))
    count_ref = refs.pop(0) if mode == "turn" else None
    if mode == "fold":
        first_ref = refs.pop(0)
        laps = [refs.pop(0) for _ in range(4)]
    mx_ref, my_ref = refs.pop(0), refs.pop(0)
    if mode == "start":
        *refs, low_ref, high_ref = refs
        starts = [refs.pop(0) for _ in range(3)]
        for target, source, factor_ref in zip((low_ref, refs[1], high_ref), p, starts):
            target[...] = source[...] * factor_ref[...]
        p = [low_ref, refs[1], high_ref]
    y_ref, a_ref = refs[-2:]
    outs = refs[:-2]

    def functions(layer, row, size):
        value = p[1][layer, row : row + size]
        return value, value * b[1][layer, row : row + size]

    plane_part(functions, y_ref, a_ref, mx_ref, my_ref, 2)

    def body(block, i, at, columns):
        value = tall_of(p, at, columns)
        buoy = tall_of(b, at, columns)
        both = [x * y for x, y in zip(value, buoy)]
        for layer in range(4):
            here = value[layer + 4]
            spot = (layer, at, columns)
            plain = depth_part(value, layer) + a_ref[0, layer, at, columns]
            times = depth_part(both, layer) + a_ref[1, layer, at, columns]
            lb = buoy[layer + 4] * plain + times - here * dg_ref[spot]
            total = 2.0 * here + (HALF * stiff_ref[spot]) * lb
            if mode == "image":
                inner = pl.ds(pl.multiple_of(i * 8, 8), 8)
                outs[block][layer, inner, columns] = (
                    sum_ref[spot] + near_ref[spot] * here + weight_ref[spot] * total
                )
                continue
            if has_old:
                old = old_ref[spot]
                total = total - old
            taper = taper_ref[spot]
            added = add_ref[spot] * lap_ref[spot]
            if mode in ("start", "born", "turn"):
                new = taper * (total + added)
            else:
                new = taper * total + added
            if mode == "turn":
                new = count_ref[spot] * new
            outs[0][spot] = new
            if mode == "fold":
                weight = laps[0][spot] * taper
                known = laps[3][spot] * old + laps[2][spot] * here
                known = known + laps[0][spot] * (lap_ref[spot] * first_ref[spot])
                outs[1][spot] = known - weight * here
                if len(outs) > 2:
                    outs[2][spot] = weight
                    outs[3][spot] = laps[1][spot]

    _, rows, columns = p[1].shape
    if mode == "image":
        per = rows // len(outs)
        for block in range(len(outs)):
            owner = lax.rem(me_ref[0] + block, len(outs))
            tiles(per, columns, functools.partial(body, block), owner * per)
    else:
        tiles(rows, columns, functools.partial(body, 0))


def piece_of(pieces, parts, c):
    each = pieces[0].shape[0]
    block, rest = divmod(c, parts * each)
    group, inner = divmod(rest, each)
    return pieces[group * (len(pieces) // parts) + block], inner


def gram_kernel(parts, sel_ref, selt_ref, *refs):
    *pieces, out_ref, lanes_ref = refs
    count = sel_ref.shape[0]
    _, rows, columns = pieces[0].shape

    def piece(c, at, column):
        ref, inner = piece_of(pieces, parts, c)
        return ref[inner, at, column : column + LANE]

    for i0 in range(0, count, 4):
        for j0 in range(i0 // 8 * 8, count, 8):

            def step(r, accs, i0=i0, j0=j0):
                at = pl.ds(pl.multiple_of(r * 8, 8), 8)
                accs = list(accs)
                for column in range(0, columns, LANE):
                    left = [piece(i0 + i, at, column) for i in range(4)]
                    for j in range(8):
                        right = piece(j0 + j, at, column)
                        for i in range(4):
                            accs[i * 8 + j] = accs[i * 8 + j] + left[i] * right
                return tuple(accs)

            zero = jnp.zeros((8, LANE), jnp.float32)
            accs = lax.fori_loop(0, rows // 8, step, (zero,) * 32)
            for i in range(4):
                for j in range(8):
                    lanes_ref[i0 + i, j0 + j : j0 + j + 1, :] = jnp.sum(
                        accs[i * 8 + j], axis=0, keepdims=True
                    )
    local = jnp.sum(lanes_ref[...], axis=-1)
    row = lax.broadcasted_iota(jnp.int32, local.shape, 0)
    column = lax.broadcasted_iota(jnp.int32, local.shape, 1)
    local = jnp.where(row // 8 > column // 8, local.T, local)
    out_ref[...] = exact(exact(sel_ref[...], local), selt_ref[...])


def exact(left, right):
    return jnp.dot(left, right, precision=lax.Precision.HIGHEST, preferred_element_type=jnp.float32)


def basis_kernel(parts, scale, gram_ref, sel_ref, *refs):
    *pieces, out_ref, triangle_ref, spread_ref = refs
    count = gram_ref.shape[0]
    _, _, rows, columns = pieces[0].shape

    @pl.when(pl.program_id(0) == 0)
    def _():
        row = lax.broadcasted_iota(jnp.int32, (count, count), 0)
        column = lax.broadcasted_iota(jnp.int32, (count, count), 1)
        left = gram_ref[...]
        unit = jnp.where(row == column, 1.0, 0.0)
        for i in range(count):
            pivot = jnp.sqrt(left[i : i + 1, i : i + 1])
            upper = left[i : i + 1, :] / pivot
            solved = unit[i : i + 1, :] / pivot
            below = left[:, i : i + 1] / pivot
            is_row = row == i
            left = jnp.where(is_row, upper, jnp.where(row > i, left - below * upper, left))
            unit = jnp.where(is_row, solved, jnp.where(row > i, unit - below * solved, unit))
        triangle_ref[...] = jnp.where(column >= row, left, 0.0) / scale
        weights = exact(unit, sel_ref[...]) * scale
        for i in range(count):
            for c in range(count):
                spread_ref[i * count + c] = jnp.broadcast_to(
                    weights[i : i + 1, c : c + 1], (8, LANE)
                )

    def piece(c, at, columns):
        ref, inner = piece_of(pieces, parts, c)
        return ref[inner, 0, at, columns]

    halves = [slice(column, column + LANE) for column in range(0, columns, LANE)]
    for r in range(0, rows, 8):
        at = slice(r, r + 8)
        values = [[piece(c, at, half) for half in halves] for c in range(count)]
        for i in range(count):
            totals = [None] * len(halves)
            for c in range(count):
                weight = spread_ref[i * count + c]
                for h in range(len(halves)):
                    term = weight * values[c][h]
                    totals[h] = term if totals[h] is None else totals[h] + term
            for h, half in enumerate(halves):
                out_ref[i, 0, at, half] = totals[h]


def halo(block):
    count = lax.axis_size("slab")
    forward = [(i, i + 1) for i in range(count - 1)]
    backward = [(target, source) for source, target in forward]
    return lax.ppermute(block, "slab", forward), lax.ppermute(block, "slab", backward)


def whole(shape):
    zeros = (0,) * len(shape)
    return pl.BlockSpec(tuple(shape), lambda *_: zeros)


def add_up(value):
    for axis in ("slab", "dirs"):
        size, stride = lax.axis_size(axis), 1
        while stride < size:
            value = value + lax.ppermute(value, axis, [(i, i ^ stride) for i in range(size)])
            stride *= 2
    return value


def shards(
    perturbations,
    background_now,
    background_prev,
    stiffness,
    buoyancy,
    absorb_mask,
    source_cells,
    source_amp,
    receiver_cells,
    column_order,
):
    shape = buoyancy.shape
    layers, rows, columns = shape
    sketch_count = perturbations.shape[0]
    each = sketch_count // GROUPS
    owners = lax.axis_size("dirs")
    me = lax.axis_index("dirs").astype(jnp.int32).reshape(1)
    f32 = jnp.float32
    field = jax.ShapeDtypeStruct(shape, f32)
    cells_here = layers * rows * columns
    def after(value, earlier):
        return lax.optimization_barrier((value, earlier))[0]

    def view(array, index):
        return array, pl.BlockSpec((None, *shape), lambda *_: (index, 0, 0, 0))

    low, high = halo(jnp.stack([buoyancy, background_now]))
    b_low, u_low = view(low, 0), view(low, 1)
    b_high, u_high = view(high, 0), view(high, 1)

    def matrix(*size):
        return jax.ShapeDtypeStruct(size, jnp.bfloat16)

    copied = (stiffness, buoyancy, background_now, background_prev)
    matrices = (matrix(columns, columns), matrix(rows, 2 * rows), matrix(rows, 3 * rows))
    (
        counts, source_field, taper, mx, my2, my3, stiffness, b_mid, current, older
    ) = pl.pallas_call(
        functools.partial(place_kernel, len(copied)),
        out_shape=(field,) * 3 + matrices + (field,) * len(copied),
        compiler_params=params(),
        cost_estimate=pl.CostEstimate(
            flops=40 * cells_here, bytes_accessed=16 * cells_here, transcendentals=0
        ),
        name="place",
    )(
        receiver_cells.reshape(1, -1),
        source_cells.reshape(1, -1),
        source_amp.reshape(1, -1),
        absorb_mask,
        *copied,
    )

    def flat(array):
        return array, whole(array.shape)

    ends = halo(after(perturbations, counts))
    buoy = (b_low, flat(b_mid), b_high)
    current, older = flat(current), flat(older)
    fields = [None]
    laps = []
    dg = None
    for t in range(STEPS):
        first, last = t == 0, t == STEPS - 1
        if t > 1:
            u_low, u_high = (flat(end) for end in halo(current[0]))
        operands = [u_low, current, u_high, *buoy, flat(stiffness)]
        if not first:
            operands.append(flat(dg))
        if not last:
            operands += [flat(taper), flat(source_field), older]
        operands += [flat(mx), flat(my3)]
        slots = 3 if first else 2
        out_shape = (field,) if last else (field, field)
        if first:
            out_shape = (field, jax.ShapeDtypeStruct((2, *shape), f32), field)
        results = pl.pallas_call(
            functools.partial(background_kernel, source_weight(t), first, last),
            grid=(1,),
            in_specs=[spec for _, spec in operands],
            out_specs=[whole(out.shape) for out in out_shape],
            out_shape=out_shape,
            scratch_shapes=[
                pltpu.VMEM((slots, layers, 3 * rows, columns), jnp.bfloat16),
                pltpu.VMEM((slots, layers, rows, columns), f32),
            ],
            compiler_params=params(),
            cost_estimate=pl.CostEstimate(
                flops=60 * cells_here, bytes_accessed=56 * cells_here, transcendentals=0
            ),
            name=f"background{t}",
        )(*[array for array, _ in operands])
        laps.append(results[0])
        if not last:
            older = current
            fields.append(results[1])
        if first:
            pair, dg = results[1], results[2]
            low, high = halo(pair)
            current, start = view(pair, 0), view(pair, 1)
            u_low, start_low = view(low, 0), view(low, 1)
            u_high, start_high = view(high, 0), view(high, 1)
        elif not last:
            current = flat(results[1])

    def wave(mode, group, p, old, add, lap, extra=()):
        low, high = ends if mode == "start" else halo(p)
        one = pl.BlockSpec((None, *shape), lambda d: (d, 0, 0, 0))
        shifted = pl.BlockSpec((None, *shape), lambda d: (d + group * each, 0, 0, 0))
        same = whole(shape)
        operands, specs = [low, p, high], [shifted if mode == "start" else one] * 3
        if old is not None:
            operands.append(old)
            specs.append(one)
        operands += [array for array, _ in buoy] + [dg, stiffness]
        specs += [spec for _, spec in buoy] + [same] * 2
        if mode != "image":
            operands += [taper, add, lap]
            specs += [same, shifted if mode in ("start", "born", "turn") else one, same]
        if mode == "turn":
            operands.append(counts)
            specs.append(same)
        if mode == "fold":
            specs += [one] + [same] * 4
        if mode == "image":
            specs += [one, pl.BlockSpec(memory_space=pltpu.SMEM)] + [same] * 2
        operands += [*extra, mx, my2]
        specs += [whole(mx.shape), whole(my2.shape)]
        if mode == "start":
            operands += [array for array, _ in (start_low, start, start_high)]
            specs += [spec for _, spec in (start_low, start, start_high)]
        out_shape, out_spec = (jax.ShapeDtypeStruct((each, *shape), f32),), [one]
        if mode == "start":
            out_shape, out_spec = out_shape * 2, out_spec * 2
        if mode == "fold":
            out_shape, out_spec = out_shape * 2, out_spec * 2
            if group == 0:
                out_shape, out_spec = out_shape + (field,) * 2, out_spec + [same] * 2
        if mode == "image":
            split = (layers, rows // owners, columns)
            out_shape = (jax.ShapeDtypeStruct((each, *split), f32),) * owners
            out_spec = [pl.BlockSpec((None, *split), lambda d: (d, 0, 0, 0))] * owners
        results = pl.pallas_call(
            functools.partial(wave_kernel, mode, old is not None),
            grid=(each,),
            in_specs=specs,
            out_specs=out_spec,
            out_shape=out_shape,
            scratch_shapes=[
                pltpu.VMEM((2, layers, 2 * rows, columns), jnp.bfloat16),
                pltpu.VMEM((2, layers, rows, columns), f32),
            ]
            + [pltpu.VMEM(shape, f32)] * (2 if mode == "start" else 0),
            compiler_params=params(),
            cost_estimate=pl.CostEstimate(
                flops=60 * each * cells_here,
                bytes_accessed=28 * each * cells_here,
                transcendentals=0,
            ),
            name=mode,
        )(*operands)
        return results[0] if len(results) == 1 else results

    born = [[None] * GROUPS for _ in range(STEPS + 1)]
    ahead = {(2, 1): fields[3], (3, 1): laps[3]}
    for t in (1, 2):
        for g in range(GROUPS):
            if t == 1:
                new, born[1][g] = wave(
                    "start", g, perturbations, None, perturbations, laps[1]
                )
            else:
                new = wave("born", g, born[t][g], born[t - 1][g], perturbations, laps[t])
            if (t + 1, g) in ahead:
                new = after(new, ahead[t + 1, g])
            born[t + 1][g] = new
    adjoint = [[None] * GROUPS for _ in range(STEPS + 1)]
    for g in range(GROUPS):
        adjoint[3][g] = wave("turn", g, born[3][g], born[2][g], perturbations, laps[3])
    for g in range(GROUPS):
        adjoint[2][g] = wave("adjoint", g, adjoint[3][g], None, born[3][g], counts)
    known = [None] * GROUPS
    for g in range(GROUPS):
        adjoint[1][g], known[g], *rest = wave(
            "fold", g, adjoint[2][g], adjoint[3][g], born[2][g], counts, (born[1][g], *laps)
        )
        if g == 0:
            weight, near = rest
    sketch = []
    for g in range(GROUPS):
        blocks = wave(
            "image", g, adjoint[1][g], None, None, None, (known[g], me, weight, near)
        )
        sketch.append(blocks[0])
        for s in range(1, owners):
            ring = [(i, (i + s) % owners) for i in range(owners)]
            sketch.append(lax.ppermute(blocks[s], "dirs", ring))

    total_dirs = owners * sketch_count
    local_rows = rows // owners
    square = (total_dirs, total_dirs)
    place = jnp.arange(total_dirs, dtype=jnp.int32)
    owner = (me[0] - place // sketch_count + owners) % owners
    local = owner * sketch_count + place % sketch_count
    selector = (column_order[:, None] == local[None, :]).astype(f32)
    gram = pl.pallas_call(
        functools.partial(gram_kernel, GROUPS),
        out_shape=jax.ShapeDtypeStruct(square, f32),
        scratch_shapes=[pltpu.VMEM((*square, LANE), f32)],
        compiler_params=params(),
        name="gram",
    )(selector, selector.T, *[s.reshape(each, layers * local_rows, columns) for s in sketch])
    gram = add_up(gram)
    grid_cells = layers * lax.axis_size("slab") * rows * columns
    part = (each, 1, local_rows, columns)
    basis, triangle = pl.pallas_call(
        functools.partial(basis_kernel, GROUPS, math.sqrt(grid_cells)),
        grid=(layers,),
        in_specs=[whole(square)] * 2
        + [pl.BlockSpec(part, lambda l: (0, l, 0, 0))] * len(sketch),
        out_specs=[
            pl.BlockSpec((total_dirs, 1, local_rows, columns), lambda l: (0, l, 0, 0)),
            whole(square),
        ],
        out_shape=(
            jax.ShapeDtypeStruct((total_dirs, layers, local_rows, columns), f32),
            jax.ShapeDtypeStruct(square, f32),
        ),
        scratch_shapes=[pltpu.VMEM((total_dirs * total_dirs, 8, LANE), f32)],
        compiler_params=params(),
        name="basis",
    )(gram, selector, *sketch)
    return basis, triangle


def solution(mesh):
    return jax.shard_map(
        shards,
        mesh=mesh,
        in_specs=(
            P("dirs", "slab", None, None),
            P("slab", None, None),
            P("slab", None, None),
            P("slab", None, None),
            P("slab", None, None),
            P("slab", None, None),
            P("slab"),
            P("slab"),
            P("slab"),
            P(),
        ),
        out_specs=(P(None, "slab", "dirs", None), P()),
        check_vma=False,
    )
```

```python
import functools
import math

import jax
import jax.numpy as jnp
from jax import lax
from jax.experimental import pallas as pl
from jax.experimental.pallas import tpu as pltpu
from jax.sharding import PartitionSpec as P

STEPS = 4
DAMPING = 0.3
TAPS = (8064.0, -1008.0, 128.0, -9.0)
CENTRE = 6.0 * sum(TAPS)
HALF = 0.5 / 5040.0
GROUPS = 2
VMEM = 22 * 1024 * 1024
LANE = 128


def band(shape, period):
    row = lax.broadcasted_iota(jnp.int32, shape, 0)
    column = lax.broadcasted_iota(jnp.int32, shape, 1) % period
    distance = jnp.abs(row - column)
    matrix = jnp.zeros(shape, jnp.float32)
    for k, tap in enumerate(TAPS, 1):
        matrix = jnp.where(distance == k, tap, matrix)
    return matrix.astype(jnp.bfloat16)


def source_weight(t):
    return (1.0 - 0.4 * t) * math.exp(-0.125 * t * t)


def params():
    return pltpu.CompilerParams(vmem_limit_bytes=VMEM)


def split_rows(y_ref, slot, layer, row, values, parts, rows):
    size = values.shape[0]
    for s in range(parts):
        part = values.astype(jnp.bfloat16)
        y_ref[slot, layer, s * rows + row : s * rows + row + size, :] = part
        if s < parts - 1:
            values = values - part.astype(jnp.float32)


def plane_part(functions, y_ref, a_ref, mx_ref, my_ref, parts):
    _, layers, rows, _ = a_ref.shape
    for layer in range(layers):
        for row in range(0, rows, 32):
            for slot, values in enumerate(functions(layer, row, 32)):
                split_rows(y_ref, slot, layer, row, values, parts, rows)
    for slot in range(a_ref.shape[0]):
        for layer in range(layers):
            y = y_ref[slot, layer]
            along = jnp.dot(y, mx_ref[...], preferred_element_type=jnp.float32)
            total = jnp.dot(my_ref[...], y, preferred_element_type=jnp.float32)
            for s in range(parts):
                total = total + along[s * rows : (s + 1) * rows]
            a_ref[slot, layer] = total


def depth_part(tall, layer):
    total = None
    for k, tap in enumerate(TAPS, 1):
        term = tap * (tall[layer + 4 + k] + tall[layer + 4 - k])
        total = term if total is None else total + term
    return total


def tall_of(refs, rows, columns):
    low, mid, high = refs
    return [ref[layer, rows, columns] for ref in (low, mid, high) for layer in range(4)]


def tiles(rows, columns, body, start=0):
    def step(i, carry):
        at = pl.ds(pl.multiple_of(start + i * 8, 8), 8)
        for column in range(0, columns, LANE):
            body(i, at, slice(column, column + LANE))
        return carry

    lax.fori_loop(0, rows // 8, step, 0)


def place_kernel(copies, rc_ref, sc_ref, amp_ref, mask_ref, *refs):
    sources, refs = refs[:copies], refs[copies:]
    m_ref, src_ref, taper_ref, mx_ref, my2_ref, my3_ref = refs[:6]
    for source, target in zip(sources, refs[6:]):
        target[...] = source[...]
    layers, rows, columns = m_ref.shape
    for matrix in (mx_ref, my2_ref, my3_ref):
        matrix[...] = band(matrix.shape, matrix.shape[0])
    count = rc_ref.shape[1]
    lines = layers * rows
    chunk = min(256, count)
    total = None
    for start in range(0, count, chunk):
        cells = rc_ref[:, start : start + chunk]
        line = lax.broadcasted_iota(jnp.int32, (lines, chunk), 0) == cells // columns
        column = lax.broadcasted_iota(jnp.int32, (columns, chunk), 0) == cells % columns
        part = lax.dot_general(
            jnp.where(line, 1.0, 0.0).astype(jnp.bfloat16),
            jnp.where(column, 1.0, 0.0).astype(jnp.bfloat16),
            (((1,), (1,)), ((), ())),
            preferred_element_type=jnp.float32,
        )
        total = part if total is None else total + part
    m_ref[...] = total.reshape(m_ref.shape)
    cells = sc_ref[...]
    count = cells.shape[1]
    line = lax.broadcasted_iota(jnp.int32, (lines, count), 0) == cells // columns
    column = lax.broadcasted_iota(jnp.int32, (columns, count), 0) == cells % columns
    part = lax.dot_general(
        jnp.where(line, 1.0, 0.0),
        jnp.where(column, amp_ref[...], 0.0),
        (((1,), (1,)), ((), ())),
        precision=lax.Precision.HIGHEST,
        preferred_element_type=jnp.float32,
    )
    src_ref[...] = part.reshape(src_ref.shape)
    taper_ref[...] = 1.0 - DAMPING * mask_ref[...].astype(jnp.float32)


def background_kernel(weight, first, last, *refs):
    refs = list(refs)
    u = [refs.pop(0) for _ in range(3)]
    b = [refs.pop(0) for _ in range(3)]
    stiff_ref = refs.pop(0)
    dg_ref = None if first else refs.pop(0)
    taper_ref = src_ref = older_ref = new_ref = None
    if not last:
        taper_ref, src_ref, older_ref = (refs.pop(0) for _ in range(3))
    mx_ref, my_ref = refs.pop(0), refs.pop(0)
    lap_ref = refs.pop(0)
    if not last:
        new_ref = refs.pop(0)
    if first:
        dg_ref = refs.pop(0)
    y_ref, a_ref = refs

    def functions(layer, row, size):
        value = u[1][layer, row : row + size]
        buoy = b[1][layer, row : row + size]
        return [value, value * buoy] + ([buoy] if first else [])

    plane_part(functions, y_ref, a_ref, mx_ref, my_ref, 3)

    def body(i, at, columns):
        value = tall_of(u, at, columns)
        buoy = tall_of(b, at, columns)
        both = [x * y for x, y in zip(value, buoy)]
        for layer in range(4):
            here, b_here = value[layer + 4], buoy[layer + 4]
            if first:
                dg = depth_part(buoy, layer) + a_ref[2, layer, at, columns] + CENTRE * b_here
                dg_ref[layer, at, columns] = dg
            else:
                dg = dg_ref[layer, at, columns]
            plain = depth_part(value, layer) + a_ref[0, layer, at, columns]
            times = depth_part(both, layer) + a_ref[1, layer, at, columns]
            lap = HALF * (b_here * plain + times - here * dg)
            lap_ref[layer, at, columns] = lap
            if not last:
                new_ref[layer, at, columns] = (
                    taper_ref[layer, at, columns]
                    * (
                        2.0 * here
                        - older_ref[layer, at, columns]
                        + stiff_ref[layer, at, columns] * lap
                    )
                    + weight * src_ref[layer, at, columns]
                )

    tiles(*lap_ref.shape[1:], body)


def wave_kernel(mode, has_old, *refs):
    refs = list(refs)
    p = [refs.pop(0) for _ in range(3)]
    old_ref = refs.pop(0) if has_old else None
    b = [refs.pop(0) for _ in range(3)]
    dg_ref, stiff_ref = refs.pop(0), refs.pop(0)
    if mode == "image":
        sum_ref, me_ref, weight_ref, near_ref = (refs.pop(0) for _ in range(4))
    else:
        taper_ref, add_ref, lap_ref = (refs.pop(0) for _ in range(3))
    count_ref = refs.pop(0) if mode == "turn" else None
    if mode == "fold":
        first_ref = refs.pop(0)
        laps = [refs.pop(0) for _ in range(4)]
    mx_ref, my_ref = refs.pop(0), refs.pop(0)
    y_ref, a_ref = refs[-2:]
    outs = refs[:-2]

    def functions(layer, row, size):
        value = p[1][layer, row : row + size]
        return value, value * b[1][layer, row : row + size]

    plane_part(functions, y_ref, a_ref, mx_ref, my_ref, 2)

    def body(block, i, at, columns):
        value = tall_of(p, at, columns)
        buoy = tall_of(b, at, columns)
        both = [x * y for x, y in zip(value, buoy)]
        for layer in range(4):
            here = value[layer + 4]
            spot = (layer, at, columns)
            plain = depth_part(value, layer) + a_ref[0, layer, at, columns]
            times = depth_part(both, layer) + a_ref[1, layer, at, columns]
            lb = buoy[layer + 4] * plain + times - here * dg_ref[spot]
            total = 2.0 * here + (HALF * stiff_ref[spot]) * lb
            if mode == "image":
                inner = pl.ds(pl.multiple_of(i * 8, 8), 8)
                outs[block][layer, inner, columns] = (
                    sum_ref[spot] + near_ref[spot] * here + weight_ref[spot] * total
                )
                continue
            if has_old:
                old = old_ref[spot]
                total = total - old
            taper = taper_ref[spot]
            added = add_ref[spot] * lap_ref[spot]
            if mode in ("born", "turn"):
                new = taper * (total + added)
            else:
                new = taper * total + added
            if mode == "turn":
                new = count_ref[spot] * new
            outs[0][spot] = new
            if mode == "fold":
                weight = laps[0][spot] * taper
                known = laps[3][spot] * old + laps[2][spot] * here
                known = known + laps[0][spot] * (lap_ref[spot] * first_ref[spot])
                outs[1][spot] = known - weight * here
                if len(outs) > 2:
                    outs[2][spot] = weight
                    outs[3][spot] = laps[1][spot]

    _, rows, columns = p[1].shape
    if mode == "image":
        per = rows // len(outs)
        for block in range(len(outs)):
            owner = lax.rem(me_ref[0] + block, len(outs))
            tiles(per, columns, functools.partial(body, block), owner * per)
    else:
        tiles(rows, columns, functools.partial(body, 0))


def piece_of(pieces, parts, c):
    each = pieces[0].shape[0]
    block, rest = divmod(c, parts * each)
    group, inner = divmod(rest, each)
    return pieces[group * (len(pieces) // parts) + block], inner


def gram_kernel(parts, sel_ref, selt_ref, *refs):
    *pieces, out_ref, lanes_ref = refs
    count = sel_ref.shape[0]
    _, rows, columns = pieces[0].shape

    def piece(c, at, column):
        ref, inner = piece_of(pieces, parts, c)
        return ref[inner, at, column : column + LANE]

    for i0 in range(0, count, 4):
        for j0 in range(i0 // 8 * 8, count, 8):

            def step(r, accs, i0=i0, j0=j0):
                at = pl.ds(pl.multiple_of(r * 8, 8), 8)
                accs = list(accs)
                for column in range(0, columns, LANE):
                    left = [piece(i0 + i, at, column) for i in range(4)]
                    for j in range(8):
                        right = piece(j0 + j, at, column)
                        for i in range(4):
                            accs[i * 8 + j] = accs[i * 8 + j] + left[i] * right
                return tuple(accs)

            zero = jnp.zeros((8, LANE), jnp.float32)
            accs = lax.fori_loop(0, rows // 8, step, (zero,) * 32)
            for i in range(4):
                for j in range(8):
                    lanes_ref[i0 + i, j0 + j : j0 + j + 1, :] = jnp.sum(
                        accs[i * 8 + j], axis=0, keepdims=True
                    )
    local = jnp.sum(lanes_ref[...], axis=-1)
    row = lax.broadcasted_iota(jnp.int32, local.shape, 0)
    column = lax.broadcasted_iota(jnp.int32, local.shape, 1)
    local = jnp.where(row // 8 > column // 8, local.T, local)
    out_ref[...] = exact(exact(sel_ref[...], local), selt_ref[...])


def exact(left, right):
    return jnp.dot(left, right, precision=lax.Precision.HIGHEST, preferred_element_type=jnp.float32)


def basis_kernel(parts, scale, gram_ref, sel_ref, *refs):
    *pieces, out_ref, triangle_ref, spread_ref = refs
    count = gram_ref.shape[0]
    _, _, rows, columns = pieces[0].shape

    @pl.when(pl.program_id(0) == 0)
    def _():
        row = lax.broadcasted_iota(jnp.int32, (count, count), 0)
        column = lax.broadcasted_iota(jnp.int32, (count, count), 1)
        left = gram_ref[...]
        unit = jnp.where(row == column, 1.0, 0.0)
        for i in range(count):
            pivot = jnp.sqrt(left[i : i + 1, i : i + 1])
            upper = left[i : i + 1, :] / pivot
            solved = unit[i : i + 1, :] / pivot
            below = left[:, i : i + 1] / pivot
            is_row = row == i
            left = jnp.where(is_row, upper, jnp.where(row > i, left - below * upper, left))
            unit = jnp.where(is_row, solved, jnp.where(row > i, unit - below * solved, unit))
        triangle_ref[...] = jnp.where(column >= row, left, 0.0) / scale
        weights = exact(unit, sel_ref[...]) * scale
        for i in range(count):
            for c in range(count):
                spread_ref[i * count + c] = jnp.broadcast_to(
                    weights[i : i + 1, c : c + 1], (8, LANE)
                )

    def piece(c, at, columns):
        ref, inner = piece_of(pieces, parts, c)
        return ref[inner, 0, at, columns]

    halves = [slice(column, column + LANE) for column in range(0, columns, LANE)]
    for r in range(0, rows, 8):
        at = slice(r, r + 8)
        values = [[piece(c, at, half) for half in halves] for c in range(count)]
        for i in range(count):
            totals = [None] * len(halves)
            for c in range(count):
                weight = spread_ref[i * count + c]
                for h in range(len(halves)):
                    term = weight * values[c][h]
                    totals[h] = term if totals[h] is None else totals[h] + term
            for h, half in enumerate(halves):
                out_ref[i, 0, at, half] = totals[h]


def halo(block):
    count = lax.axis_size("slab")
    forward = [(i, i + 1) for i in range(count - 1)]
    backward = [(target, source) for source, target in forward]
    return lax.ppermute(block, "slab", forward), lax.ppermute(block, "slab", backward)


def whole(shape):
    zeros = (0,) * len(shape)
    return pl.BlockSpec(tuple(shape), lambda *_: zeros)


def add_up(value):
    for axis in ("slab", "dirs"):
        size, stride = lax.axis_size(axis), 1
        while stride < size:
            value = value + lax.ppermute(value, axis, [(i, i ^ stride) for i in range(size)])
            stride *= 2
    return value


def shards(
    perturbations,
    background_now,
    background_prev,
    stiffness,
    buoyancy,
    absorb_mask,
    source_cells,
    source_amp,
    receiver_cells,
    column_order,
):
    shape = buoyancy.shape
    layers, rows, columns = shape
    sketch_count = perturbations.shape[0]
    each = sketch_count // GROUPS
    owners = lax.axis_size("dirs")
    me = lax.axis_index("dirs").astype(jnp.int32).reshape(1)
    f32 = jnp.float32
    field = jax.ShapeDtypeStruct(shape, f32)
    cells_here = layers * rows * columns
    def after(value, earlier):
        return lax.optimization_barrier((value, earlier))[0]

    def view(array, index):
        return array, pl.BlockSpec((None, *shape), lambda *_: (index, 0, 0, 0))

    low, high = halo(jnp.stack([buoyancy, background_now]))
    b_low, u_low = view(low, 0), view(low, 1)
    b_high, u_high = view(high, 0), view(high, 1)

    def matrix(*size):
        return jax.ShapeDtypeStruct(size, jnp.bfloat16)

    copied = (stiffness, buoyancy, background_now, background_prev, perturbations)
    matrices = (matrix(columns, columns), matrix(rows, 2 * rows), matrix(rows, 3 * rows))
    (
        counts, source_field, taper, mx, my2, my3, stiffness, b_mid, current, older, perturbations
    ) = pl.pallas_call(
        functools.partial(place_kernel, len(copied)),
        out_shape=(field,) * 3 + matrices + (*[field] * 4, jax.ShapeDtypeStruct(perturbations.shape, f32)),
        compiler_params=params(),
        cost_estimate=pl.CostEstimate(
            flops=40 * cells_here, bytes_accessed=16 * cells_here, transcendentals=0
        ),
        name="place",
    )(
        receiver_cells.reshape(1, -1),
        source_cells.reshape(1, -1),
        source_amp.reshape(1, -1),
        absorb_mask,
        *copied,
    )

    def flat(array):
        return array, whole(array.shape)

    buoy = (b_low, flat(b_mid), b_high)
    current, older = flat(current), flat(older)
    fields = [None]
    laps = []
    dg = None
    for t in range(STEPS):
        first, last = t == 0, t == STEPS - 1
        if not first:
            u_low, u_high = (flat(end) for end in halo(current[0]))
        operands = [u_low, current, u_high, *buoy, flat(stiffness)]
        if not first:
            operands.append(flat(dg))
        if not last:
            operands += [flat(taper), flat(source_field), older]
        operands += [flat(mx), flat(my3)]
        slots = 3 if first else 2
        out_shape = (field,) * (1 + (not last) + first)
        results = pl.pallas_call(
            functools.partial(background_kernel, source_weight(t), first, last),
            grid=(1,),
            in_specs=[spec for _, spec in operands],
            out_specs=[whole(out.shape) for out in out_shape],
            out_shape=out_shape,
            scratch_shapes=[
                pltpu.VMEM((slots, layers, 3 * rows, columns), jnp.bfloat16),
                pltpu.VMEM((slots, layers, rows, columns), f32),
            ],
            compiler_params=params(),
            cost_estimate=pl.CostEstimate(
                flops=60 * cells_here, bytes_accessed=56 * cells_here, transcendentals=0
            ),
            name=f"background{t}",
        )(*[array for array, _ in operands])
        laps.append(results[0])
        if not last:
            older, current = current, flat(results[1])
            fields.append(results[1])
        if first:
            dg = results[2]

    def wave(mode, group, p, old, add, lap, extra=(), ends=None):
        low, high = ends or halo(p)
        one = pl.BlockSpec((None, *shape), lambda d: (d, 0, 0, 0))
        shifted = pl.BlockSpec((None, *shape), lambda d: (d + group * each, 0, 0, 0))
        same = whole(shape)
        operands, specs = [low, p, high], [shifted if ends else one] * 3
        if old is not None:
            operands.append(old)
            specs.append(one if old.shape[0] == each else shifted)
        operands += [array for array, _ in buoy] + [dg, stiffness]
        specs += [spec for _, spec in buoy] + [same] * 2
        if mode != "image":
            operands += [taper, add, lap]
            specs += [same, shifted if mode in ("born", "turn") else one, same]
        if mode == "turn":
            operands.append(counts)
            specs.append(same)
        if mode == "fold":
            specs += [shifted] + [same] * 4
        if mode == "image":
            specs += [one, pl.BlockSpec(memory_space=pltpu.SMEM)] + [same] * 2
        operands += [*extra, mx, my2]
        specs += [whole(mx.shape), whole(my2.shape)]
        out_shape, out_spec = (jax.ShapeDtypeStruct((each, *shape), f32),), [one]
        if mode == "fold":
            out_shape, out_spec = out_shape * 2, out_spec * 2
            if group == 0:
                out_shape, out_spec = out_shape + (field,) * 2, out_spec + [same] * 2
        if mode == "image":
            split = (layers, rows // owners, columns)
            out_shape = (jax.ShapeDtypeStruct((each, *split), f32),) * owners
            out_spec = [pl.BlockSpec((None, *split), lambda d: (d, 0, 0, 0))] * owners
        results = pl.pallas_call(
            functools.partial(wave_kernel, mode, old is not None),
            grid=(each,),
            in_specs=specs,
            out_specs=out_spec,
            out_shape=out_shape,
            scratch_shapes=[
                pltpu.VMEM((2, layers, 2 * rows, columns), jnp.bfloat16),
                pltpu.VMEM((2, layers, rows, columns), f32),
            ],
            compiler_params=params(),
            cost_estimate=pl.CostEstimate(
                flops=60 * each * cells_here,
                bytes_accessed=28 * each * cells_here,
                transcendentals=0,
            ),
            name=mode,
        )(*operands)
        return results[0] if len(results) == 1 else results

    born = [[None] * GROUPS for _ in range(STEPS + 1)]
    begun = taper * (perturbations * laps[0])
    ends = halo(begun)
    ahead = {(3, 0): fields[3], (3, 1): laps[3]}
    for t in (1, 2):
        for g in range(GROUPS):
            if t == 1:
                new = wave("born", g, begun, None, perturbations, laps[1], ends=ends)
            else:
                old = begun if t == 2 else born[t - 1][g]
                new = wave("born", g, born[t][g], old, perturbations, laps[t])
            if (t + 1, g) in ahead:
                new = after(new, ahead[t + 1, g])
            born[t + 1][g] = new
    adjoint = [[None] * GROUPS for _ in range(STEPS + 1)]
    for g in range(GROUPS):
        adjoint[3][g] = wave("turn", g, born[3][g], born[2][g], perturbations, laps[3])
    for g in range(GROUPS):
        adjoint[2][g] = wave("adjoint", g, adjoint[3][g], None, born[3][g], counts)
    known = [None] * GROUPS
    for g in range(GROUPS):
        adjoint[1][g], known[g], *rest = wave(
            "fold", g, adjoint[2][g], adjoint[3][g], born[2][g], counts, (begun, *laps)
        )
        if g == 0:
            weight, near = rest
    sketch = []
    for g in range(GROUPS):
        blocks = wave(
            "image", g, adjoint[1][g], None, None, None, (known[g], me, weight, near)
        )
        sketch.append(blocks[0])
        for s in range(1, owners):
            ring = [(i, (i + s) % owners) for i in range(owners)]
            sketch.append(lax.ppermute(blocks[s], "dirs", ring))

    total_dirs = owners * sketch_count
    local_rows = rows // owners
    square = (total_dirs, total_dirs)
    place = jnp.arange(total_dirs, dtype=jnp.int32)
    owner = (me[0] - place // sketch_count + owners) % owners
    local = owner * sketch_count + place % sketch_count
    selector = (column_order[:, None] == local[None, :]).astype(f32)
    gram = pl.pallas_call(
        functools.partial(gram_kernel, GROUPS),
        out_shape=jax.ShapeDtypeStruct(square, f32),
        scratch_shapes=[pltpu.VMEM((*square, LANE), f32)],
        compiler_params=params(),
        name="gram",
    )(selector, selector.T, *[s.reshape(each, layers * local_rows, columns) for s in sketch])
    gram = add_up(gram)
    grid_cells = layers * lax.axis_size("slab") * rows * columns
    part = (each, 1, local_rows, columns)
    basis, triangle = pl.pallas_call(
        functools.partial(basis_kernel, GROUPS, math.sqrt(grid_cells)),
        grid=(layers,),
        in_specs=[whole(square)] * 2
        + [pl.BlockSpec(part, lambda l: (0, l, 0, 0))] * len(sketch),
        out_specs=[
            pl.BlockSpec((total_dirs, 1, local_rows, columns), lambda l: (0, l, 0, 0)),
            whole(square),
        ],
        out_shape=(
            jax.ShapeDtypeStruct((total_dirs, layers, local_rows, columns), f32),
            jax.ShapeDtypeStruct(square, f32),
        ),
        scratch_shapes=[pltpu.VMEM((total_dirs * total_dirs, 8, LANE), f32)],
        compiler_params=params(),
        name="basis",
    )(gram, selector, *sketch)
    return basis, triangle


def solution(mesh):
    return jax.shard_map(
        shards,
        mesh=mesh,
        in_specs=(
            P("dirs", "slab", None, None),
            P("slab", None, None),
            P("slab", None, None),
            P("slab", None, None),
            P("slab", None, None),
            P("slab", None, None),
            P("slab"),
            P("slab"),
            P("slab"),
            P(),
        ),
        out_specs=(P(None, "slab", "dirs", None), P()),
        check_vma=False,
    )
```

```python
import functools
import math

import jax
import jax.numpy as jnp
from jax import lax
from jax.experimental import pallas as pl
from jax.experimental.pallas import tpu as pltpu
from jax.sharding import PartitionSpec as P

STEPS = 4
DAMPING = 0.3
TAPS = (8064.0, -1008.0, 128.0, -9.0)
CENTRE = 6.0 * sum(TAPS)
HALF = 0.5 / 5040.0
GROUPS = 2
VMEM = 22 * 1024 * 1024
LANE = 128


def band(shape, period):
    row = lax.broadcasted_iota(jnp.int32, shape, 0)
    column = lax.broadcasted_iota(jnp.int32, shape, 1) % period
    distance = jnp.abs(row - column)
    matrix = jnp.zeros(shape, jnp.float32)
    for k, tap in enumerate(TAPS, 1):
        matrix = jnp.where(distance == k, tap, matrix)
    return matrix.astype(jnp.bfloat16)


def source_weight(t):
    return (1.0 - 0.4 * t) * math.exp(-0.125 * t * t)


def params():
    return pltpu.CompilerParams(vmem_limit_bytes=VMEM)


def split_rows(y_ref, slot, layer, row, values, parts, rows):
    size = values.shape[0]
    for s in range(parts):
        part = values.astype(jnp.bfloat16)
        y_ref[slot, layer, s * rows + row : s * rows + row + size, :] = part
        if s < parts - 1:
            values = values - part.astype(jnp.float32)


def plane_part(functions, y_ref, a_ref, mx_ref, my_ref, parts):
    _, layers, rows, _ = a_ref.shape
    for layer in range(layers):
        for row in range(0, rows, 32):
            for slot, values in enumerate(functions(layer, row, 32)):
                split_rows(y_ref, slot, layer, row, values, parts, rows)
    for slot in range(a_ref.shape[0]):
        for layer in range(layers):
            y = y_ref[slot, layer]
            along = jnp.dot(y, mx_ref[...], preferred_element_type=jnp.float32)
            total = jnp.dot(my_ref[...], y, preferred_element_type=jnp.float32)
            for s in range(parts):
                total = total + along[s * rows : (s + 1) * rows]
            a_ref[slot, layer] = total


def depth_part(tall, layer):
    total = None
    for k, tap in enumerate(TAPS, 1):
        term = tap * (tall[layer + 4 + k] + tall[layer + 4 - k])
        total = term if total is None else total + term
    return total


def tall_of(refs, rows, columns):
    low, mid, high = refs
    return [ref[layer, rows, columns] for ref in (low, mid, high) for layer in range(4)]


def tiles(rows, columns, body, start=0):
    def step(i, carry):
        at = pl.ds(pl.multiple_of(start + i * 8, 8), 8)
        for column in range(0, columns, LANE):
            body(i, at, slice(column, column + LANE))
        return carry

    lax.fori_loop(0, rows // 8, step, 0)


def place_kernel(copies, rc_ref, sc_ref, amp_ref, mask_ref, *refs):
    sources, refs = refs[:copies], refs[copies:]
    m_ref, src_ref, taper_ref, mx_ref, my2_ref, my3_ref = refs[:6]
    for source, target in zip(sources, refs[6:]):
        target[...] = source[...]
    layers, rows, columns = m_ref.shape
    for matrix in (mx_ref, my2_ref, my3_ref):
        matrix[...] = band(matrix.shape, matrix.shape[0])
    count = rc_ref.shape[1]
    lines = layers * rows
    chunk = min(256, count)
    total = None
    for start in range(0, count, chunk):
        cells = rc_ref[:, start : start + chunk]
        line = lax.broadcasted_iota(jnp.int32, (lines, chunk), 0) == cells // columns
        column = lax.broadcasted_iota(jnp.int32, (columns, chunk), 0) == cells % columns
        part = lax.dot_general(
            jnp.where(line, 1.0, 0.0).astype(jnp.bfloat16),
            jnp.where(column, 1.0, 0.0).astype(jnp.bfloat16),
            (((1,), (1,)), ((), ())),
            preferred_element_type=jnp.float32,
        )
        total = part if total is None else total + part
    m_ref[...] = total.reshape(m_ref.shape)
    cells = sc_ref[...]
    count = cells.shape[1]
    line = lax.broadcasted_iota(jnp.int32, (lines, count), 0) == cells // columns
    column = lax.broadcasted_iota(jnp.int32, (columns, count), 0) == cells % columns
    part = lax.dot_general(
        jnp.where(line, 1.0, 0.0),
        jnp.where(column, amp_ref[...], 0.0),
        (((1,), (1,)), ((), ())),
        precision=lax.Precision.HIGHEST,
        preferred_element_type=jnp.float32,
    )
    src_ref[...] = part.reshape(src_ref.shape)
    taper_ref[...] = 1.0 - DAMPING * mask_ref[...].astype(jnp.float32)


def marks_kernel(cells_ref, line_ref, column_ref):
    cells = cells_ref[...]
    columns = column_ref.shape[0]
    line = lax.broadcasted_iota(jnp.int32, line_ref.shape, 0) == cells // columns
    column = lax.broadcasted_iota(jnp.int32, column_ref.shape, 0) == cells % columns
    line_ref[...] = jnp.where(line, 1.0, 0.0).astype(jnp.bfloat16)
    column_ref[...] = jnp.where(column, 1.0, 0.0)


def halves(values):
    high = values.astype(jnp.bfloat16)
    return high, (values - high.astype(jnp.float32)).astype(jnp.bfloat16)


def read_at(field, line_ref, column_ref):
    total = None
    for part in halves(field):
        lines = lax.dot_general(
            part, line_ref[...], (((0,), (0,)), ((), ())), preferred_element_type=jnp.float32
        )
        total = lines if total is None else total + lines
    return jnp.sum(total * column_ref[...], axis=0, keepdims=True)


def add_at(records, line_ref, column_ref):
    total = None
    for part in halves(records):
        spread = (column_ref[...] * part.astype(jnp.float32)).astype(jnp.bfloat16)
        field = lax.dot_general(
            line_ref[...], spread, (((1,), (1,)), ((), ())), preferred_element_type=jnp.float32
        )
        total = field if total is None else total + field
    return total


def background_kernel(weight, first, last, *refs):
    refs = list(refs)
    u = [refs.pop(0) for _ in range(3)]
    b = [refs.pop(0) for _ in range(3)]
    stiff_ref = refs.pop(0)
    dg_ref = None if first else refs.pop(0)
    taper_ref = src_ref = older_ref = new_ref = None
    if not last:
        taper_ref, src_ref, older_ref = (refs.pop(0) for _ in range(3))
    mx_ref, my_ref = refs.pop(0), refs.pop(0)
    lap_ref = refs.pop(0)
    if not last:
        new_ref = refs.pop(0)
    if first:
        dg_ref = refs.pop(0)
    y_ref, a_ref = refs

    def functions(layer, row, size):
        value = u[1][layer, row : row + size]
        buoy = b[1][layer, row : row + size]
        return [value, value * buoy] + ([buoy] if first else [])

    plane_part(functions, y_ref, a_ref, mx_ref, my_ref, 3)

    def body(i, at, columns):
        value = tall_of(u, at, columns)
        buoy = tall_of(b, at, columns)
        both = [x * y for x, y in zip(value, buoy)]
        for layer in range(4):
            here, b_here = value[layer + 4], buoy[layer + 4]
            if first:
                dg = depth_part(buoy, layer) + a_ref[2, layer, at, columns] + CENTRE * b_here
                dg_ref[layer, at, columns] = dg
            else:
                dg = dg_ref[layer, at, columns]
            plain = depth_part(value, layer) + a_ref[0, layer, at, columns]
            times = depth_part(both, layer) + a_ref[1, layer, at, columns]
            lap = HALF * (b_here * plain + times - here * dg)
            lap_ref[layer, at, columns] = lap
            if not last:
                new_ref[layer, at, columns] = (
                    taper_ref[layer, at, columns]
                    * (
                        2.0 * here
                        - older_ref[layer, at, columns]
                        + stiff_ref[layer, at, columns] * lap
                    )
                    + weight * src_ref[layer, at, columns]
                )

    tiles(*lap_ref.shape[1:], body)


def wave_kernel(mode, has_old, *refs):
    refs = list(refs)
    p = [refs.pop(0) for _ in range(3)]
    old_ref = refs.pop(0) if has_old else None
    b = [refs.pop(0) for _ in range(3)]
    dg_ref, stiff_ref = refs.pop(0), refs.pop(0)
    if mode == "image":
        sum_ref, me_ref, weight_ref, near_ref = (refs.pop(0) for _ in range(4))
    else:
        taper_ref, add_ref, lap_ref = (refs.pop(0) for _ in range(3))
    if mode in ("turn", "read"):
        count_ref = refs.pop(0)
    if mode == "read":
        line_ref, column_ref = refs.pop(0), refs.pop(0)
    if mode == "spread":
        marks = [refs.pop(0) for _ in range(4)]
    if mode == "fold":
        first_ref = refs.pop(0)
        laps = [refs.pop(0) for _ in range(4)]
    mx_ref, my_ref = refs.pop(0), refs.pop(0)
    if mode == "spread":
        *refs, low_ref, high_ref = refs
        low_ref[...] = add_at(p[0][...], *marks[:2]).reshape(low_ref.shape)
        high_ref[...] = add_at(p[2][...], *marks[2:]).reshape(high_ref.shape)
        p = [low_ref, p[1], high_ref]
    y_ref, a_ref = refs[-2:]
    outs = refs[:-2]

    def functions(layer, row, size):
        value = p[1][layer, row : row + size]
        return value, value * b[1][layer, row : row + size]

    plane_part(functions, y_ref, a_ref, mx_ref, my_ref, 2)

    def body(block, i, at, columns):
        value = tall_of(p, at, columns)
        buoy = tall_of(b, at, columns)
        both = [x * y for x, y in zip(value, buoy)]
        for layer in range(4):
            here = value[layer + 4]
            spot = (layer, at, columns)
            plain = depth_part(value, layer) + a_ref[0, layer, at, columns]
            times = depth_part(both, layer) + a_ref[1, layer, at, columns]
            lb = buoy[layer + 4] * plain + times - here * dg_ref[spot]
            total = 2.0 * here + (HALF * stiff_ref[spot]) * lb
            if mode == "image":
                inner = pl.ds(pl.multiple_of(i * 8, 8), 8)
                outs[block][layer, inner, columns] = (
                    sum_ref[spot] + near_ref[spot] * here + weight_ref[spot] * total
                )
                continue
            if has_old:
                old = old_ref[spot]
                total = total - old
            taper = taper_ref[spot]
            added = add_ref[spot] * lap_ref[spot]
            if mode in ("born", "turn", "read"):
                new = taper * (total + added)
            else:
                new = taper * total + added
            if mode == "read":
                a_ref[0, layer, at, columns] = new
            if mode in ("turn", "read"):
                new = count_ref[spot] * new
            outs[0][spot] = new
            if mode == "fold":
                weight = laps[0][spot] * taper
                known = laps[3][spot] * old + laps[2][spot] * here
                known = known + laps[0][spot] * (lap_ref[spot] * first_ref[spot])
                outs[1][spot] = known - weight * here
                if len(outs) > 2:
                    outs[2][spot] = weight
                    outs[3][spot] = laps[1][spot]

    _, rows, columns = p[1].shape
    if mode == "image":
        per = rows // len(outs)
        for block in range(len(outs)):
            owner = lax.rem(me_ref[0] + block, len(outs))
            tiles(per, columns, functools.partial(body, block), owner * per)
    else:
        tiles(rows, columns, functools.partial(body, 0))
    if mode == "read":
        outs[1][...] = read_at(a_ref[0].reshape(-1, columns), line_ref, column_ref)


def piece_of(pieces, parts, c):
    each = pieces[0].shape[0]
    block, rest = divmod(c, parts * each)
    group, inner = divmod(rest, each)
    return pieces[group * (len(pieces) // parts) + block], inner


def gram_kernel(parts, sel_ref, selt_ref, *refs):
    *pieces, out_ref, lanes_ref = refs
    count = sel_ref.shape[0]
    _, rows, columns = pieces[0].shape

    def piece(c, at, column):
        ref, inner = piece_of(pieces, parts, c)
        return ref[inner, at, column : column + LANE]

    for i0 in range(0, count, 4):
        for j0 in range(i0 // 8 * 8, count, 8):

            def step(r, accs, i0=i0, j0=j0):
                at = pl.ds(pl.multiple_of(r * 8, 8), 8)
                accs = list(accs)
                for column in range(0, columns, LANE):
                    left = [piece(i0 + i, at, column) for i in range(4)]
                    for j in range(8):
                        right = piece(j0 + j, at, column)
                        for i in range(4):
                            accs[i * 8 + j] = accs[i * 8 + j] + left[i] * right
                return tuple(accs)

            zero = jnp.zeros((8, LANE), jnp.float32)
            accs = lax.fori_loop(0, rows // 8, step, (zero,) * 32)
            for i in range(4):
                for j in range(8):
                    lanes_ref[i0 + i, j0 + j : j0 + j + 1, :] = jnp.sum(
                        accs[i * 8 + j], axis=0, keepdims=True
                    )
    local = jnp.sum(lanes_ref[...], axis=-1)
    row = lax.broadcasted_iota(jnp.int32, local.shape, 0)
    column = lax.broadcasted_iota(jnp.int32, local.shape, 1)
    local = jnp.where(row // 8 > column // 8, local.T, local)
    out_ref[...] = exact(exact(sel_ref[...], local), selt_ref[...])


def exact(left, right):
    return jnp.dot(left, right, precision=lax.Precision.HIGHEST, preferred_element_type=jnp.float32)


def basis_kernel(parts, scale, gram_ref, sel_ref, *refs):
    *pieces, out_ref, triangle_ref, spread_ref = refs
    count = gram_ref.shape[0]
    _, _, rows, columns = pieces[0].shape

    @pl.when(pl.program_id(0) == 0)
    def _():
        row = lax.broadcasted_iota(jnp.int32, (count, count), 0)
        column = lax.broadcasted_iota(jnp.int32, (count, count), 1)
        left = gram_ref[...]
        unit = jnp.where(row == column, 1.0, 0.0)
        for i in range(count):
            pivot = jnp.sqrt(left[i : i + 1, i : i + 1])
            upper = left[i : i + 1, :] / pivot
            solved = unit[i : i + 1, :] / pivot
            below = left[:, i : i + 1] / pivot
            is_row = row == i
            left = jnp.where(is_row, upper, jnp.where(row > i, left - below * upper, left))
            unit = jnp.where(is_row, solved, jnp.where(row > i, unit - below * solved, unit))
        triangle_ref[...] = jnp.where(column >= row, left, 0.0) / scale
        weights = exact(unit, sel_ref[...]) * scale
        for i in range(count):
            for c in range(count):
                spread_ref[i * count + c] = jnp.broadcast_to(
                    weights[i : i + 1, c : c + 1], (8, LANE)
                )

    def piece(c, at, columns):
        ref, inner = piece_of(pieces, parts, c)
        return ref[inner, 0, at, columns]

    halves = [slice(column, column + LANE) for column in range(0, columns, LANE)]
    for r in range(0, rows, 8):
        at = slice(r, r + 8)
        values = [[piece(c, at, half) for half in halves] for c in range(count)]
        for i in range(count):
            totals = [None] * len(halves)
            for c in range(count):
                weight = spread_ref[i * count + c]
                for h in range(len(halves)):
                    term = weight * values[c][h]
                    totals[h] = term if totals[h] is None else totals[h] + term
            for h, half in enumerate(halves):
                out_ref[i, 0, at, half] = totals[h]


def halo(block):
    count = lax.axis_size("slab")
    forward = [(i, i + 1) for i in range(count - 1)]
    backward = [(target, source) for source, target in forward]
    return lax.ppermute(block, "slab", forward), lax.ppermute(block, "slab", backward)


def whole(shape):
    zeros = (0,) * len(shape)
    return pl.BlockSpec(tuple(shape), lambda *_: zeros)


def add_up(value):
    for axis in ("slab", "dirs"):
        size, stride = lax.axis_size(axis), 1
        while stride < size:
            value = value + lax.ppermute(value, axis, [(i, i ^ stride) for i in range(size)])
            stride *= 2
    return value


def shards(
    perturbations,
    background_now,
    background_prev,
    stiffness,
    buoyancy,
    absorb_mask,
    source_cells,
    source_amp,
    receiver_cells,
    column_order,
):
    shape = buoyancy.shape
    layers, rows, columns = shape
    sketch_count = perturbations.shape[0]
    each = sketch_count // GROUPS
    owners = lax.axis_size("dirs")
    me = lax.axis_index("dirs").astype(jnp.int32).reshape(1)
    f32 = jnp.float32
    field = jax.ShapeDtypeStruct(shape, f32)
    cells_here = layers * rows * columns
    def after(value, earlier):
        return lax.optimization_barrier((value, earlier))[0]

    def view(array, index):
        return array, pl.BlockSpec((None, *shape), lambda *_: (index, 0, 0, 0))

    low, high = halo(jnp.stack([buoyancy, background_now]))
    b_low, u_low = view(low, 0), view(low, 1)
    b_high, u_high = view(high, 0), view(high, 1)

    def matrix(*size):
        return jax.ShapeDtypeStruct(size, jnp.bfloat16)

    copied = (stiffness, buoyancy, background_now, background_prev, perturbations)
    matrices = (matrix(columns, columns), matrix(rows, 2 * rows), matrix(rows, 3 * rows))
    (
        counts, source_field, taper, mx, my2, my3, stiffness, b_mid, current, older, perturbations
    ) = pl.pallas_call(
        functools.partial(place_kernel, len(copied)),
        out_shape=(field,) * 3 + matrices + (*[field] * 4, jax.ShapeDtypeStruct(perturbations.shape, f32)),
        compiler_params=params(),
        cost_estimate=pl.CostEstimate(
            flops=40 * cells_here, bytes_accessed=16 * cells_here, transcendentals=0
        ),
        name="place",
    )(
        receiver_cells.reshape(1, -1),
        source_cells.reshape(1, -1),
        source_amp.reshape(1, -1),
        absorb_mask,
        *copied,
    )

    def marks(cells):
        return pl.pallas_call(
            marks_kernel,
            out_shape=(
                matrix(layers * rows, receivers),
                jax.ShapeDtypeStruct((columns, receivers), f32),
            ),
            compiler_params=params(),
            name="marks",
        )(cells)

    cells = receiver_cells.reshape(1, -1)
    receivers = cells.shape[-1]
    at_mine = marks(cells)
    at_low, at_high = (marks(other) for other in halo(cells))

    def flat(array):
        return array, whole(array.shape)

    buoy = (b_low, flat(b_mid), b_high)
    current, older = flat(current), flat(older)
    fields = [None]
    laps = []
    dg = None
    for t in range(STEPS):
        first, last = t == 0, t == STEPS - 1
        if not first:
            u_low, u_high = (flat(end) for end in halo(current[0]))
        operands = [u_low, current, u_high, *buoy, flat(stiffness)]
        if not first:
            operands.append(flat(dg))
        if not last:
            operands += [flat(taper), flat(source_field), older]
        operands += [flat(mx), flat(my3)]
        slots = 3 if first else 2
        out_shape = (field,) * (1 + (not last) + first)
        results = pl.pallas_call(
            functools.partial(background_kernel, source_weight(t), first, last),
            grid=(1,),
            in_specs=[spec for _, spec in operands],
            out_specs=[whole(out.shape) for out in out_shape],
            out_shape=out_shape,
            scratch_shapes=[
                pltpu.VMEM((slots, layers, 3 * rows, columns), jnp.bfloat16),
                pltpu.VMEM((slots, layers, rows, columns), f32),
            ],
            compiler_params=params(),
            cost_estimate=pl.CostEstimate(
                flops=60 * cells_here, bytes_accessed=56 * cells_here, transcendentals=0
            ),
            name=f"background{t}",
        )(*[array for array, _ in operands])
        laps.append(results[0])
        if not last:
            older, current = current, flat(results[1])
            fields.append(results[1])
        if first:
            dg = after(results[2], (at_mine, at_low, at_high))

    def wave(mode, group, p, old, add, lap, extra=(), records=None, wait=None):
        low, high = halo(p if records is None else records)
        if wait is not None:
            low = after(low, wait)
        one = pl.BlockSpec((None, *shape), lambda d: (d, 0, 0, 0))
        shifted = pl.BlockSpec((None, *shape), lambda d: (d + group * each, 0, 0, 0))
        same = whole(shape)
        heard = pl.BlockSpec((None, 1, receivers), lambda d: (d, 0, 0))
        side = one if records is None else heard
        operands, specs = [low, p, high], [side, one, side]
        if old is not None:
            operands.append(old)
            specs.append(one)
        operands += [array for array, _ in buoy] + [dg, stiffness]
        specs += [spec for _, spec in buoy] + [same] * 2
        if mode != "image":
            operands += [taper, add, lap]
            specs += [same, shifted if mode in ("born", "turn", "read") else one, same]
        if mode in ("turn", "read"):
            operands.append(counts)
            specs.append(same)
        if mode == "read":
            operands += at_mine
            specs += [whole(mark.shape) for mark in at_mine]
        if mode == "spread":
            operands += [*at_low, *at_high]
            specs += [whole(mark.shape) for mark in (*at_low, *at_high)]
        if mode == "fold":
            specs += [one] + [same] * 4
        if mode == "image":
            specs += [one, pl.BlockSpec(memory_space=pltpu.SMEM)] + [same] * 2
        operands += [*extra, mx, my2]
        specs += [whole(mx.shape), whole(my2.shape)]
        out_shape, out_spec = (jax.ShapeDtypeStruct((each, *shape), f32),), [one]
        if mode == "fold":
            out_shape, out_spec = out_shape * 2, out_spec * 2
            if group == 0:
                out_shape, out_spec = out_shape + (field,) * 2, out_spec + [same] * 2
        if mode == "read":
            out_shape += (jax.ShapeDtypeStruct((each, 1, receivers), f32),)
            out_spec = out_spec + [heard]
        if mode == "image":
            split = (layers, rows // owners, columns)
            out_shape = (jax.ShapeDtypeStruct((each, *split), f32),) * owners
            out_spec = [pl.BlockSpec((None, *split), lambda d: (d, 0, 0, 0))] * owners
        results = pl.pallas_call(
            functools.partial(wave_kernel, mode, old is not None),
            grid=(each,),
            in_specs=specs,
            out_specs=out_spec,
            out_shape=out_shape,
            scratch_shapes=[
                pltpu.VMEM((2, layers, 2 * rows, columns), jnp.bfloat16),
                pltpu.VMEM((2, layers, rows, columns), f32),
            ]
            + [pltpu.VMEM(shape, f32)] * (2 if mode == "spread" else 0),
            compiler_params=params(),
            cost_estimate=pl.CostEstimate(
                flops=60 * each * cells_here,
                bytes_accessed=28 * each * cells_here,
                transcendentals=0,
            ),
            name=mode,
        )(*operands)
        return results[0] if len(results) == 1 else results

    born = [[None] * GROUPS for _ in range(STEPS + 1)]
    for g in range(GROUPS):
        born[1][g] = taper * (perturbations[g * each : (g + 1) * each] * laps[0])
    born[1][1] = after(born[1][1], fields[2])
    ahead = {(2, 1): fields[3], (3, 1): laps[3]}
    for t in (1, 2):
        for g in range(GROUPS):
            old = born[t - 1][g] if t > 1 else None
            new = wave("born", g, born[t][g], old, perturbations, laps[t])
            if (t + 1, g) in ahead:
                new = after(new, ahead[t + 1, g])
            born[t + 1][g] = new
    adjoint = [[None] * GROUPS for _ in range(STEPS + 1)]
    adjoint[3][0] = wave("turn", 0, born[3][0], born[2][0], perturbations, laps[3])
    adjoint[3][1], records = wave("read", 1, born[3][1], born[2][1], perturbations, laps[3])
    adjoint[2][0] = wave("adjoint", 0, adjoint[3][0], None, born[3][0], counts)
    adjoint[2][1] = wave(
        "spread", 1, adjoint[3][1], None, born[3][1], counts,
        records=records, wait=adjoint[2][0],
    )
    known = [None] * GROUPS
    for g in range(GROUPS):
        adjoint[1][g], known[g], *rest = wave(
            "fold", g, adjoint[2][g], adjoint[3][g], born[2][g], counts, (born[1][g], *laps),
            wait=adjoint[1][g - 1] if g else None,
        )
        if g == 0:
            weight, near = rest
    sketch = []
    for g in range(GROUPS):
        blocks = wave(
            "image", g, adjoint[1][g], None, None, None, (known[g], me, weight, near)
        )
        sketch.append(blocks[0])
        for s in range(1, owners):
            ring = [(i, (i + s) % owners) for i in range(owners)]
            sketch.append(lax.ppermute(blocks[s], "dirs", ring))

    total_dirs = owners * sketch_count
    local_rows = rows // owners
    square = (total_dirs, total_dirs)
    place = jnp.arange(total_dirs, dtype=jnp.int32)
    owner = (me[0] - place // sketch_count + owners) % owners
    local = owner * sketch_count + place % sketch_count
    selector = (column_order[:, None] == local[None, :]).astype(f32)
    gram = pl.pallas_call(
        functools.partial(gram_kernel, GROUPS),
        out_shape=jax.ShapeDtypeStruct(square, f32),
        scratch_shapes=[pltpu.VMEM((*square, LANE), f32)],
        compiler_params=params(),
        name="gram",
    )(selector, selector.T, *[s.reshape(each, layers * local_rows, columns) for s in sketch])
    gram = add_up(gram)
    grid_cells = layers * lax.axis_size("slab") * rows * columns
    part = (each, 1, local_rows, columns)
    basis, triangle = pl.pallas_call(
        functools.partial(basis_kernel, GROUPS, math.sqrt(grid_cells)),
        grid=(layers,),
        in_specs=[whole(square)] * 2
        + [pl.BlockSpec(part, lambda l: (0, l, 0, 0))] * len(sketch),
        out_specs=[
            pl.BlockSpec((total_dirs, 1, local_rows, columns), lambda l: (0, l, 0, 0)),
            whole(square),
        ],
        out_shape=(
            jax.ShapeDtypeStruct((total_dirs, layers, local_rows, columns), f32),
            jax.ShapeDtypeStruct(square, f32),
        ),
        scratch_shapes=[pltpu.VMEM((total_dirs * total_dirs, 8, LANE), f32)],
        compiler_params=params(),
        name="basis",
    )(gram, selector, *sketch)
    return basis, triangle


def solution(mesh):
    return jax.shard_map(
        shards,
        mesh=mesh,
        in_specs=(
            P("dirs", "slab", None, None),
            P("slab", None, None),
            P("slab", None, None),
            P("slab", None, None),
            P("slab", None, None),
            P("slab", None, None),
            P("slab"),
            P("slab"),
            P("slab"),
            P(),
        ),
        out_specs=(P(None, "slab", "dirs", None), P()),
        check_vma=False,
    )
```

```python
import functools
import math

import jax
import jax.numpy as jnp
from jax import lax
from jax.experimental import pallas as pl
from jax.experimental.pallas import tpu as pltpu
from jax.sharding import PartitionSpec as P

STEPS = 4
DAMPING = 0.3
TAPS = (8064.0, -1008.0, 128.0, -9.0)
CENTRE = 6.0 * sum(TAPS)
HALF = 0.5 / 5040.0
GROUPS = 2
VMEM = 22 * 1024 * 1024
LANE = 128
WHOLE = ("born", "turn", "adjoint", "fold", "image")


def band(shape, period):
    row = lax.broadcasted_iota(jnp.int32, shape, 0)
    column = lax.broadcasted_iota(jnp.int32, shape, 1) % period
    distance = jnp.abs(row - column)
    matrix = jnp.zeros(shape, jnp.float32)
    for k, tap in enumerate(TAPS, 1):
        matrix = jnp.where(distance == k, tap, matrix)
    return matrix.astype(jnp.bfloat16)


def source_weight(t):
    return (1.0 - 0.4 * t) * math.exp(-0.125 * t * t)


def params():
    return pltpu.CompilerParams(vmem_limit_bytes=VMEM)


def split_rows(y_ref, slot, layer, row, values, parts, rows):
    size = values.shape[0]
    for s in range(parts):
        part = values.astype(jnp.bfloat16)
        y_ref[slot, layer, s * rows + row : s * rows + row + size, :] = part
        if s < parts - 1:
            values = values - part.astype(jnp.float32)


def plane_part(functions, y_ref, a_ref, mx_ref, my_ref, parts):
    _, layers, rows, _ = a_ref.shape
    for layer in range(layers):
        for row in range(0, rows, 32):
            for slot, values in enumerate(functions(layer, row, 32)):
                split_rows(y_ref, slot, layer, row, values, parts, rows)
    for slot in range(a_ref.shape[0]):
        for layer in range(layers):
            y = y_ref[slot, layer]
            along = jnp.dot(y, mx_ref[...], preferred_element_type=jnp.float32)
            total = jnp.dot(my_ref[...], y, preferred_element_type=jnp.float32)
            for s in range(parts):
                total = total + along[s * rows : (s + 1) * rows]
            a_ref[slot, layer] = total


def depth_part(tall, layer):
    total = None
    for k, tap in enumerate(TAPS, 1):
        term = tap * (tall[layer + 4 + k] + tall[layer + 4 - k])
        total = term if total is None else total + term
    return total


def tall_of(refs, rows, columns):
    low, mid, high = refs
    return [ref[layer, rows, columns] for ref in (low, mid, high) for layer in range(4)]


def tiles(rows, columns, body, start=0):
    def step(i, carry):
        at = pl.ds(pl.multiple_of(start + i * 8, 8), 8)
        for column in range(0, columns, LANE):
            body(i, at, slice(column, column + LANE))
        return carry

    lax.fori_loop(0, rows // 8, step, 0)


def place_kernel(copies, rc_ref, sc_ref, amp_ref, mask_ref, *refs):
    sources, refs = refs[:copies], refs[copies:]
    m_ref, src_ref, taper_ref, mx_ref, my2_ref, my3_ref = refs[:6]
    for source, target in zip(sources, refs[6:]):
        target[...] = source[...]
    layers, rows, columns = m_ref.shape
    for matrix in (mx_ref, my2_ref, my3_ref):
        matrix[...] = band(matrix.shape, matrix.shape[0])
    count = rc_ref.shape[1]
    lines = layers * rows
    chunk = min(256, count)
    total = None
    for start in range(0, count, chunk):
        cells = rc_ref[:, start : start + chunk]
        line = lax.broadcasted_iota(jnp.int32, (lines, chunk), 0) == cells // columns
        column = lax.broadcasted_iota(jnp.int32, (columns, chunk), 0) == cells % columns
        part = lax.dot_general(
            jnp.where(line, 1.0, 0.0).astype(jnp.bfloat16),
            jnp.where(column, 1.0, 0.0).astype(jnp.bfloat16),
            (((1,), (1,)), ((), ())),
            preferred_element_type=jnp.float32,
        )
        total = part if total is None else total + part
    m_ref[...] = total.reshape(m_ref.shape)
    cells = sc_ref[...]
    count = cells.shape[1]
    line = lax.broadcasted_iota(jnp.int32, (lines, count), 0) == cells // columns
    column = lax.broadcasted_iota(jnp.int32, (columns, count), 0) == cells % columns
    part = lax.dot_general(
        jnp.where(line, 1.0, 0.0),
        jnp.where(column, amp_ref[...], 0.0),
        (((1,), (1,)), ((), ())),
        precision=lax.Precision.HIGHEST,
        preferred_element_type=jnp.float32,
    )
    src_ref[...] = part.reshape(src_ref.shape)
    taper_ref[...] = 1.0 - DAMPING * mask_ref[...].astype(jnp.float32)


def background_kernel(weight, first, last, *refs):
    refs = list(refs)
    u = [refs.pop(0) for _ in range(3)]
    b = [refs.pop(0) for _ in range(3)]
    stiff_ref = refs.pop(0)
    dg_ref = None if first else refs.pop(0)
    taper_ref = src_ref = older_ref = new_ref = None
    if not last:
        taper_ref, src_ref, older_ref = (refs.pop(0) for _ in range(3))
    mx_ref, my_ref = refs.pop(0), refs.pop(0)
    lap_ref = refs.pop(0)
    if not last:
        new_ref = refs.pop(0)
    if first:
        dg_ref = refs.pop(0)
    y_ref, a_ref = refs

    def functions(layer, row, size):
        value = u[1][layer, row : row + size]
        buoy = b[1][layer, row : row + size]
        return [value, value * buoy] + ([buoy] if first else [])

    plane_part(functions, y_ref, a_ref, mx_ref, my_ref, 3)

    def body(i, at, columns):
        value = tall_of(u, at, columns)
        buoy = tall_of(b, at, columns)
        both = [x * y for x, y in zip(value, buoy)]
        for layer in range(4):
            here, b_here = value[layer + 4], buoy[layer + 4]
            if first:
                dg = depth_part(buoy, layer) + a_ref[2, layer, at, columns] + CENTRE * b_here
                dg_ref[layer, at, columns] = dg
            else:
                dg = dg_ref[layer, at, columns]
            plain = depth_part(value, layer) + a_ref[0, layer, at, columns]
            times = depth_part(both, layer) + a_ref[1, layer, at, columns]
            lap = HALF * (b_here * plain + times - here * dg)
            lap_ref[layer, at, columns] = lap
            if not last:
                new_ref[layer, at, columns] = (
                    taper_ref[layer, at, columns]
                    * (
                        2.0 * here
                        - older_ref[layer, at, columns]
                        + stiff_ref[layer, at, columns] * lap
                    )
                    + weight * src_ref[layer, at, columns]
                )

    tiles(*lap_ref.shape[1:], body)


def wave_kernel(mode, has_old, *refs):
    refs = list(refs)
    p = [refs.pop(0) for _ in range(3)]
    old_ref = refs.pop(0) if has_old else None
    b = [refs.pop(0) for _ in range(3)]
    dg_ref, stiff_ref = refs.pop(0), refs.pop(0)
    if mode == "image":
        sum_ref, me_ref, weight_ref, near_ref = (refs.pop(0) for _ in range(4))
    else:
        taper_ref, add_ref, lap_ref = (refs.pop(0) for _ in range(3))
    count_ref = refs.pop(0) if mode == "turn" else None
    if mode == "fold":
        first_ref = refs.pop(0)
        laps = [refs.pop(0) for _ in range(4)]
    mx_ref, my_ref = refs.pop(0), refs.pop(0)
    y_ref, a_ref = refs[-2:]
    outs = refs[:-2]

    def functions(layer, row, size):
        value = p[1][layer, row : row + size]
        return value, value * b[1][layer, row : row + size]

    plane_part(functions, y_ref, a_ref, mx_ref, my_ref, 2)

    def body(block, i, at, columns):
        value = tall_of(p, at, columns)
        buoy = tall_of(b, at, columns)
        both = [x * y for x, y in zip(value, buoy)]
        for layer in range(4):
            here = value[layer + 4]
            spot = (layer, at, columns)
            plain = depth_part(value, layer) + a_ref[0, layer, at, columns]
            times = depth_part(both, layer) + a_ref[1, layer, at, columns]
            lb = buoy[layer + 4] * plain + times - here * dg_ref[spot]
            total = 2.0 * here + (HALF * stiff_ref[spot]) * lb
            if mode == "image":
                inner = pl.ds(pl.multiple_of(i * 8, 8), 8)
                outs[block][layer, inner, columns] = (
                    sum_ref[spot] + near_ref[spot] * here + weight_ref[spot] * total
                )
                continue
            if has_old:
                old = old_ref[spot]
                total = total - old
            taper = taper_ref[spot]
            added = add_ref[spot] * lap_ref[spot]
            if mode in ("born", "turn"):
                new = taper * (total + added)
            else:
                new = taper * total + added
            if mode == "turn":
                new = count_ref[spot] * new
            outs[0][spot] = new
            if mode == "fold":
                weight = laps[0][spot] * taper
                known = laps[3][spot] * old + laps[2][spot] * here
                known = known + laps[0][spot] * (lap_ref[spot] * first_ref[spot])
                outs[1][spot] = known - weight * here
                if len(outs) > 2:
                    outs[2][spot] = weight
                    outs[3][spot] = laps[1][spot]

    _, rows, columns = p[1].shape
    if mode == "image":
        per = rows // len(outs)
        for block in range(len(outs)):
            owner = lax.rem(me_ref[0] + block, len(outs))
            tiles(per, columns, functools.partial(body, block), owner * per)
    else:
        tiles(rows, columns, functools.partial(body, 0))


def all_waves(mode, has_old, picks, each, *refs):
    for d in range(each):
        views = [ref if at is None else ref.at[d + at] for ref, at in zip(refs, picks)]
        wave_kernel(mode, has_old, *views, *refs[len(picks) :])


def piece_of(pieces, parts, c):
    each = pieces[0].shape[0]
    block, rest = divmod(c, parts * each)
    group, inner = divmod(rest, each)
    return pieces[group * (len(pieces) // parts) + block], inner


def gram_kernel(parts, sel_ref, selt_ref, *refs):
    *pieces, out_ref, lanes_ref = refs
    count = sel_ref.shape[0]
    _, rows, columns = pieces[0].shape

    def piece(c, at, column):
        ref, inner = piece_of(pieces, parts, c)
        return ref[inner, at, column : column + LANE]

    for i0 in range(0, count, 4):
        for j0 in range(i0 // 8 * 8, count, 8):

            def step(r, accs, i0=i0, j0=j0):
                at = pl.ds(pl.multiple_of(r * 8, 8), 8)
                accs = list(accs)
                for column in range(0, columns, LANE):
                    left = [piece(i0 + i, at, column) for i in range(4)]
                    for j in range(8):
                        right = piece(j0 + j, at, column)
                        for i in range(4):
                            accs[i * 8 + j] = accs[i * 8 + j] + left[i] * right
                return tuple(accs)

            zero = jnp.zeros((8, LANE), jnp.float32)
            accs = lax.fori_loop(0, rows // 8, step, (zero,) * 32)
            for i in range(4):
                for j in range(8):
                    lanes_ref[i0 + i, j0 + j : j0 + j + 1, :] = jnp.sum(
                        accs[i * 8 + j], axis=0, keepdims=True
                    )
    local = jnp.sum(lanes_ref[...], axis=-1)
    row = lax.broadcasted_iota(jnp.int32, local.shape, 0)
    column = lax.broadcasted_iota(jnp.int32, local.shape, 1)
    local = jnp.where(row // 8 > column // 8, local.T, local)
    out_ref[...] = exact(exact(sel_ref[...], local), selt_ref[...])


def exact(left, right):
    return jnp.dot(left, right, precision=lax.Precision.HIGHEST, preferred_element_type=jnp.float32)


def basis_kernel(parts, scale, gram_ref, sel_ref, *refs):
    *pieces, out_ref, triangle_ref, spread_ref = refs
    count = gram_ref.shape[0]
    _, _, rows, columns = pieces[0].shape

    @pl.when(pl.program_id(0) == 0)
    def _():
        row = lax.broadcasted_iota(jnp.int32, (count, count), 0)
        column = lax.broadcasted_iota(jnp.int32, (count, count), 1)
        left = gram_ref[...]
        unit = jnp.where(row == column, 1.0, 0.0)
        for i in range(count):
            pivot = jnp.sqrt(left[i : i + 1, i : i + 1])
            upper = left[i : i + 1, :] / pivot
            solved = unit[i : i + 1, :] / pivot
            below = left[:, i : i + 1] / pivot
            is_row = row == i
            left = jnp.where(is_row, upper, jnp.where(row > i, left - below * upper, left))
            unit = jnp.where(is_row, solved, jnp.where(row > i, unit - below * solved, unit))
        triangle_ref[...] = jnp.where(column >= row, left, 0.0) / scale
        weights = exact(unit, sel_ref[...]) * scale
        for i in range(count):
            for c in range(count):
                spread_ref[i * count + c] = jnp.broadcast_to(
                    weights[i : i + 1, c : c + 1], (8, LANE)
                )

    def piece(c, at, columns):
        ref, inner = piece_of(pieces, parts, c)
        return ref[inner, 0, at, columns]

    halves = [slice(column, column + LANE) for column in range(0, columns, LANE)]
    for r in range(0, rows, 8):
        at = slice(r, r + 8)
        values = [[piece(c, at, half) for half in halves] for c in range(count)]
        for i in range(count):
            totals = [None] * len(halves)
            for c in range(count):
                weight = spread_ref[i * count + c]
                for h in range(len(halves)):
                    term = weight * values[c][h]
                    totals[h] = term if totals[h] is None else totals[h] + term
            for h, half in enumerate(halves):
                out_ref[i, 0, at, half] = totals[h]


def halo(block):
    count = lax.axis_size("slab")
    forward = [(i, i + 1) for i in range(count - 1)]
    backward = [(target, source) for source, target in forward]
    return lax.ppermute(block, "slab", forward), lax.ppermute(block, "slab", backward)


def whole(shape):
    zeros = (0,) * len(shape)
    return pl.BlockSpec(tuple(shape), lambda *_: zeros)


def add_up(value):
    for axis in ("slab", "dirs"):
        size, stride = lax.axis_size(axis), 1
        while stride < size:
            value = value + lax.ppermute(value, axis, [(i, i ^ stride) for i in range(size)])
            stride *= 2
    return value


def shards(
    perturbations,
    background_now,
    background_prev,
    stiffness,
    buoyancy,
    absorb_mask,
    source_cells,
    source_amp,
    receiver_cells,
    column_order,
):
    shape = buoyancy.shape
    layers, rows, columns = shape
    sketch_count = perturbations.shape[0]
    each = sketch_count // GROUPS
    owners = lax.axis_size("dirs")
    me = lax.axis_index("dirs").astype(jnp.int32).reshape(1)
    f32 = jnp.float32
    field = jax.ShapeDtypeStruct(shape, f32)
    cells_here = layers * rows * columns
    b_low, b_high = halo(buoyancy)
    u_low, u_high = halo(background_now)

    def matrix(*size):
        return jax.ShapeDtypeStruct(size, jnp.bfloat16)

    copied = (stiffness, buoyancy, background_now, background_prev)
    matrices = (matrix(columns, columns), matrix(rows, 2 * rows), matrix(rows, 3 * rows))
    (
        counts, source_field, taper, mx, my2, my3, stiffness, b_mid, current, older
    ) = pl.pallas_call(
        functools.partial(place_kernel, len(copied)),
        out_shape=(field,) * 3 + matrices + (field,) * len(copied),
        compiler_params=params(),
        cost_estimate=pl.CostEstimate(
            flops=40 * cells_here, bytes_accessed=16 * cells_here, transcendentals=0
        ),
        name="place",
    )(
        receiver_cells.reshape(1, -1),
        source_cells.reshape(1, -1),
        source_amp.reshape(1, -1),
        absorb_mask,
        *copied,
    )

    buoy = (b_low, b_mid, b_high)
    fields = [current]
    laps = []
    dg = None
    for t in range(STEPS):
        first, last = t == 0, t == STEPS - 1
        if not first:
            u_low, u_high = halo(current)
        operands = [u_low, current, u_high, *buoy, stiffness]
        if not first:
            operands.append(dg)
        if not last:
            operands += [taper, source_field, older]
        operands += [mx, my3]
        slots = 3 if first else 2
        results = pl.pallas_call(
            functools.partial(background_kernel, source_weight(t), first, last),
            out_shape=(field,) * (1 + (not last) + first),
            scratch_shapes=[
                pltpu.VMEM((slots, layers, 3 * rows, columns), jnp.bfloat16),
                pltpu.VMEM((slots, layers, rows, columns), f32),
            ],
            compiler_params=params(),
            cost_estimate=pl.CostEstimate(
                flops=60 * cells_here, bytes_accessed=56 * cells_here, transcendentals=0
            ),
            name=f"background{t}",
        )(*operands)
        results = list(results)
        laps.append(results.pop(0))
        if not last:
            older, current = current, results.pop(0)
            fields.append(current)
        if first:
            dg = results.pop(0)

    def wave(mode, group, p, old, add, lap, extra=()):
        low, high = halo(p)
        one = pl.BlockSpec((None, *shape), lambda d: (d, 0, 0, 0))
        shifted = pl.BlockSpec((None, *shape), lambda d: (d + group * each, 0, 0, 0))
        same = whole(shape)
        operands, specs = [low, p, high], [one] * 3
        if old is not None:
            operands.append(old)
            specs.append(one)
        operands += [*buoy, dg, stiffness]
        specs += [same] * 5
        if mode != "image":
            operands += [taper, add, lap]
            specs += [same, shifted if mode in ("born", "turn") else one, same]
        if mode == "turn":
            operands.append(counts)
            specs.append(same)
        if mode == "fold":
            specs += [one] + [same] * 4
        if mode == "image":
            specs += [one, pl.BlockSpec(memory_space=pltpu.SMEM)] + [same] * 2
        operands += [*extra, mx, my2]
        specs += [whole(mx.shape), whole(my2.shape)]
        out_shape, out_spec = (jax.ShapeDtypeStruct((each, *shape), f32),), [one]
        if mode == "fold":
            out_shape, out_spec = out_shape * 2, out_spec * 2
            if group == 0:
                out_shape, out_spec = out_shape + (field,) * 2, out_spec + [same] * 2
        elif mode == "image":
            split = (layers, rows // owners, columns)
            out_shape = (jax.ShapeDtypeStruct((each, *split), f32),) * owners
            out_spec = [pl.BlockSpec((None, *split), lambda d: (d, 0, 0, 0))] * owners
        kernel, how = functools.partial(wave_kernel, mode, old is not None), {}
        if mode in WHOLE:
            picks = [
                None
                if not spec.block_shape or spec.block_shape[0] is not None
                else group * each if spec is shifted else 0
                for spec in [*specs, *out_spec]
            ]
            kernel = functools.partial(all_waves, mode, old is not None, picks, each)
            memory = [spec.memory_space or pltpu.VMEM for spec in specs]
            how["in_specs"] = [pl.BlockSpec(memory_space=space) for space in memory]
            how["out_specs"] = [pl.BlockSpec(memory_space=pltpu.VMEM)] * len(out_spec)
        else:
            how = {"grid": (each,), "in_specs": specs, "out_specs": out_spec}
        results = pl.pallas_call(
            kernel,
            **how,
            out_shape=out_shape,
            scratch_shapes=[
                pltpu.VMEM((2, layers, 2 * rows, columns), jnp.bfloat16),
                pltpu.VMEM((2, layers, rows, columns), f32),
            ],
            compiler_params=params(),
            cost_estimate=pl.CostEstimate(
                flops=60 * each * cells_here,
                bytes_accessed=28 * each * cells_here,
                transcendentals=0,
            ),
            name=mode,
        )(*operands)
        return results[0] if len(results) == 1 else results

    def after(value, earlier):
        return lax.optimization_barrier((value, earlier))[0]

    born = [[None] * GROUPS for _ in range(STEPS + 1)]
    for g in range(GROUPS):
        mine = perturbations[g * each : (g + 1) * each]
        born[1][g] = taper * (mine * laps[0])
    born[1][1] = after(born[1][1], fields[2])
    ahead = {(2, 1): fields[3], (3, 1): laps[3]}
    for t in (1, 2):
        for g in range(GROUPS):
            old = born[t - 1][g] if t > 1 else None
            new = wave("born", g, born[t][g], old, perturbations, laps[t])
            if (t + 1, g) in ahead:
                new = after(new, ahead[t + 1, g])
            born[t + 1][g] = new
    adjoint = [[None] * GROUPS for _ in range(STEPS + 1)]
    for g in range(GROUPS):
        adjoint[3][g] = wave("turn", g, born[3][g], born[2][g], perturbations, laps[3])
    for g in range(GROUPS):
        adjoint[2][g] = wave("adjoint", g, adjoint[3][g], None, born[3][g], counts)
    known = [None] * GROUPS
    for g in range(GROUPS):
        adjoint[1][g], known[g], *rest = wave(
            "fold", g, adjoint[2][g], adjoint[3][g], born[2][g], counts, (born[1][g], *laps)
        )
        if g == 0:
            weight, near = rest
    sketch = []
    for g in range(GROUPS):
        blocks = wave(
            "image", g, adjoint[1][g], None, None, None, (known[g], me, weight, near)
        )
        sketch.append(blocks[0])
        for s in range(1, owners):
            ring = [(i, (i + s) % owners) for i in range(owners)]
            sketch.append(lax.ppermute(blocks[s], "dirs", ring))

    total_dirs = owners * sketch_count
    local_rows = rows // owners
    square = (total_dirs, total_dirs)
    place = jnp.arange(total_dirs, dtype=jnp.int32)
    owner = (me[0] - place // sketch_count + owners) % owners
    local = owner * sketch_count + place % sketch_count
    selector = (column_order[:, None] == local[None, :]).astype(f32)
    gram = pl.pallas_call(
        functools.partial(gram_kernel, GROUPS),
        out_shape=jax.ShapeDtypeStruct(square, f32),
        scratch_shapes=[pltpu.VMEM((*square, LANE), f32)],
        compiler_params=params(),
        name="gram",
    )(selector, selector.T, *[s.reshape(each, layers * local_rows, columns) for s in sketch])
    gram = add_up(gram)
    grid_cells = layers * lax.axis_size("slab") * rows * columns
    part = (each, 1, local_rows, columns)
    basis, triangle = pl.pallas_call(
        functools.partial(basis_kernel, GROUPS, math.sqrt(grid_cells)),
        grid=(layers,),
        in_specs=[whole(square)] * 2
        + [pl.BlockSpec(part, lambda l: (0, l, 0, 0))] * len(sketch),
        out_specs=[
            pl.BlockSpec((total_dirs, 1, local_rows, columns), lambda l: (0, l, 0, 0)),
            whole(square),
        ],
        out_shape=(
            jax.ShapeDtypeStruct((total_dirs, layers, local_rows, columns), f32),
            jax.ShapeDtypeStruct(square, f32),
        ),
        scratch_shapes=[pltpu.VMEM((total_dirs * total_dirs, 8, LANE), f32)],
        compiler_params=params(),
        name="basis",
    )(gram, selector, *sketch)
    return basis, triangle


def solution(mesh):
    return jax.shard_map(
        shards,
        mesh=mesh,
        in_specs=(
            P("dirs", "slab", None, None),
            P("slab", None, None),
            P("slab", None, None),
            P("slab", None, None),
            P("slab", None, None),
            P("slab", None, None),
            P("slab"),
            P("slab"),
            P("slab"),
            P(),
        ),
        out_specs=(P(None, "slab", "dirs", None), P()),
        check_vma=False,
    )
```

```python
import functools
import math

import jax
import jax.numpy as jnp
from jax import lax
from jax.experimental import pallas as pl
from jax.experimental.pallas import tpu as pltpu
from jax.sharding import PartitionSpec as P

STEPS = 4
DAMPING = 0.3
TAPS = (8064.0, -1008.0, 128.0, -9.0)
CENTRE = 6.0 * sum(TAPS)
HALF = 0.5 / 5040.0
GROUPS = 2
VMEM = 22 * 1024 * 1024
LANE = 128


def band(shape, period):
    row = lax.broadcasted_iota(jnp.int32, shape, 0)
    column = lax.broadcasted_iota(jnp.int32, shape, 1) % period
    distance = jnp.abs(row - column)
    matrix = jnp.zeros(shape, jnp.float32)
    for k, tap in enumerate(TAPS, 1):
        matrix = jnp.where(distance == k, tap, matrix)
    return matrix.astype(jnp.bfloat16)


def source_weight(t):
    return (1.0 - 0.4 * t) * math.exp(-0.125 * t * t)


def params():
    return pltpu.CompilerParams(vmem_limit_bytes=VMEM)


def split_rows(y_ref, slot, layer, row, values, parts, rows):
    size = values.shape[0]
    for s in range(parts):
        part = values.astype(jnp.bfloat16)
        y_ref[slot, layer, s * rows + row : s * rows + row + size, :] = part
        if s < parts - 1:
            values = values - part.astype(jnp.float32)


def plane_part(functions, y_ref, a_ref, mx_ref, my_ref, parts):
    _, layers, rows, _ = a_ref.shape
    for layer in range(layers):
        for row in range(0, rows, 32):
            for slot, values in enumerate(functions(layer, row, 32)):
                split_rows(y_ref, slot, layer, row, values, parts, rows)
    for slot in range(a_ref.shape[0]):
        for layer in range(layers):
            y = y_ref[slot, layer]
            along = jnp.dot(y, mx_ref[...], preferred_element_type=jnp.float32)
            total = jnp.dot(my_ref[...], y, preferred_element_type=jnp.float32)
            for s in range(parts):
                total = total + along[s * rows : (s + 1) * rows]
            a_ref[slot, layer] = total


def depth_part(tall, layer):
    total = None
    for k, tap in enumerate(TAPS, 1):
        term = tap * (tall[layer + 4 + k] + tall[layer + 4 - k])
        total = term if total is None else total + term
    return total


def tall_of(refs, rows, columns):
    low, mid, high = refs
    return [ref[layer, rows, columns] for ref in (low, mid, high) for layer in range(4)]


def tiles(rows, columns, body, start=0):
    def step(i, carry):
        at = pl.ds(pl.multiple_of(start + i * 8, 8), 8)
        for column in range(0, columns, LANE):
            body(i, at, slice(column, column + LANE))
        return carry

    lax.fori_loop(0, rows // 8, step, 0, unroll=2)


def place_kernel(copies, rc_ref, sc_ref, amp_ref, mask_ref, *refs):
    sources, refs = refs[:copies], refs[copies:]
    m_ref, src_ref, taper_ref, mx_ref, my2_ref, my3_ref = refs[:6]
    for source, target in zip(sources, refs[6:]):
        target[...] = source[...]
    layers, rows, columns = m_ref.shape
    for matrix in (mx_ref, my2_ref, my3_ref):
        matrix[...] = band(matrix.shape, matrix.shape[0])
    count = rc_ref.shape[1]
    lines = layers * rows
    chunk = min(256, count)
    total = None
    for start in range(0, count, chunk):
        cells = rc_ref[:, start : start + chunk]
        line = lax.broadcasted_iota(jnp.int32, (lines, chunk), 0) == cells // columns
        column = lax.broadcasted_iota(jnp.int32, (columns, chunk), 0) == cells % columns
        part = lax.dot_general(
            jnp.where(line, 1.0, 0.0).astype(jnp.bfloat16),
            jnp.where(column, 1.0, 0.0).astype(jnp.bfloat16),
            (((1,), (1,)), ((), ())),
            preferred_element_type=jnp.float32,
        )
        total = part if total is None else total + part
    m_ref[...] = total.reshape(m_ref.shape)
    cells = sc_ref[...]
    count = cells.shape[1]
    line = lax.broadcasted_iota(jnp.int32, (lines, count), 0) == cells // columns
    column = lax.broadcasted_iota(jnp.int32, (columns, count), 0) == cells % columns
    part = lax.dot_general(
        jnp.where(line, 1.0, 0.0),
        jnp.where(column, amp_ref[...], 0.0),
        (((1,), (1,)), ((), ())),
        precision=lax.Precision.HIGHEST,
        preferred_element_type=jnp.float32,
    )
    src_ref[...] = part.reshape(src_ref.shape)
    taper_ref[...] = 1.0 - DAMPING * mask_ref[...].astype(jnp.float32)


def background_kernel(weight, first, last, *refs):
    refs = list(refs)
    u = [refs.pop(0) for _ in range(3)]
    b = [refs.pop(0) for _ in range(3)]
    stiff_ref = refs.pop(0)
    dg_ref = None if first else refs.pop(0)
    taper_ref = src_ref = older_ref = new_ref = None
    if not last:
        taper_ref, src_ref, older_ref = (refs.pop(0) for _ in range(3))
    mx_ref, my_ref = refs.pop(0), refs.pop(0)
    lap_ref = refs.pop(0)
    if not last:
        new_ref = refs.pop(0)
    if first:
        dg_ref = refs.pop(0)
    y_ref, a_ref = refs

    def functions(layer, row, size):
        value = u[1][layer, row : row + size]
        buoy = b[1][layer, row : row + size]
        return [value, value * buoy] + ([buoy] if first else [])

    plane_part(functions, y_ref, a_ref, mx_ref, my_ref, 3)

    def body(i, at, columns):
        value = tall_of(u, at, columns)
        buoy = tall_of(b, at, columns)
        both = [x * y for x, y in zip(value, buoy)]
        for layer in range(4):
            here, b_here = value[layer + 4], buoy[layer + 4]
            if first:
                dg = depth_part(buoy, layer) + a_ref[2, layer, at, columns] + CENTRE * b_here
                dg_ref[layer, at, columns] = dg
            else:
                dg = dg_ref[layer, at, columns]
            plain = depth_part(value, layer) + a_ref[0, layer, at, columns]
            times = depth_part(both, layer) + a_ref[1, layer, at, columns]
            lap = HALF * (b_here * plain + times - here * dg)
            lap_ref[layer, at, columns] = lap
            if not last:
                new_ref[layer, at, columns] = (
                    taper_ref[layer, at, columns]
                    * (
                        2.0 * here
                        - older_ref[layer, at, columns]
                        + stiff_ref[layer, at, columns] * lap
                    )
                    + weight * src_ref[layer, at, columns]
                )

    tiles(*lap_ref.shape[1:], body)


def wave_kernel(mode, has_old, *refs):
    refs = list(refs)
    p = [refs.pop(0) for _ in range(3)]
    old_ref = refs.pop(0) if has_old else None
    b = [refs.pop(0) for _ in range(3)]
    dg_ref, stiff_ref = refs.pop(0), refs.pop(0)
    if mode == "image":
        sum_ref, me_ref, weight_ref, near_ref = (refs.pop(0) for _ in range(4))
    else:
        taper_ref, add_ref, lap_ref = (refs.pop(0) for _ in range(3))
    count_ref = refs.pop(0) if mode == "turn" else None
    if mode == "fold":
        first_ref = refs.pop(0)
        laps = [refs.pop(0) for _ in range(4)]
    mx_ref, my_ref = refs.pop(0), refs.pop(0)
    y_ref, a_ref = refs[-2:]
    outs = refs[:-2]

    def functions(layer, row, size):
        value = p[1][layer, row : row + size]
        return value, value * b[1][layer, row : row + size]

    plane_part(functions, y_ref, a_ref, mx_ref, my_ref, 2)

    def body(block, i, at, columns):
        value = tall_of(p, at, columns)
        buoy = tall_of(b, at, columns)
        both = [x * y for x, y in zip(value, buoy)]
        for layer in range(4):
            here = value[layer + 4]
            spot = (layer, at, columns)
            plain = depth_part(value, layer) + a_ref[0, layer, at, columns]
            times = depth_part(both, layer) + a_ref[1, layer, at, columns]
            lb = buoy[layer + 4] * plain + times - here * dg_ref[spot]
            total = 2.0 * here + (HALF * stiff_ref[spot]) * lb
            if mode == "image":
                inner = pl.ds(pl.multiple_of(i * 8, 8), 8)
                outs[block][layer, inner, columns] = (
                    sum_ref[spot] + near_ref[spot] * here + weight_ref[spot] * total
                )
                continue
            if has_old:
                old = old_ref[spot]
                total = total - old
            taper = taper_ref[spot]
            added = add_ref[spot] * lap_ref[spot]
            if mode in ("born", "turn"):
                new = taper * (total + added)
            else:
                new = taper * total + added
            if mode == "turn":
                new = count_ref[spot] * new
            outs[0][spot] = new
            if mode == "fold":
                weight = laps[0][spot] * taper
                known = laps[3][spot] * old + laps[2][spot] * here
                known = known + laps[0][spot] * (lap_ref[spot] * first_ref[spot])
                outs[1][spot] = known - weight * here
                if len(outs) > 2:
                    outs[2][spot] = weight
                    outs[3][spot] = laps[1][spot]

    _, rows, columns = p[1].shape
    if mode == "image":
        per = rows // len(outs)
        for block in range(len(outs)):
            owner = lax.rem(me_ref[0] + block, len(outs))
            tiles(per, columns, functools.partial(body, block), owner * per)
    else:
        tiles(rows, columns, functools.partial(body, 0))


def piece_of(pieces, parts, c):
    each = pieces[0].shape[0]
    block, rest = divmod(c, parts * each)
    group, inner = divmod(rest, each)
    return pieces[group * (len(pieces) // parts) + block], inner


def gram_kernel(parts, sel_ref, selt_ref, *refs):
    *pieces, out_ref, lanes_ref = refs
    count = sel_ref.shape[0]
    _, rows, columns = pieces[0].shape

    def piece(c, at, column):
        ref, inner = piece_of(pieces, parts, c)
        return ref[inner, at, column : column + LANE]

    for i0 in range(0, count, 4):
        for j0 in range(i0 // 8 * 8, count, 8):

            def step(r, accs, i0=i0, j0=j0):
                at = pl.ds(pl.multiple_of(r * 8, 8), 8)
                accs = list(accs)
                for column in range(0, columns, LANE):
                    left = [piece(i0 + i, at, column) for i in range(4)]
                    for j in range(8):
                        right = piece(j0 + j, at, column)
                        for i in range(4):
                            accs[i * 8 + j] = accs[i * 8 + j] + left[i] * right
                return tuple(accs)

            zero = jnp.zeros((8, LANE), jnp.float32)
            accs = lax.fori_loop(0, rows // 8, step, (zero,) * 32)
            for i in range(4):
                for j in range(8):
                    lanes_ref[i0 + i, j0 + j : j0 + j + 1, :] = jnp.sum(
                        accs[i * 8 + j], axis=0, keepdims=True
                    )
    local = jnp.sum(lanes_ref[...], axis=-1)
    row = lax.broadcasted_iota(jnp.int32, local.shape, 0)
    column = lax.broadcasted_iota(jnp.int32, local.shape, 1)
    local = jnp.where(row // 8 > column // 8, local.T, local)
    out_ref[...] = exact(exact(sel_ref[...], local), selt_ref[...])


def exact(left, right):
    return jnp.dot(left, right, precision=lax.Precision.HIGHEST, preferred_element_type=jnp.float32)


def basis_kernel(parts, scale, gram_ref, sel_ref, *refs):
    *pieces, out_ref, triangle_ref, spread_ref = refs
    count = gram_ref.shape[0]
    _, _, rows, columns = pieces[0].shape

    @pl.when(pl.program_id(0) == 0)
    def _():
        row = lax.broadcasted_iota(jnp.int32, (count, count), 0)
        column = lax.broadcasted_iota(jnp.int32, (count, count), 1)
        left = gram_ref[...]
        unit = jnp.where(row == column, 1.0, 0.0)
        for i in range(count):
            pivot = jnp.sqrt(left[i : i + 1, i : i + 1])
            upper = left[i : i + 1, :] / pivot
            solved = unit[i : i + 1, :] / pivot
            below = left[:, i : i + 1] / pivot
            is_row = row == i
            left = jnp.where(is_row, upper, jnp.where(row > i, left - below * upper, left))
            unit = jnp.where(is_row, solved, jnp.where(row > i, unit - below * solved, unit))
        triangle_ref[...] = jnp.where(column >= row, left, 0.0) / scale
        weights = exact(unit, sel_ref[...]) * scale
        for i in range(count):
            for c in range(count):
                spread_ref[i * count + c] = jnp.broadcast_to(
                    weights[i : i + 1, c : c + 1], (8, LANE)
                )

    def piece(c, at, columns):
        ref, inner = piece_of(pieces, parts, c)
        return ref[inner, 0, at, columns]

    halves = [slice(column, column + LANE) for column in range(0, columns, LANE)]
    for r in range(0, rows, 8):
        at = slice(r, r + 8)
        values = [[piece(c, at, half) for half in halves] for c in range(count)]
        for i in range(count):
            totals = [None] * len(halves)
            for c in range(count):
                weight = spread_ref[i * count + c]
                for h in range(len(halves)):
                    term = weight * values[c][h]
                    totals[h] = term if totals[h] is None else totals[h] + term
            for h, half in enumerate(halves):
                out_ref[i, 0, at, half] = totals[h]


def halo(block):
    count = lax.axis_size("slab")
    forward = [(i, i + 1) for i in range(count - 1)]
    backward = [(target, source) for source, target in forward]
    return lax.ppermute(block, "slab", forward), lax.ppermute(block, "slab", backward)


def whole(shape):
    zeros = (0,) * len(shape)
    return pl.BlockSpec(tuple(shape), lambda *_: zeros)


def add_up(value):
    for axis in ("slab", "dirs"):
        size, stride = lax.axis_size(axis), 1
        while stride < size:
            value = value + lax.ppermute(value, axis, [(i, i ^ stride) for i in range(size)])
            stride *= 2
    return value


def shards(
    perturbations,
    background_now,
    background_prev,
    stiffness,
    buoyancy,
    absorb_mask,
    source_cells,
    source_amp,
    receiver_cells,
    column_order,
):
    shape = buoyancy.shape
    layers, rows, columns = shape
    sketch_count = perturbations.shape[0]
    each = sketch_count // GROUPS
    owners = lax.axis_size("dirs")
    me = lax.axis_index("dirs").astype(jnp.int32).reshape(1)
    f32 = jnp.float32
    field = jax.ShapeDtypeStruct(shape, f32)
    cells_here = layers * rows * columns
    b_low, b_high = halo(buoyancy)
    u_low, u_high = halo(background_now)

    def matrix(*size):
        return jax.ShapeDtypeStruct(size, jnp.bfloat16)

    copied = (stiffness, buoyancy, background_now, background_prev)
    matrices = (matrix(columns, columns), matrix(rows, 2 * rows), matrix(rows, 3 * rows))
    (
        counts, source_field, taper, mx, my2, my3, stiffness, b_mid, current, older
    ) = pl.pallas_call(
        functools.partial(place_kernel, len(copied)),
        out_shape=(field,) * 3 + matrices + (field,) * len(copied),
        compiler_params=params(),
        cost_estimate=pl.CostEstimate(
            flops=40 * cells_here, bytes_accessed=16 * cells_here, transcendentals=0
        ),
        name="place",
    )(
        receiver_cells.reshape(1, -1),
        source_cells.reshape(1, -1),
        source_amp.reshape(1, -1),
        absorb_mask,
        *copied,
    )

    buoy = (b_low, b_mid, b_high)
    fields = [current]
    laps = []
    dg = None
    for t in range(STEPS):
        first, last = t == 0, t == STEPS - 1
        if not first:
            u_low, u_high = halo(current)
        operands = [u_low, current, u_high, *buoy, stiffness]
        if not first:
            operands.append(dg)
        if not last:
            operands += [taper, source_field, older]
        operands += [mx, my3]
        slots = 3 if first else 2
        results = pl.pallas_call(
            functools.partial(background_kernel, source_weight(t), first, last),
            out_shape=(field,) * (1 + (not last) + first),
            scratch_shapes=[
                pltpu.VMEM((slots, layers, 3 * rows, columns), jnp.bfloat16),
                pltpu.VMEM((slots, layers, rows, columns), f32),
            ],
            compiler_params=params(),
            cost_estimate=pl.CostEstimate(
                flops=60 * cells_here, bytes_accessed=56 * cells_here, transcendentals=0
            ),
            name=f"background{t}",
        )(*operands)
        results = list(results)
        laps.append(results.pop(0))
        if not last:
            older, current = current, results.pop(0)
            fields.append(current)
        if first:
            dg = results.pop(0)

    def wave(mode, group, p, old, add, lap, extra=()):
        low, high = halo(p)
        one = pl.BlockSpec((None, *shape), lambda d: (d, 0, 0, 0))
        shifted = pl.BlockSpec((None, *shape), lambda d: (d + group * each, 0, 0, 0))
        same = whole(shape)
        operands, specs = [low, p, high], [one] * 3
        if old is not None:
            operands.append(old)
            specs.append(one)
        operands += [*buoy, dg, stiffness]
        specs += [same] * 5
        if mode != "image":
            operands += [taper, add, lap]
            specs += [same, shifted if mode in ("born", "turn") else one, same]
        if mode == "turn":
            operands.append(counts)
            specs.append(same)
        if mode == "fold":
            specs += [one] + [same] * 4
        if mode == "image":
            specs += [one, pl.BlockSpec(memory_space=pltpu.SMEM)] + [same] * 2
        operands += [*extra, mx, my2]
        specs += [whole(mx.shape), whole(my2.shape)]
        out_shape, out_spec = (jax.ShapeDtypeStruct((each, *shape), f32),), [one]
        if mode == "fold":
            out_shape, out_spec = out_shape * 2, out_spec * 2
            if group == 0:
                out_shape, out_spec = out_shape + (field,) * 2, out_spec + [same] * 2
        elif mode == "image":
            split = (layers, rows // owners, columns)
            out_shape = (jax.ShapeDtypeStruct((each, *split), f32),) * owners
            out_spec = [pl.BlockSpec((None, *split), lambda d: (d, 0, 0, 0))] * owners
        results = pl.pallas_call(
            functools.partial(wave_kernel, mode, old is not None),
            grid=(each,),
            in_specs=specs,
            out_specs=out_spec,
            out_shape=out_shape,
            scratch_shapes=[
                pltpu.VMEM((2, layers, 2 * rows, columns), jnp.bfloat16),
                pltpu.VMEM((2, layers, rows, columns), f32),
            ],
            compiler_params=params(),
            cost_estimate=pl.CostEstimate(
                flops=60 * each * cells_here,
                bytes_accessed=28 * each * cells_here,
                transcendentals=0,
            ),
            name=mode,
        )(*operands)
        return results[0] if len(results) == 1 else results

    def after(value, earlier):
        return lax.optimization_barrier((value, earlier))[0]

    born = [[None] * GROUPS for _ in range(STEPS + 1)]
    for g in range(GROUPS):
        mine = perturbations[g * each : (g + 1) * each]
        born[1][g] = taper * (mine * laps[0])
    born[1][1] = after(born[1][1], fields[2])
    ahead = {(2, 1): fields[3], (3, 1): laps[3]}
    for t in (1, 2):
        for g in range(GROUPS):
            old = born[t - 1][g] if t > 1 else None
            new = wave("born", g, born[t][g], old, perturbations, laps[t])
            if (t + 1, g) in ahead:
                new = after(new, ahead[t + 1, g])
            born[t + 1][g] = new
    adjoint = [[None] * GROUPS for _ in range(STEPS + 1)]
    for g in range(GROUPS):
        adjoint[3][g] = wave("turn", g, born[3][g], born[2][g], perturbations, laps[3])
    for g in range(GROUPS):
        adjoint[2][g] = wave("adjoint", g, adjoint[3][g], None, born[3][g], counts)
    known = [None] * GROUPS
    for g in range(GROUPS):
        adjoint[1][g], known[g], *rest = wave(
            "fold", g, adjoint[2][g], adjoint[3][g], born[2][g], counts, (born[1][g], *laps)
        )
        if g == 0:
            weight, near = rest
    sketch = []
    for g in range(GROUPS):
        blocks = wave(
            "image", g, adjoint[1][g], None, None, None, (known[g], me, weight, near)
        )
        sketch.append(blocks[0])
        for s in range(1, owners):
            ring = [(i, (i + s) % owners) for i in range(owners)]
            sketch.append(lax.ppermute(blocks[s], "dirs", ring))

    total_dirs = owners * sketch_count
    local_rows = rows // owners
    square = (total_dirs, total_dirs)
    place = jnp.arange(total_dirs, dtype=jnp.int32)
    owner = (me[0] - place // sketch_count + owners) % owners
    local = owner * sketch_count + place % sketch_count
    selector = (column_order[:, None] == local[None, :]).astype(f32)
    gram = pl.pallas_call(
        functools.partial(gram_kernel, GROUPS),
        out_shape=jax.ShapeDtypeStruct(square, f32),
        scratch_shapes=[pltpu.VMEM((*square, LANE), f32)],
        compiler_params=params(),
        name="gram",
    )(selector, selector.T, *[s.reshape(each, layers * local_rows, columns) for s in sketch])
    gram = add_up(gram)
    grid_cells = layers * lax.axis_size("slab") * rows * columns
    part = (each, 1, local_rows, columns)
    basis, triangle = pl.pallas_call(
        functools.partial(basis_kernel, GROUPS, math.sqrt(grid_cells)),
        grid=(layers,),
        in_specs=[whole(square)] * 2
        + [pl.BlockSpec(part, lambda l: (0, l, 0, 0))] * len(sketch),
        out_specs=[
            pl.BlockSpec((total_dirs, 1, local_rows, columns), lambda l: (0, l, 0, 0)),
            whole(square),
        ],
        out_shape=(
            jax.ShapeDtypeStruct((total_dirs, layers, local_rows, columns), f32),
            jax.ShapeDtypeStruct(square, f32),
        ),
        scratch_shapes=[pltpu.VMEM((total_dirs * total_dirs, 8, LANE), f32)],
        compiler_params=params(),
        name="basis",
    )(gram, selector, *sketch)
    return basis, triangle


def solution(mesh):
    return jax.shard_map(
        shards,
        mesh=mesh,
        in_specs=(
            P("dirs", "slab", None, None),
            P("slab", None, None),
            P("slab", None, None),
            P("slab", None, None),
            P("slab", None, None),
            P("slab", None, None),
            P("slab"),
            P("slab"),
            P("slab"),
            P(),
        ),
        out_specs=(P(None, "slab", "dirs", None), P()),
        check_vma=False,
    )
```

```python
import functools
import math

import jax
import jax.numpy as jnp
from jax import lax
from jax.experimental import pallas as pl
from jax.experimental.pallas import tpu as pltpu
from jax.sharding import PartitionSpec as P

STEPS = 4
DAMPING = 0.3
TAPS = (8064.0, -1008.0, 128.0, -9.0)
CENTRE = 6.0 * sum(TAPS)
HALF = 0.5 / 5040.0
GROUPS = 2
VMEM = 22 * 1024 * 1024
LANE = 128


def band(shape, period):
    row = lax.broadcasted_iota(jnp.int32, shape, 0)
    column = lax.broadcasted_iota(jnp.int32, shape, 1) % period
    distance = jnp.abs(row - column)
    matrix = jnp.zeros(shape, jnp.float32)
    for k, tap in enumerate(TAPS, 1):
        matrix = jnp.where(distance == k, tap, matrix)
    return matrix.astype(jnp.bfloat16)


def source_weight(t):
    return (1.0 - 0.4 * t) * math.exp(-0.125 * t * t)


def params():
    return pltpu.CompilerParams(vmem_limit_bytes=VMEM)


def split_rows(y_ref, slot, layer, row, values, parts, rows):
    size = values.shape[0]
    for s in range(parts):
        part = values.astype(jnp.bfloat16)
        y_ref[slot, layer, s * rows + row : s * rows + row + size, :] = part
        if s < parts - 1:
            values = values - part.astype(jnp.float32)


def plane_part(functions, y_ref, a_ref, mx_ref, my_ref, parts):
    _, layers, rows, _ = a_ref.shape
    for layer in range(layers):
        for row in range(0, rows, 32):
            for slot, values in enumerate(functions(layer, row, 32)):
                split_rows(y_ref, slot, layer, row, values, parts, rows)
    for slot in range(a_ref.shape[0]):
        for layer in range(layers):
            y = y_ref[slot, layer]
            along = jnp.dot(y, mx_ref[...], preferred_element_type=jnp.float32)
            total = jnp.dot(my_ref[...], y, preferred_element_type=jnp.float32)
            for s in range(parts):
                total = total + along[s * rows : (s + 1) * rows]
            a_ref[slot, layer] = total


def depth_part(tall, layer):
    total = None
    for k, tap in enumerate(TAPS, 1):
        term = tap * (tall[layer + 4 + k] + tall[layer + 4 - k])
        total = term if total is None else total + term
    return total


def tall_of(refs, rows, columns):
    low, mid, high = refs
    return [ref[layer, rows, columns] for ref in (low, mid, high) for layer in range(4)]


def tiles(rows, columns, body, start=0):
    def step(i, carry):
        at = pl.ds(pl.multiple_of(start + i * 8, 8), 8)
        for column in range(0, columns, LANE):
            body(i, at, slice(column, column + LANE))
        return carry

    lax.fori_loop(0, rows // 8, step, 0, unroll=4)


def place_kernel(copies, rc_ref, sc_ref, amp_ref, mask_ref, *refs):
    sources, refs = refs[:copies], refs[copies:]
    m_ref, src_ref, taper_ref, mx_ref, my2_ref, my3_ref = refs[:6]
    for source, target in zip(sources, refs[6:]):
        target[...] = source[...]
    layers, rows, columns = m_ref.shape
    for matrix in (mx_ref, my2_ref, my3_ref):
        matrix[...] = band(matrix.shape, matrix.shape[0])
    count = rc_ref.shape[1]
    lines = layers * rows
    chunk = min(256, count)
    total = None
    for start in range(0, count, chunk):
        cells = rc_ref[:, start : start + chunk]
        line = lax.broadcasted_iota(jnp.int32, (lines, chunk), 0) == cells // columns
        column = lax.broadcasted_iota(jnp.int32, (columns, chunk), 0) == cells % columns
        part = lax.dot_general(
            jnp.where(line, 1.0, 0.0).astype(jnp.bfloat16),
            jnp.where(column, 1.0, 0.0).astype(jnp.bfloat16),
            (((1,), (1,)), ((), ())),
            preferred_element_type=jnp.float32,
        )
        total = part if total is None else total + part
    m_ref[...] = total.reshape(m_ref.shape)
    cells = sc_ref[...]
    count = cells.shape[1]
    line = lax.broadcasted_iota(jnp.int32, (lines, count), 0) == cells // columns
    column = lax.broadcasted_iota(jnp.int32, (columns, count), 0) == cells % columns
    part = lax.dot_general(
        jnp.where(line, 1.0, 0.0),
        jnp.where(column, amp_ref[...], 0.0),
        (((1,), (1,)), ((), ())),
        precision=lax.Precision.HIGHEST,
        preferred_element_type=jnp.float32,
    )
    src_ref[...] = part.reshape(src_ref.shape)
    taper_ref[...] = 1.0 - DAMPING * mask_ref[...].astype(jnp.float32)


def background_kernel(weight, first, last, *refs):
    refs = list(refs)
    u = [refs.pop(0) for _ in range(3)]
    b = [refs.pop(0) for _ in range(3)]
    stiff_ref = refs.pop(0)
    dg_ref = None if first else refs.pop(0)
    taper_ref = src_ref = older_ref = new_ref = None
    if not last:
        taper_ref, src_ref, older_ref = (refs.pop(0) for _ in range(3))
    mx_ref, my_ref = refs.pop(0), refs.pop(0)
    lap_ref = refs.pop(0)
    if not last:
        new_ref = refs.pop(0)
    if first:
        dg_ref = refs.pop(0)
    y_ref, a_ref = refs

    def functions(layer, row, size):
        value = u[1][layer, row : row + size]
        buoy = b[1][layer, row : row + size]
        return [value, value * buoy] + ([buoy] if first else [])

    plane_part(functions, y_ref, a_ref, mx_ref, my_ref, 3)

    def body(i, at, columns):
        value = tall_of(u, at, columns)
        buoy = tall_of(b, at, columns)
        both = [x * y for x, y in zip(value, buoy)]
        for layer in range(4):
            here, b_here = value[layer + 4], buoy[layer + 4]
            if first:
                dg = depth_part(buoy, layer) + a_ref[2, layer, at, columns] + CENTRE * b_here
                dg_ref[layer, at, columns] = dg
            else:
                dg = dg_ref[layer, at, columns]
            plain = depth_part(value, layer) + a_ref[0, layer, at, columns]
            times = depth_part(both, layer) + a_ref[1, layer, at, columns]
            lap = HALF * (b_here * plain + times - here * dg)
            lap_ref[layer, at, columns] = lap
            if not last:
                new_ref[layer, at, columns] = (
                    taper_ref[layer, at, columns]
                    * (
                        2.0 * here
                        - older_ref[layer, at, columns]
                        + stiff_ref[layer, at, columns] * lap
                    )
                    + weight * src_ref[layer, at, columns]
                )

    tiles(*lap_ref.shape[1:], body)


def wave_kernel(mode, has_old, *refs):
    refs = list(refs)
    p = [refs.pop(0) for _ in range(3)]
    old_ref = refs.pop(0) if has_old else None
    b = [refs.pop(0) for _ in range(3)]
    dg_ref, stiff_ref = refs.pop(0), refs.pop(0)
    if mode == "image":
        sum_ref, me_ref, weight_ref, near_ref = (refs.pop(0) for _ in range(4))
    else:
        taper_ref, add_ref, lap_ref = (refs.pop(0) for _ in range(3))
    count_ref = refs.pop(0) if mode == "turn" else None
    if mode == "fold":
        first_ref = refs.pop(0)
        laps = [refs.pop(0) for _ in range(4)]
    mx_ref, my_ref = refs.pop(0), refs.pop(0)
    y_ref, a_ref = refs[-2:]
    outs = refs[:-2]

    def functions(layer, row, size):
        value = p[1][layer, row : row + size]
        return value, value * b[1][layer, row : row + size]

    plane_part(functions, y_ref, a_ref, mx_ref, my_ref, 2)

    def body(block, i, at, columns):
        value = tall_of(p, at, columns)
        buoy = tall_of(b, at, columns)
        both = [x * y for x, y in zip(value, buoy)]
        for layer in range(4):
            here = value[layer + 4]
            spot = (layer, at, columns)
            plain = depth_part(value, layer) + a_ref[0, layer, at, columns]
            times = depth_part(both, layer) + a_ref[1, layer, at, columns]
            lb = buoy[layer + 4] * plain + times - here * dg_ref[spot]
            total = 2.0 * here + (HALF * stiff_ref[spot]) * lb
            if mode == "image":
                inner = pl.ds(pl.multiple_of(i * 8, 8), 8)
                outs[block][layer, inner, columns] = (
                    sum_ref[spot] + near_ref[spot] * here + weight_ref[spot] * total
                )
                continue
            if has_old:
                old = old_ref[spot]
                total = total - old
            taper = taper_ref[spot]
            added = add_ref[spot] * lap_ref[spot]
            if mode in ("born", "turn"):
                new = taper * (total + added)
            else:
                new = taper * total + added
            if mode == "turn":
                new = count_ref[spot] * new
            outs[0][spot] = new
            if mode == "fold":
                weight = laps[0][spot] * taper
                known = laps[3][spot] * old + laps[2][spot] * here
                known = known + laps[0][spot] * (lap_ref[spot] * first_ref[spot])
                outs[1][spot] = known - weight * here
                if len(outs) > 2:
                    outs[2][spot] = weight
                    outs[3][spot] = laps[1][spot]

    _, rows, columns = p[1].shape
    if mode == "image":
        per = rows // len(outs)
        for block in range(len(outs)):
            owner = lax.rem(me_ref[0] + block, len(outs))
            tiles(per, columns, functools.partial(body, block), owner * per)
    else:
        tiles(rows, columns, functools.partial(body, 0))


def piece_of(pieces, parts, c):
    each = pieces[0].shape[0]
    block, rest = divmod(c, parts * each)
    group, inner = divmod(rest, each)
    return pieces[group * (len(pieces) // parts) + block], inner


def gram_kernel(parts, sel_ref, selt_ref, *refs):
    *pieces, out_ref, lanes_ref = refs
    count = sel_ref.shape[0]
    _, rows, columns = pieces[0].shape

    def piece(c, at, column):
        ref, inner = piece_of(pieces, parts, c)
        return ref[inner, at, column : column + LANE]

    for i0 in range(0, count, 4):
        for j0 in range(i0 // 8 * 8, count, 8):

            def step(r, accs, i0=i0, j0=j0):
                at = pl.ds(pl.multiple_of(r * 8, 8), 8)
                accs = list(accs)
                for column in range(0, columns, LANE):
                    left = [piece(i0 + i, at, column) for i in range(4)]
                    for j in range(8):
                        right = piece(j0 + j, at, column)
                        for i in range(4):
                            accs[i * 8 + j] = accs[i * 8 + j] + left[i] * right
                return tuple(accs)

            zero = jnp.zeros((8, LANE), jnp.float32)
            accs = lax.fori_loop(0, rows // 8, step, (zero,) * 32)
            for i in range(4):
                for j in range(8):
                    lanes_ref[i0 + i, j0 + j : j0 + j + 1, :] = jnp.sum(
                        accs[i * 8 + j], axis=0, keepdims=True
                    )
    local = jnp.sum(lanes_ref[...], axis=-1)
    row = lax.broadcasted_iota(jnp.int32, local.shape, 0)
    column = lax.broadcasted_iota(jnp.int32, local.shape, 1)
    local = jnp.where(row // 8 > column // 8, local.T, local)
    out_ref[...] = exact(exact(sel_ref[...], local), selt_ref[...])


def exact(left, right):
    return jnp.dot(left, right, precision=lax.Precision.HIGHEST, preferred_element_type=jnp.float32)


def basis_kernel(parts, scale, gram_ref, sel_ref, *refs):
    *pieces, out_ref, triangle_ref, spread_ref = refs
    count = gram_ref.shape[0]
    _, _, rows, columns = pieces[0].shape

    @pl.when(pl.program_id(0) == 0)
    def _():
        row = lax.broadcasted_iota(jnp.int32, (count, count), 0)
        column = lax.broadcasted_iota(jnp.int32, (count, count), 1)
        left = gram_ref[...]
        unit = jnp.where(row == column, 1.0, 0.0)
        for i in range(count):
            pivot = jnp.sqrt(left[i : i + 1, i : i + 1])
            upper = left[i : i + 1, :] / pivot
            solved = unit[i : i + 1, :] / pivot
            below = left[:, i : i + 1] / pivot
            is_row = row == i
            left = jnp.where(is_row, upper, jnp.where(row > i, left - below * upper, left))
            unit = jnp.where(is_row, solved, jnp.where(row > i, unit - below * solved, unit))
        triangle_ref[...] = jnp.where(column >= row, left, 0.0) / scale
        weights = exact(unit, sel_ref[...]) * scale
        for i in range(count):
            for c in range(count):
                spread_ref[i * count + c] = jnp.broadcast_to(
                    weights[i : i + 1, c : c + 1], (8, LANE)
                )

    def piece(c, at, columns):
        ref, inner = piece_of(pieces, parts, c)
        return ref[inner, 0, at, columns]

    halves = [slice(column, column + LANE) for column in range(0, columns, LANE)]
    for r in range(0, rows, 8):
        at = slice(r, r + 8)
        values = [[piece(c, at, half) for half in halves] for c in range(count)]
        for i in range(count):
            totals = [None] * len(halves)
            for c in range(count):
                weight = spread_ref[i * count + c]
                for h in range(len(halves)):
                    term = weight * values[c][h]
                    totals[h] = term if totals[h] is None else totals[h] + term
            for h, half in enumerate(halves):
                out_ref[i, 0, at, half] = totals[h]


def halo(block):
    count = lax.axis_size("slab")
    forward = [(i, i + 1) for i in range(count - 1)]
    backward = [(target, source) for source, target in forward]
    return lax.ppermute(block, "slab", forward), lax.ppermute(block, "slab", backward)


def whole(shape):
    zeros = (0,) * len(shape)
    return pl.BlockSpec(tuple(shape), lambda *_: zeros)


def add_up(value):
    for axis in ("slab", "dirs"):
        size, stride = lax.axis_size(axis), 1
        while stride < size:
            value = value + lax.ppermute(value, axis, [(i, i ^ stride) for i in range(size)])
            stride *= 2
    return value


def shards(
    perturbations,
    background_now,
    background_prev,
    stiffness,
    buoyancy,
    absorb_mask,
    source_cells,
    source_amp,
    receiver_cells,
    column_order,
):
    shape = buoyancy.shape
    layers, rows, columns = shape
    sketch_count = perturbations.shape[0]
    each = sketch_count // GROUPS
    owners = lax.axis_size("dirs")
    me = lax.axis_index("dirs").astype(jnp.int32).reshape(1)
    f32 = jnp.float32
    field = jax.ShapeDtypeStruct(shape, f32)
    cells_here = layers * rows * columns
    b_low, b_high = halo(buoyancy)
    u_low, u_high = halo(background_now)

    def matrix(*size):
        return jax.ShapeDtypeStruct(size, jnp.bfloat16)

    copied = (stiffness, buoyancy, background_now, background_prev)
    matrices = (matrix(columns, columns), matrix(rows, 2 * rows), matrix(rows, 3 * rows))
    (
        counts, source_field, taper, mx, my2, my3, stiffness, b_mid, current, older
    ) = pl.pallas_call(
        functools.partial(place_kernel, len(copied)),
        out_shape=(field,) * 3 + matrices + (field,) * len(copied),
        compiler_params=params(),
        cost_estimate=pl.CostEstimate(
            flops=40 * cells_here, bytes_accessed=16 * cells_here, transcendentals=0
        ),
        name="place",
    )(
        receiver_cells.reshape(1, -1),
        source_cells.reshape(1, -1),
        source_amp.reshape(1, -1),
        absorb_mask,
        *copied,
    )

    buoy = (b_low, b_mid, b_high)
    fields = [current]
    laps = []
    dg = None
    for t in range(STEPS):
        first, last = t == 0, t == STEPS - 1
        if not first:
            u_low, u_high = halo(current)
        operands = [u_low, current, u_high, *buoy, stiffness]
        if not first:
            operands.append(dg)
        if not last:
            operands += [taper, source_field, older]
        operands += [mx, my3]
        slots = 3 if first else 2
        results = pl.pallas_call(
            functools.partial(background_kernel, source_weight(t), first, last),
            out_shape=(field,) * (1 + (not last) + first),
            scratch_shapes=[
                pltpu.VMEM((slots, layers, 3 * rows, columns), jnp.bfloat16),
                pltpu.VMEM((slots, layers, rows, columns), f32),
            ],
            compiler_params=params(),
            cost_estimate=pl.CostEstimate(
                flops=60 * cells_here, bytes_accessed=56 * cells_here, transcendentals=0
            ),
            name=f"background{t}",
        )(*operands)
        results = list(results)
        laps.append(results.pop(0))
        if not last:
            older, current = current, results.pop(0)
            fields.append(current)
        if first:
            dg = results.pop(0)

    def wave(mode, group, p, old, add, lap, extra=()):
        low, high = halo(p)
        one = pl.BlockSpec((None, *shape), lambda d: (d, 0, 0, 0))
        shifted = pl.BlockSpec((None, *shape), lambda d: (d + group * each, 0, 0, 0))
        same = whole(shape)
        operands, specs = [low, p, high], [one] * 3
        if old is not None:
            operands.append(old)
            specs.append(one)
        operands += [*buoy, dg, stiffness]
        specs += [same] * 5
        if mode != "image":
            operands += [taper, add, lap]
            specs += [same, shifted if mode in ("born", "turn") else one, same]
        if mode == "turn":
            operands.append(counts)
            specs.append(same)
        if mode == "fold":
            specs += [one] + [same] * 4
        if mode == "image":
            specs += [one, pl.BlockSpec(memory_space=pltpu.SMEM)] + [same] * 2
        operands += [*extra, mx, my2]
        specs += [whole(mx.shape), whole(my2.shape)]
        out_shape, out_spec = (jax.ShapeDtypeStruct((each, *shape), f32),), [one]
        if mode == "fold":
            out_shape, out_spec = out_shape * 2, out_spec * 2
            if group == 0:
                out_shape, out_spec = out_shape + (field,) * 2, out_spec + [same] * 2
        elif mode == "image":
            split = (layers, rows // owners, columns)
            out_shape = (jax.ShapeDtypeStruct((each, *split), f32),) * owners
            out_spec = [pl.BlockSpec((None, *split), lambda d: (d, 0, 0, 0))] * owners
        results = pl.pallas_call(
            functools.partial(wave_kernel, mode, old is not None),
            grid=(each,),
            in_specs=specs,
            out_specs=out_spec,
            out_shape=out_shape,
            scratch_shapes=[
                pltpu.VMEM((2, layers, 2 * rows, columns), jnp.bfloat16),
                pltpu.VMEM((2, layers, rows, columns), f32),
            ],
            compiler_params=params(),
            cost_estimate=pl.CostEstimate(
                flops=60 * each * cells_here,
                bytes_accessed=28 * each * cells_here,
                transcendentals=0,
            ),
            name=mode,
        )(*operands)
        return results[0] if len(results) == 1 else results

    def after(value, earlier):
        return lax.optimization_barrier((value, earlier))[0]

    born = [[None] * GROUPS for _ in range(STEPS + 1)]
    for g in range(GROUPS):
        mine = perturbations[g * each : (g + 1) * each]
        born[1][g] = taper * (mine * laps[0])
    born[1][1] = after(born[1][1], fields[2])
    ahead = {(2, 1): fields[3], (3, 1): laps[3]}
    for t in (1, 2):
        for g in range(GROUPS):
            old = born[t - 1][g] if t > 1 else None
            new = wave("born", g, born[t][g], old, perturbations, laps[t])
            if (t + 1, g) in ahead:
                new = after(new, ahead[t + 1, g])
            born[t + 1][g] = new
    adjoint = [[None] * GROUPS for _ in range(STEPS + 1)]
    for g in range(GROUPS):
        adjoint[3][g] = wave("turn", g, born[3][g], born[2][g], perturbations, laps[3])
    for g in range(GROUPS):
        adjoint[2][g] = wave("adjoint", g, adjoint[3][g], None, born[3][g], counts)
    known = [None] * GROUPS
    for g in range(GROUPS):
        adjoint[1][g], known[g], *rest = wave(
            "fold", g, adjoint[2][g], adjoint[3][g], born[2][g], counts, (born[1][g], *laps)
        )
        if g == 0:
            weight, near = rest
    sketch = []
    for g in range(GROUPS):
        blocks = wave(
            "image", g, adjoint[1][g], None, None, None, (known[g], me, weight, near)
        )
        sketch.append(blocks[0])
        for s in range(1, owners):
            ring = [(i, (i + s) % owners) for i in range(owners)]
            sketch.append(lax.ppermute(blocks[s], "dirs", ring))

    total_dirs = owners * sketch_count
    local_rows = rows // owners
    square = (total_dirs, total_dirs)
    place = jnp.arange(total_dirs, dtype=jnp.int32)
    owner = (me[0] - place // sketch_count + owners) % owners
    local = owner * sketch_count + place % sketch_count
    selector = (column_order[:, None] == local[None, :]).astype(f32)
    gram = pl.pallas_call(
        functools.partial(gram_kernel, GROUPS),
        out_shape=jax.ShapeDtypeStruct(square, f32),
        scratch_shapes=[pltpu.VMEM((*square, LANE), f32)],
        compiler_params=params(),
        name="gram",
    )(selector, selector.T, *[s.reshape(each, layers * local_rows, columns) for s in sketch])
    gram = add_up(gram)
    grid_cells = layers * lax.axis_size("slab") * rows * columns
    part = (each, 1, local_rows, columns)
    basis, triangle = pl.pallas_call(
        functools.partial(basis_kernel, GROUPS, math.sqrt(grid_cells)),
        grid=(layers,),
        in_specs=[whole(square)] * 2
        + [pl.BlockSpec(part, lambda l: (0, l, 0, 0))] * len(sketch),
        out_specs=[
            pl.BlockSpec((total_dirs, 1, local_rows, columns), lambda l: (0, l, 0, 0)),
            whole(square),
        ],
        out_shape=(
            jax.ShapeDtypeStruct((total_dirs, layers, local_rows, columns), f32),
            jax.ShapeDtypeStruct(square, f32),
        ),
        scratch_shapes=[pltpu.VMEM((total_dirs * total_dirs, 8, LANE), f32)],
        compiler_params=params(),
        name="basis",
    )(gram, selector, *sketch)
    return basis, triangle


def solution(mesh):
    return jax.shard_map(
        shards,
        mesh=mesh,
        in_specs=(
            P("dirs", "slab", None, None),
            P("slab", None, None),
            P("slab", None, None),
            P("slab", None, None),
            P("slab", None, None),
            P("slab", None, None),
            P("slab"),
            P("slab"),
            P("slab"),
            P(),
        ),
        out_specs=(P(None, "slab", "dirs", None), P()),
        check_vma=False,
    )
```
